256 devices in a mesh: gx: 16 (over x, y), gy: 16 (over z, core).
Axes of the slice: x: 4, y: 4, z: 8, core: 2. Of those that a mesh axis runs over, the one named last changes fastest.
Arguments:
- source: float32 [256, 256, 128], P('gx', 'gy'), may hold values from -12 to 12
- dielectric: float32 [256, 256, 128], P('gx', 'gy'), may hold values from 0.2 to 4
- screening: float32 [256, 256, 128], P('gx', 'gy'), may hold values from 0.05 to 2
Outputs:
- solution: float32 [256, 256, 128], P('gx', 'gy')
The draws below stay inside these ranges and needn't reach their ends.
All inputs are finite; a program needn't handle non-finite values.
Results may differ from the reference program's by a relative error of at most 0.0001.
Values sent between devices are 32-bit elements; how exact they have to be, the bound alone decides.
No kernel may reach another device: no remote copies, remote signals or barrier semaphores. Data moves between devices by JAX's collectives and lax.ppermute only.
A program may use at most 128 MiB of HBM per device.

```python
import math
import jax
import jax.numpy as jnp

LEVELS = 5
SWEEPS = 3
COARSE = 6
NX = 256
NY = 256
NZ = 128


def draw_source(key, part):
    return jnp.clip(2.0 * jax.random.normal(key, (NX, NY, NZ), jnp.float32), -12.0, 12.0)


def block_levels(stream_key, extent, cuts, least, top_value):
    factor_of, own = 1.0, jax.random.fold_in(stream_key, 6)
    for dim, blocks in cuts:
        heights = jnp.exp(jax.random.uniform(jax.random.fold_in(own, dim), (blocks,), jnp.float32, least / len(cuts), top_value / len(cuts)))
        factor_of = factor_of * jnp.repeat(heights, extent[dim] // blocks).reshape([-1 if axis == dim else 1 for axis in range(len(extent))])
    return factor_of


def setup_inputs(seed: int = 0) -> dict:
    key_list = jax.random.split(jax.random.key(seed), 4)
    return {
        "source": draw_source(jax.random.fold_in(key_list[3], 71), 0),
        "dielectric": jnp.clip(jnp.exp(math.log(4.0) - 2.9957323 * jax.random.uniform(key_list[1], (NX, NY, NZ), jnp.float32) ** block_levels(key_list[1], (NX, NY, NZ), ((0, 16), (1, 16)), -0.2, 0.2)), 0.2, 4.0),
        "screening": jnp.clip(jnp.exp(math.log(2.0) - 3.6888794 * jax.random.uniform(key_list[2], (NX, NY, NZ), jnp.float32) ** block_levels(key_list[2], (NX, NY, NZ), ((0, 16), (1, 16)), -0.2, 0.2)), 0.05, 2.0),
    }


OMEGA = 0.8


def zero_rims(values):
    return jnp.pad(values, ((1, 1), (1, 1), (0, 0)))


def face_weights(padded, screening):
    centre = padded[1:-1, 1:-1]
    low_x = 0.5 * (padded[:-2, 1:-1] + centre)
    high_x = 0.5 * (padded[2:, 1:-1] + centre)
    low_y = 0.5 * (padded[1:-1, :-2] + centre)
    high_y = 0.5 * (padded[1:-1, 2:] + centre)
    z_padded = jnp.pad(centre, ((0, 0), (0, 0), (1, 1)))
    low_z = 0.5 * (z_padded[:, :, :-2] + centre)
    high_z = 0.5 * (z_padded[:, :, 2:] + centre)
    return jnp.stack([low_x, high_x, low_y, high_y, low_z, high_z, screening])


def diagonal(stencil):
    return stencil[0] + stencil[1] + stencil[2] + stencil[3] + stencil[4] + stencil[5] + stencil[6]


def operate(values, stencil, padder):
    padded = padder(values)
    z_padded = jnp.pad(values, ((0, 0), (0, 0), (1, 1)))
    beside = stencil[0] * padded[:-2, 1:-1] + stencil[1] * padded[2:, 1:-1]
    beside = beside + stencil[2] * padded[1:-1, :-2] + stencil[3] * padded[1:-1, 2:]
    beside = beside + stencil[4] * z_padded[:, :, :-2] + stencil[5] * z_padded[:, :, 2:]
    return diagonal(stencil) * values - beside


def jacobi_step(values, right_side, stencil, padder):
    return values + OMEGA * (right_side - operate(values, stencil, padder)) / diagonal(stencil)


def first_sweep(right_side, stencil):
    return OMEGA * right_side / diagonal(stencil)


def restrict(values):
    count_x, count_y, count_z = values.shape
    return values.reshape(count_x // 2, 2, count_y // 2, 2, count_z // 2, 2).sum(axis=(1, 3, 5))


def coarsen(stencil):
    count_c, count_x, count_y, count_z = stencil.shape
    blocks = stencil.reshape(count_c, count_x // 2, 2, count_y // 2, 2, count_z // 2, 2)
    low_x = blocks[0][:, 0].sum(axis=(2, 4))
    high_x = blocks[1][:, 1].sum(axis=(2, 4))
    low_y = blocks[2][:, :, :, 0].sum(axis=(1, 4))
    high_y = blocks[3][:, :, :, 1].sum(axis=(1, 4))
    low_z = blocks[4][:, :, :, :, :, 0].sum(axis=(1, 3))
    high_z = blocks[5][:, :, :, :, :, 1].sum(axis=(1, 3))
    screen = blocks[6].sum(axis=(1, 3, 5))
    return jnp.stack([low_x, high_x, low_y, high_y, low_z, high_z, screen])


def prolong(values):
    count_x, count_y, count_z = values.shape
    spread_out = jnp.broadcast_to(values[:, None, :, None, :, None], (count_x, 2, count_y, 2, count_z, 2))
    return spread_out.reshape(2 * count_x, 2 * count_y, 2 * count_z)


def descend(right_side, stencil, padder, count):
    stored = []
    for _ in range(count):
        values = first_sweep(right_side, stencil)
        for _ in range(SWEEPS - 1):
            values = jacobi_step(values, right_side, stencil, padder)
        residual = right_side - operate(values, stencil, padder)
        stored.append((values, right_side, stencil))
        right_side = restrict(residual)
        stencil = coarsen(stencil)
    return right_side, stencil, stored


def bottom(right_side, stencil, padder):
    values = first_sweep(right_side, stencil)
    for _ in range(COARSE - 1):
        values = jacobi_step(values, right_side, stencil, padder)
    return values


def ascend(values, stored, padder):
    for fine_values, right_side, stencil in reversed(stored):
        values = fine_values + prolong(values)
        for _ in range(SWEEPS):
            values = jacobi_step(values, right_side, stencil, padder)
    return values


def reference(source, dielectric, screening):
    padded = jnp.pad(dielectric, ((1, 1), (1, 1), (0, 0)))
    stencil = face_weights(padded, screening)
    coarse_side, coarse_stencil, stored = descend(source, stencil, zero_rims, LEVELS - 1)
    values = bottom(coarse_side, coarse_stencil, zero_rims)
    return ascend(values, stored, zero_rims)
```

```python
import jax
import jax.numpy as jnp
from jax import lax
from jax.experimental import pallas as pl
from jax.experimental.pallas import tpu as pltpu
from jax.sharding import PartitionSpec as P

OMEGA = 0.8
F32 = jnp.float32
LANES = 128


def roll(values, shift, dim):
    return pltpu.roll(values, shift % values.shape[dim], dim)


def lane_of(values):
    return lax.broadcasted_iota(jnp.int32, values.shape, values.ndim - 1)


def row_of(values):
    return lax.broadcasted_iota(jnp.int32, values.shape, values.ndim - 2)


def bit_of(values, bit):
    return ((lane_of(values) >> bit) & 1) == 1


def pair(values, bit):
    step, dim = 1 << bit, values.ndim - 1
    other = jnp.where(bit_of(values, bit), roll(values, step, dim), roll(values, -step, dim))
    return values + other


def keep(values, bit, want):
    step, dim = 1 << bit, values.ndim - 1
    if want:
        return jnp.where(bit_of(values, bit), values, roll(values, -step, dim))
    return jnp.where(bit_of(values, bit), roll(values, step, dim), values)


def spread(values, which, bits):
    for bit in range(bits):
        values = keep(values, bit, (which >> bit) & 1)
    return values


def relax_factor(diag):
    good = diag > 0.0
    return jnp.where(good, OMEGA / jnp.where(good, diag, 1.0), 0.0)


def loop(first, last, step, body):
    count = (last - first + 1) // step
    assert count * step == last - first + 1

    def run(index, carry):
        body(first + index * step)
        return carry

    lax.fori_loop(0, count, run, 0)


def beside(vals, faces, plane, count, level):
    fx, fy, fz = faces
    shift = 1 << level
    v = vals[pl.ds(plane, count)]
    y_face, z_face = fy[pl.ds(plane, count)], fz[pl.ds(plane, count)]
    total = fx[pl.ds(plane, count)] * vals[pl.ds(plane - 1, count)]
    total = total + fx[pl.ds(plane + 1, count)] * vals[pl.ds(plane + 1, count)]
    total = total + y_face * roll(v, 1, 1) + roll(y_face * v, -1, 1)
    total = total + z_face * roll(v, shift, 2) + roll(z_face * v, -shift, 2)
    return v, total


def sweep(out, vals, side, faces, weight, first, last, step, level):
    def body(plane):
        v, total = beside(vals, faces, plane, step, level)
        here = pl.ds(plane, step)
        out[here] = (1.0 - OMEGA) * v + weight[here] * (side[here] + total)

    loop(first, last, step, body)


def remains(out, vals, side, faces, diag, first, last, step, level):
    def body(plane):
        v, total = beside(vals, faces, plane, step, level)
        here = pl.ds(plane, step)
        out[here] = side[here] - diag[here] * v + total

    loop(first, last, step, body)


def block_sum(ref, plane, start, count):
    even, odd = pl.ds(start, count, stride=2), pl.ds(start + 1, count, stride=2)
    low = ref[plane, even, :] + ref[plane, odd, :]
    return low + (ref[plane + 1, even, :] + ref[plane + 1, odd, :])


def coarse_stencil(faces, diag, plane, start, count, level):
    fx, fy, fz = faces
    even, odd = pl.ds(start, count, stride=2), pl.ds(start + 1, count, stride=2)
    x_low = fx[plane, even, :] + fx[plane, odd, :]
    x_mid = fx[plane + 1, even, :] + fx[plane + 1, odd, :]
    y_low = fy[plane, even, :] + fy[plane + 1, even, :]
    y_mid = fy[plane, odd, :] + fy[plane + 1, odd, :]
    z_sum = block_sum(fz, plane, start, count)
    d_sum = block_sum(diag, plane, start, count)
    d_new = pair(d_sum - 2.0 * (x_mid + y_mid), level) - 2.0 * keep(z_sum, level, 1)
    return pair(x_low, level), pair(y_low, level), keep(z_sum, level, 0), d_new


def call(body, outs, scratch, limit, flops, *args):
    nbytes = sum(4 * a.size for a in args) + sum(4 * o.size for o in outs)
    return pl.pallas_call(
        body,
        out_shape=outs,
        in_specs=[pl.BlockSpec(memory_space=pltpu.VMEM)] * len(args),
        out_specs=[pl.BlockSpec(memory_space=pltpu.VMEM)] * len(outs),
        scratch_shapes=scratch,
        compiler_params=pltpu.CompilerParams(vmem_limit_bytes=limit << 20),
        cost_estimate=pl.CostEstimate(flops=flops, bytes_accessed=nbytes, transcendentals=0),
    )(*args)


def array(*shape):
    return jax.ShapeDtypeStruct(shape, F32)


def strips_kernel(eps, src, scr, xl, xr, up, down):
    at = 0
    for own, start, wide in ((eps, 0, 10), (src, 10, 9), (scr, 19, 9)):
        for part, low, count in ((xl, start, wide), (own, 0, 16), (xr, start, wide)):
            up[at : at + count] = part[low : low + count, 8:16]
            down[at : at + count] = part[low : low + count, 0:8]
            for k in range(count):
                tile, row = 104 + (at + k) // 4, 2 * ((at + k) % 4)
                up[tile, row : row + 2] = part[low + k, 6:8]
                down[tile, row : row + 2] = part[low + k, 8:10]
            at += count


def down_kernel(
    eps, src, scr, xl, xr, yl, yr,
    u0_out, fx0_out, fy0_out, fz0_out, w0_out, r0_out,
    fx1, fy1, fz1, w1, l1_own, l2_own, up, down,
    e, b, s, fx, fy, fz, w, d, ua, ub, b1, d1, va, vb,
):
    at = 0
    for ref, own, start, wide in ((e, eps, 0, 10), (b, src, 10, 9), (s, scr, 19, 9)):
        first = 10 - wide
        planes = 16 + 2 * wide
        ref[first:10, 16:32] = xl[start : start + wide]
        ref[10:26, 16:32] = own[...]
        ref[26 : 26 + wide, 16:32] = xr[start : start + wide]
        ref[first : first + planes, 8:16] = yl[at : at + planes]
        ref[first : first + planes, 32:40] = yr[at : at + planes]
        for k in range(planes):
            tile, row = 104 + (at + k) // 4, 2 * ((at + k) % 4)
            below, above = yl[tile], yr[tile]
            rows = row_of(below)
            ref[first + k, 0:8] = jnp.where(
                rows < 2, roll(above, -row, 0), jnp.where(rows >= 6, roll(below, 6 - row, 0), 0.0)
            )
        at += planes

    def stencil(plane):
        cells = e[pl.ds(plane - 1, 4)]
        centre = cells[1:3]
        x_face = 0.5 * (cells[0:3] + cells[1:4])
        y_face = 0.5 * (centre + roll(centre, 1, 1))
        lanes = lane_of(centre)
        z_face = jnp.where(lanes == 0, 0.0, 0.5 * (centre + roll(centre, 1, 2)))
        ends = jnp.where((lanes == 0) | (lanes == LANES - 1), 0.5 * centre, 0.0)
        here = pl.ds(plane, 2)
        screen = s[here]
        diag = x_face[0:2] + x_face[1:3] + y_face + roll(y_face, -1, 1)
        diag = diag + z_face + roll(z_face, -1, 2) + screen + ends
        diag = jnp.where(screen > 0.0, diag, 0.0)
        weight = relax_factor(diag)
        fx[pl.ds(plane, 3)] = x_face
        fy[here] = y_face
        fz[here] = z_face
        d[here] = diag
        w[here] = weight
        ua[here] = weight * b[here]

    loop(1, 34, 2, stencil)
    faces = (fx, fy, fz)
    sweep(ub, ua, b, faces, w, 2, 33, 2, 0)
    sweep(ua, ub, b, faces, w, 3, 32, 2, 0)
    remains(ub, ua, b, faces, d, 4, 31, 2, 0)
    u0_out[...] = ua[10:26, 16:32]

    def keep_window(plane):
        for out, ref in ((fx0_out, fx), (fy0_out, fy), (fz0_out, fz), (w0_out, w), (r0_out, ub)):
            out[plane, 8:24] = ref[plane + 7, 16:32]
            high, low = ref[plane + 7, 32:40], ref[plane + 7, 8:16]
            out[plane, 0:8] = jnp.where(row_of(high) < 4, high, low)

    loop(0, 21, 1, keep_window)

    def to_level1(plane):
        x_face, y_face, z_face, diag = coarse_stencil(faces, d, 2 * plane, 0, 20, 0)
        fx1[plane, 0:20] = x_face
        fy1[plane, 0:20] = y_face
        fz1[plane, 0:20] = z_face
        fy1[plane, 20:21] = y_face[0:1]
        d1[plane, 0:20] = diag
        w1[plane, 0:20] = relax_factor(diag)

    for ref in (fx1, fy1, fz1, w1, d1, b1):
        ref[:, 16:24] = jnp.zeros((18, 8, LANES), F32)
    loop(1, 16, 1, to_level1)
    even, odd = pl.ds(0, 20, stride=2), pl.ds(1, 20, stride=2)
    fx1[17, 0:20] = pair(fx[34, even, :] + fx[34, odd, :], 0)

    def side1(plane):
        side = pair(block_sum(ub, 2 * plane, 0, 20), 0)
        b1[plane, 0:20] = side
        va[plane, 0:20] = w1[plane, 0:20] * side

    loop(2, 15, 1, side1)
    va[:, 20:24] = jnp.zeros((18, 4, LANES), F32)
    faces1 = (fx1, fy1, fz1)
    sweep(vb, va, b1, faces1, w1, 3, 14, 4, 1)
    sweep(va, vb, b1, faces1, w1, 4, 13, 2, 1)
    remains(vb, va, b1, faces1, d1, 5, 12, 4, 1)

    own = jnp.where(bit_of(va[5:13, 8:16], 0), va[5:13, 8:16], vb[5:13, 8:16])
    l1_own[...] = own
    l2_own[2] = jnp.zeros((8, LANES), F32)
    packed = jnp.zeros((4, LANES), F32)
    quarter = lane_of(packed) & 3
    for k in range(4):
        parts = coarse_stencil(faces1, d1, 5 + 2 * k, 8, 4, 1)
        stack = parts[3]
        for q in range(3):
            stack = jnp.where(quarter == q, parts[q], stack)
        l2_own[k // 2, 4 * (k % 2) : 4 * (k % 2) + 4] = stack
        packed = jnp.where(quarter == k, pair(block_sum(vb, 5 + 2 * k, 8, 4), 1), packed)
    l2_own[2, 0:4] = packed
    up[0:3] = l2_own[...]
    down[0:3] = l2_own[...]
    for t in range(4):
        first, second = l1_own[2 * t], l1_own[2 * t + 1]
        low = row_of(first) < 4
        up[3 + t] = jnp.where(low, roll(first, -4, 0), second)
        down[3 + t] = jnp.where(low, first, roll(second, 4, 0))


def window_kernel(l2_own, l1_own, a1u, a1d, a2u, a2d, main, up, down, l1_ext):
    low = lax.broadcasted_iota(jnp.int32, (8, LANES), 0) < 4
    for k in range(5):
        t, turn = k // 2, 4 * (k % 2)
        main[3 * k] = jnp.where(low, roll(a2u[t], -turn, 0), roll(a1u[t], 4 - turn, 0))
        main[3 * k + 1] = jnp.where(low, roll(l2_own[t], -turn, 0), roll(a1d[t], 4 - turn, 0))
        main[3 * k + 2] = jnp.where(low, roll(a2d[t], -turn, 0), 0.0)
    for k in range(8):
        t, turn = 3 + k // 2, 4 * (k % 2)
        l1_ext[2 * k] = jnp.where(low, roll(a1d[t], -turn, 0), roll(a1u[t], 4 - turn, 0))
        l1_ext[2 * k + 1] = l1_own[k]
    up[0:15] = main[...]
    down[0:15] = main[...]
    up[15:23] = l1_ext[8:16]
    down[15:23] = l1_ext[0:8]


def level2_kernel(
    main, c1u, c1d, c2u, c2d,
    fx, fy, fz, w, r, u, payload,
    d, b, ua, ub, coarse,
):
    for group, part in enumerate((c2u, c1u, main, c1d, c2d)):
        sides = jnp.concatenate([part[12], part[13], part[14]], axis=0)
        for k in range(4):
            plane = 4 * group + k
            tiles = jnp.concatenate([part[3 * k], part[3 * k + 1], part[3 * k + 2]], axis=0)
            fx[plane] = spread(tiles, 0, 2)
            fy[plane] = spread(tiles, 1, 2)
            fz[plane] = spread(tiles, 2, 2)
            diag = spread(tiles, 3, 2)
            side = spread(sides, k, 2)
            weight = relax_factor(diag)
            d[plane] = diag
            b[plane] = side
            w[plane] = weight
            ua[plane] = weight * side
    faces = (fx, fy, fz)
    sweep(ub, ua, b, faces, w, 1, 18, 3, 2)
    sweep(u, ub, b, faces, w, 2, 17, 4, 2)
    remains(r, u, b, faces, d, 3, 16, 2, 2)

    gx, gy = lax.axis_index("gx"), lax.axis_index("gy")
    x_odd, y_odd = lax.rem(gx, 2), lax.rem(gy, 2)
    for plane in range(2, 8):
        parts = coarse_stencil(faces, d, 2 * plane, 0, 8, 2)
        side = pair(block_sum(r, 2 * plane, 0, 8), 2)
        rows = row_of(side)
        x_face = jnp.where(2 * gx + plane - 4 == 0, 0.0, parts[0])
        y_face = jnp.where(2 * gy + rows - 4 == 0, 0.0, parts[1])
        for index, values in enumerate((x_face, y_face, parts[2], parts[3], side)):
            coarse[index, plane] = jnp.where(y_odd == 1, roll(values, -2, 0), roll(values, -4, 0))
    x_start = 4 - 2 * x_odd
    rows = lax.broadcasted_iota(jnp.int32, (8, LANES), 0)
    slot = lax.broadcasted_iota(jnp.int32, (8, LANES), 1) & 7
    for index in range(5):
        for lead in range(2):
            total = jnp.where(slot == 2 * rows, coarse[index, x_start + lead], 0.0)
            total = total + jnp.where(slot == 2 * rows + 1, coarse[index, x_start + 2 + lead], 0.0)
            line = jnp.sum(total, axis=0, keepdims=True)
            payload[pl.ds(2 * index + lead, 64, stride=10), :] = jnp.broadcast_to(line, (64, LANES))


def level3_beside(v0, v1, faces):
    (x0, x1), (y0, y1), (z0, z1) = faces
    x_bit = bit_of(v0, 0)
    quarter = (lane_of(v0) >> 1) & 3
    from_low = jnp.where(x_bit, roll(v1, 1, 1), roll(roll(v1, -1, 1), 8, 0))
    product = x0 * v0
    from_high = jnp.where(x_bit, roll(roll(product, 1, 1), -8, 0), roll(product, -1, 1))
    totals = [x0 * from_low + x1 * v1, x1 * v0 + from_high]
    for lead, (v, y_face, z_face) in enumerate(((v0, y0, z0), (v1, y1, z1))):
        low = jnp.where(quarter == 0, roll(roll(v, -6, 1), 1, 0), roll(v, 2, 1))
        product = y_face * v
        high = jnp.where(quarter == 3, roll(roll(product, 6, 1), -1, 0), roll(product, -2, 1))
        totals[lead] = totals[lead] + y_face * low + high
        totals[lead] = totals[lead] + z_face * roll(v, 8, 1) + roll(z_face * v, -8, 1)
    return totals


def level4_beside(v, x_face, y_face, z_face):
    x_bit, y_bit = bit_of(v, 0), bit_of(v, 2)
    low = jnp.where(x_bit, roll(v, 1, 1), roll(roll(v, -1, 1), 8, 0))
    product = x_face * v
    high = jnp.where(x_bit, roll(roll(product, 1, 1), -8, 0), roll(product, -1, 1))
    total = x_face * low + high
    low = jnp.where(y_bit, roll(v, 4, 1), roll(roll(v, -4, 1), 1, 0))
    product = y_face * v
    high = jnp.where(y_bit, roll(roll(product, 4, 1), -1, 0), roll(product, -4, 1))
    total = total + y_face * low + high
    return total + z_face * roll(v, 16, 1) + roll(z_face * v, -16, 1)


def coarse_levels(got):
    lines = [[got[pl.ds(2 * index + lead, 64, stride=10), :] for lead in range(2)] for index in range(5)]
    faces, diag, side = lines[0:3], lines[3], lines[4]
    weight = [relax_factor(d) for d in diag]

    def sweep3(v, side):
        total = level3_beside(v[0], v[1], faces)
        return [(1.0 - OMEGA) * v[k] + weight[k] * (side[k] + total[k]) for k in range(2)]

    u = [weight[k] * side[k] for k in range(2)]
    u = sweep3(u, side)
    u = sweep3(u, side)
    total = level3_beside(u[0], u[1], faces)
    r = [side[k] - diag[k] * u[k] + total[k] for k in range(2)]

    (x0, x1), (y0, y1), (z0, z1) = faces
    y_sum, z_sum = pair(y0 + y1, 3), pair(z0 + z1, 1)
    x4, y4, z4 = pair(pair(x0, 1), 3), keep(y_sum, 1, 0), keep(z_sum, 3, 0)
    inner = pair(pair(x1, 1), 3) + keep(y_sum, 1, 1) + keep(z_sum, 3, 1)
    w4 = relax_factor(pair(pair(diag[0] + diag[1], 1), 3) - 2.0 * inner)
    b4 = pair(pair(r[0] + r[1], 1), 3)
    v = w4 * b4
    for _ in range(5):
        v = (1.0 - OMEGA) * v + w4 * (b4 + level4_beside(v, x4, y4, z4))

    c = [v, v]
    for _ in range(3):
        c = sweep3(c, r)
    return [u[k] + c[k] for k in range(2)]


def up_kernel(
    got, u0, fx0, fy0, fz0, w0, r0,
    fx1, fy1, fz1, w1, l1_ext, c1u, c1d,
    fx2, fy2, fz2, w2, r2, u2,
    out,
    u3, e3, ea2, eb2, r1, u1, ea1, eb1, ea0, eb0,
):
    gx, gy = lax.axis_index("gx"), lax.axis_index("gy")
    x_odd, y_odd = lax.rem(gx, 2), lax.rem(gy, 2)
    solved = coarse_levels(got)
    for lead in range(2):
        u3[lead, 16:80] = solved[lead]
    corner = 16 + 8 * (lax.div(gx, 2) - 1) + lax.div(gy, 2) - 1
    for lead in range(2):
        for a in range(3):
            three = u3[lead, pl.ds(corner + 8 * a, 8), :]
            for q in range(8):
                values = spread(three, q, 3)
                e3[4 * a + 2 * (q % 2) + lead, pl.ds(q // 2, 3, stride=4), :] = values[0:3]

    def start2(plane):
        values = e3[2 * x_odd + plane]
        values = jnp.where(y_odd == 1, roll(values, -2, 0), values)[0:12]
        for k in range(2):
            ea2[2 * plane + k, pl.ds(0, 12, stride=2), :] = values
            ea2[2 * plane + k, pl.ds(1, 12, stride=2), :] = values

    loop(1, 8, 1, start2)

    def inside(values, weight, first, last, step):
        def body(plane):
            here = pl.ds(plane, step)
            values[here] = jnp.where(weight[here] > 0.0, values[here], 0.0)

        loop(first, last, step, body)

    inside(ea2, w2, 2, 17, 4)
    faces = (fx2, fy2, fz2)
    sweep(eb2, ea2, r2, faces, w2, 3, 16, 2, 2)
    sweep(ea2, eb2, r2, faces, w2, 4, 15, 4, 2)
    sweep(eb2, ea2, r2, faces, w2, 5, 14, 2, 2)

    for part, first, tile, count in ((c1u, 1, 15, 4), (l1_ext, 5, 0, 8), (c1d, 13, 15, 4)):
        for k in range(count):
            sides, own = part[tile + 2 * k], part[tile + 2 * k + 1]
            for ref, which in ((r1, 0), (u1, 1)):
                edge = keep(sides, 0, which)
                ref[first + k, 0:8] = edge
                ref[first + k, 8:16] = keep(own, 0, which)
                ref[first + k, 16:24] = edge

    def start1(plane):
        values = (u2[plane] + eb2[plane])[5:15]
        return values

    for plane in range(5, 15):
        values = start1(plane)
        for k in range(2):
            target = 5 + 2 * (plane - 8) + k
            if 0 <= target < 18:
                ea1[target, pl.ds(2, 10, stride=2), :] = values
                ea1[target, pl.ds(3, 10, stride=2), :] = values
    inside(ea1, w1, 1, 16, 4)
    faces = (fx1, fy1, fz1)
    for plane in (0, 17):
        ea1[plane] = jnp.where(edge_inside(gx, plane), ea1[plane], 0.0)
    sweep(eb1, ea1, r1, faces, w1, 1, 16, 4, 1)
    sweep(ea1, eb1, r1, faces, w1, 2, 15, 2, 1)
    sweep(eb1, ea1, r1, faces, w1, 3, 14, 4, 1)

    for plane in range(3, 15):
        values = u1[plane] + eb1[plane]
        for k in range(2):
            target = 3 + 2 * (plane - 5) + k
            if 0 <= target < 22:
                for parity in range(2):
                    ea0[target, pl.ds(4 + parity, 10, stride=2), :] = values[6:16]
                    ea0[target, pl.ds(parity, 2, stride=2), :] = values[16:18]
    inside(ea0, w0, 0, 21, 2)
    faces = (fx0, fy0, fz0)
    sweep(eb0, ea0, r0, faces, w0, 1, 20, 2, 0)
    sweep(ea0, eb0, r0, faces, w0, 2, 19, 2, 0)

    def last(plane):
        v, total = beside(ea0, faces, plane, 2, 0)
        here = pl.ds(plane, 2)
        values = (1.0 - OMEGA) * v + w0[here] * (r0[here] + total)
        out[pl.ds(plane - 3, 2)] = u0[pl.ds(plane - 3, 2)] + values[:, 8:24]

    loop(3, 18, 2, last)


def edge_inside(gx, plane):
    where = 8 * gx + plane - 5
    return (where >= 0) & (where < 8 * lax.axis_size("gx"))


def shifted(values, axis, step):
    count = lax.axis_size(axis)
    pairs = [(k, k + step) for k in range(count) if 0 <= k + step < count]
    return lax.ppermute(values, axis, pairs)


def local(source, dielectric, screening):
    fields = (dielectric, source, screening)
    last = jnp.concatenate([dielectric[6:], source[7:], screening[7:]], axis=0)
    first = jnp.concatenate([dielectric[:10], source[:9], screening[:9]], axis=0)
    xl, xr = shifted(last, "gx", 1), shifted(first, "gx", -1)
    up, down = call(strips_kernel, [array(130, 8, LANES)] * 2, [], 16, 10_000, *fields, xl, xr)
    yl, yr = shifted(up, "gy", 1), shifted(down, "gy", -1)

    big, mid = pltpu.VMEM((36, 40, LANES), F32), pltpu.VMEM((18, 24, LANES), F32)
    outs = [array(16, 16, LANES)] + [array(22, 24, LANES)] * 5 + [array(18, 24, LANES)] * 4
    outs += [array(8, 8, LANES), array(3, 8, LANES), array(7, 8, LANES), array(7, 8, LANES)]
    made = call(down_kernel, outs, [big] * 10 + [mid] * 4, 24, 10_000_000, *fields, xl, xr, yl, yr)
    fine, level1, (l1_own, l2_own, up, down) = made[0:6], made[6:10], made[10:14]

    a1u, a1d = shifted(up, "gy", 1), shifted(down, "gy", -1)
    a2u, a2d = shifted(l2_own, "gy", 2), shifted(l2_own, "gy", -2)
    outs = [array(15, 8, LANES), array(23, 8, LANES), array(23, 8, LANES), array(16, 8, LANES)]
    main, up, down, l1_ext = call(window_kernel, outs, [], 16, 10_000, l2_own, l1_own, a1u, a1d, a2u, a2d)
    c1u, c1d = shifted(up, "gx", 1), shifted(down, "gx", -1)
    c2u, c2d = shifted(main, "gx", 2), shifted(main, "gx", -2)

    two = pltpu.VMEM((20, 24, LANES), F32)
    outs = [array(20, 24, LANES)] * 6 + [array(640, LANES)]
    scratch = [two] * 4 + [pltpu.VMEM((5, 10, 8, LANES), F32)]
    *level2, payload = call(level2_kernel, outs, scratch, 16, 5_000_000, main, c1u, c1d, c2u, c2d)

    n_x, n_y = lax.axis_size("gx"), lax.axis_size("gy")
    groups = [
        [(2 * a + p) * n_y + 2 * b + q for a in range(n_x // 2) for b in range(n_y // 2)]
        for p in range(2)
        for q in range(2)
    ]
    got = lax.all_to_all(payload, ("gx", "gy"), 0, 0, tiled=True, axis_index_groups=groups)

    scratch = [pltpu.VMEM((2, 96, LANES), F32), pltpu.VMEM((12, 16, LANES), F32)]
    scratch += [two] * 2 + [mid] * 4 + [pltpu.VMEM((22, 24, LANES), F32)] * 2
    (result,) = call(
        up_kernel, [array(16, 16, LANES)], scratch, 24, 10_000_000,
        got, *fine, *level1, l1_ext, c1u, c1d, *level2,
    )
    return result


def solution(mesh):
    spec = P("gx", "gy", None)
    return jax.shard_map(local, mesh=mesh, in_specs=(spec,) * 3, out_specs=spec, check_vma=False)
```

```python
import jax
import jax.numpy as jnp
from jax import lax
from jax.experimental import pallas as pl
from jax.experimental.pallas import tpu as pltpu
from jax.sharding import PartitionSpec as P

OMEGA = 0.8
F32 = jnp.float32
LANES = 128


def roll(values, shift, dim):
    return pltpu.roll(values, shift % values.shape[dim], dim)


def lane_of(values):
    return lax.broadcasted_iota(jnp.int32, values.shape, values.ndim - 1)


def row_of(values):
    return lax.broadcasted_iota(jnp.int32, values.shape, values.ndim - 2)


def bit_of(values, bit):
    return ((lane_of(values) >> bit) & 1) == 1


def pair(values, bit):
    step, dim = 1 << bit, values.ndim - 1
    other = jnp.where(bit_of(values, bit), roll(values, step, dim), roll(values, -step, dim))
    return values + other


def keep(values, bit, want):
    step, dim = 1 << bit, values.ndim - 1
    if want:
        return jnp.where(bit_of(values, bit), values, roll(values, -step, dim))
    return jnp.where(bit_of(values, bit), roll(values, step, dim), values)


def spread(values, which, bits):
    for bit in range(bits):
        values = keep(values, bit, (which >> bit) & 1)
    return values


def relax_factor(diag):
    good = diag > 0.0
    return jnp.where(good, OMEGA / jnp.where(good, diag, 1.0), 0.0)


def loop(first, last, step, body, unroll=4):
    count = (last - first + 1) // step
    assert count * step == last - first + 1
    trips = count // unroll

    def run(index, carry):
        for k in range(unroll):
            body(first + (index * unroll + k) * step)
        return carry

    if trips > 1:
        lax.fori_loop(0, trips, run, 0)
    else:
        trips = 0
    for k in range(trips * unroll, count):
        body(first + k * step)


def beside(vals, faces, plane, count, level):
    fx, fy, fz = faces
    shift = 1 << level
    v = vals[pl.ds(plane, count)]
    y_face, z_face = fy[pl.ds(plane, count)], fz[pl.ds(plane, count)]
    total = fx[pl.ds(plane, count)] * vals[pl.ds(plane - 1, count)]
    total = total + fx[pl.ds(plane + 1, count)] * vals[pl.ds(plane + 1, count)]
    total = total + y_face * roll(v, 1, 1) + roll(y_face * v, -1, 1)
    total = total + z_face * roll(v, shift, 2) + roll(z_face * v, -shift, 2)
    return v, total


def sweep(out, vals, side, faces, weight, first, last, step, level, unroll=4):
    def body(plane):
        v, total = beside(vals, faces, plane, step, level)
        here = pl.ds(plane, step)
        out[here] = (1.0 - OMEGA) * v + weight[here] * (side[here] + total)

    loop(first, last, step, body, unroll)


def remains(out, vals, side, faces, diag, first, last, step, level, unroll=4):
    def body(plane):
        v, total = beside(vals, faces, plane, step, level)
        here = pl.ds(plane, step)
        out[here] = side[here] - diag[here] * v + total

    loop(first, last, step, body, unroll)


def block_sum(ref, plane, start, count):
    even, odd = pl.ds(start, count, stride=2), pl.ds(start + 1, count, stride=2)
    low = ref[plane, even, :] + ref[plane, odd, :]
    return low + (ref[plane + 1, even, :] + ref[plane + 1, odd, :])


def coarse_stencil(faces, diag, plane, start, count, level):
    fx, fy, fz = faces
    even, odd = pl.ds(start, count, stride=2), pl.ds(start + 1, count, stride=2)
    x_low = fx[plane, even, :] + fx[plane, odd, :]
    x_mid = fx[plane + 1, even, :] + fx[plane + 1, odd, :]
    y_low = fy[plane, even, :] + fy[plane + 1, even, :]
    y_mid = fy[plane, odd, :] + fy[plane + 1, odd, :]
    z_sum = block_sum(fz, plane, start, count)
    d_sum = block_sum(diag, plane, start, count)
    d_new = pair(d_sum - 2.0 * (x_mid + y_mid), level) - 2.0 * keep(z_sum, level, 1)
    return pair(x_low, level), pair(y_low, level), keep(z_sum, level, 0), d_new


def call(body, outs, scratch, limit, flops, *args, space=pltpu.VMEM):
    nbytes = sum(4 * a.size for a in args) + sum(4 * o.size for o in outs)
    return pl.pallas_call(
        body,
        out_shape=outs,
        in_specs=[pl.BlockSpec(memory_space=space)] * len(args),
        out_specs=[pl.BlockSpec(memory_space=pltpu.VMEM)] * len(outs),
        scratch_shapes=scratch,
        compiler_params=pltpu.CompilerParams(vmem_limit_bytes=limit << 20),
        cost_estimate=pl.CostEstimate(flops=flops, bytes_accessed=nbytes, transcendentals=0),
    )(*args)


def array(*shape):
    return jax.ShapeDtypeStruct(shape, F32)


def x_strips_kernel(eps, src, scr, first, second, sems):
    even = is_even("gx", 1).astype(jnp.int32)
    copies = []
    for own, start, wide in ((eps, 0, 10), (src, 10, 9), (scr, 19, 9)):
        for out, low in ((first, (16 - wide) * even), (second, (16 - wide) * (1 - even))):
            source, target = own.at[pl.ds(low, wide)], out.at[pl.ds(start, wide)]
            copies.append(pltpu.make_async_copy(source, target, sems.at[len(copies)]))
    for copy in copies:
        copy.start()
    for copy in copies:
        copy.wait()


def y_strips_kernel(eps, src, scr, xa, xb, first, second):
    x_even = is_even("gx", 1)
    y_even = is_even("gy", 1)

    def fill(up, down, xl, xr):
        at = 0
        for own, start, wide in ((eps, 0, 10), (src, 10, 9), (scr, 19, 9)):
            for part, low, count in ((xl, start, wide), (own, 0, 16), (xr, start, wide)):
                up[at : at + count] = part[low : low + count, 8:16]
                down[at : at + count] = part[low : low + count, 0:8]
                for k in range(count):
                    tile, row = 104 + (at + k) // 4, 2 * ((at + k) % 4)
                    up[tile, row : row + 2] = part[low + k, 6:8]
                    down[tile, row : row + 2] = part[low + k, 8:10]
                at += count

    for x_want, (xl, xr) in ((True, (xb, xa)), (False, (xa, xb))):
        for y_want, (up, down) in ((True, (first, second)), (False, (second, first))):
            pl.when((x_even == x_want) & (y_even == y_want))(
                lambda up=up, down=down, xl=xl, xr=xr: fill(up, down, xl, xr)
            )


def down_kernel(
    eps, src, scr, xa, xb, ya, yb,
    u0_out, fx0_out, fy0_out, fz0_out, w0_out, r0_out,
    fx1, fy1, fz1, w1, l1_own, l2_own, ship_a, ship_b,
    e, b, s, fx, fy, fz, w, d, ua, ub, b1, d1, va, vb,
):
    x_even = is_even("gx", 1).astype(jnp.int32)
    y_even = is_even("gy", 1)
    row_a = pl.multiple_of(8 + 24 * y_even.astype(jnp.int32), 8)
    row_b = pl.multiple_of(32 - 24 * y_even.astype(jnp.int32), 8)
    at = 0
    for ref, own, start, wide in ((e, eps, 0, 10), (b, src, 10, 9), (s, scr, 19, 9)):
        first = 10 - wide
        planes = 16 + 2 * wide
        ref[10:26, 16:32] = own[...]
        ref[pl.ds(first + (26 - first) * x_even, wide), 16:32] = xa[start : start + wide]
        ref[pl.ds(26 - (26 - first) * x_even, wide), 16:32] = xb[start : start + wide]
        ref[first : first + planes, pl.ds(row_a, 8)] = ya[at : at + planes]
        ref[first : first + planes, pl.ds(row_b, 8)] = yb[at : at + planes]

        def fill(below_ref, above_ref, ref=ref, first=first, planes=planes, at=at):
            for k in range(planes):
                tile, row = 104 + (at + k) // 4, 2 * ((at + k) % 4)
                below, above = below_ref[tile], above_ref[tile]
                rows = row_of(below)
                ref[first + k, 0:8] = jnp.where(
                    rows < 2, roll(above, -row, 0), jnp.where(rows >= 6, roll(below, 6 - row, 0), 0.0)
                )

        pl.when(y_even)(lambda fill=fill: fill(yb, ya))
        pl.when(jnp.logical_not(y_even))(lambda fill=fill: fill(ya, yb))
        at += planes

    def stencil(plane):
        cells = e[pl.ds(plane - 1, 4)]
        centre = cells[1:3]
        x_face = 0.5 * (cells[0:3] + cells[1:4])
        y_face = 0.5 * (centre + roll(centre, 1, 1))
        lanes = lane_of(centre)
        z_face = jnp.where(lanes == 0, 0.0, 0.5 * (centre + roll(centre, 1, 2)))
        ends = jnp.where((lanes == 0) | (lanes == LANES - 1), 0.5 * centre, 0.0)
        here = pl.ds(plane, 2)
        screen = s[here]
        diag = x_face[0:2] + x_face[1:3] + y_face + roll(y_face, -1, 1)
        diag = diag + z_face + roll(z_face, -1, 2) + screen + ends
        diag = jnp.where(screen > 0.0, diag, 0.0)
        weight = relax_factor(diag)
        fx[pl.ds(plane, 3)] = x_face
        fy[here] = y_face
        fz[here] = z_face
        d[here] = diag
        w[here] = weight
        ua[here] = weight * b[here]

    loop(1, 34, 2, stencil, 8)
    faces = (fx, fy, fz)
    sweep(ub, ua, b, faces, w, 2, 33, 2, 0, 8)
    sweep(ua, ub, b, faces, w, 3, 32, 2, 0, 8)
    remains(ub, ua, b, faces, d, 4, 31, 2, 0, 8)
    u0_out[...] = ua[10:26, 16:32]

    def keep_window(plane):
        for out, ref in ((fx0_out, fx), (fy0_out, fy), (fz0_out, fz), (w0_out, w), (r0_out, ub)):
            out[plane, 8:24] = ref[plane + 7, 16:32]
            high, low = ref[plane + 7, 32:40], ref[plane + 7, 8:16]
            out[plane, 0:8] = jnp.where(row_of(high) < 4, high, low)

    loop(0, 21, 1, keep_window, 8)

    def to_level1(plane):
        x_face, y_face, z_face, diag = coarse_stencil(faces, d, 2 * plane, 0, 20, 0)
        fx1[plane, 0:20] = x_face
        fy1[plane, 0:20] = y_face
        fz1[plane, 0:20] = z_face
        fy1[plane, 20:21] = y_face[0:1]
        d1[plane, 0:20] = diag
        w1[plane, 0:20] = relax_factor(diag)

    for ref in (fx1, fy1, fz1, w1, d1, b1):
        ref[:, 16:24] = jnp.zeros((18, 8, LANES), F32)
    loop(1, 16, 1, to_level1, 8)
    even, odd = pl.ds(0, 20, stride=2), pl.ds(1, 20, stride=2)
    fx1[17, 0:20] = pair(fx[34, even, :] + fx[34, odd, :], 0)

    def side1(plane):
        side = pair(block_sum(ub, 2 * plane, 0, 20), 0)
        b1[plane, 0:20] = side
        va[plane, 0:20] = w1[plane, 0:20] * side

    loop(2, 15, 1, side1, 8)
    va[:, 20:24] = jnp.zeros((18, 4, LANES), F32)
    faces1 = (fx1, fy1, fz1)
    sweep(vb, va, b1, faces1, w1, 3, 14, 4, 1)
    sweep(va, vb, b1, faces1, w1, 4, 13, 2, 1)
    remains(vb, va, b1, faces1, d1, 5, 12, 4, 1)

    own = jnp.where(bit_of(va[5:13, 8:16], 0), va[5:13, 8:16], vb[5:13, 8:16])
    l1_own[...] = own
    l2_own[2] = jnp.zeros((8, LANES), F32)
    packed = jnp.zeros((4, LANES), F32)
    quarter = lane_of(packed) & 3
    for k in range(4):
        parts = coarse_stencil(faces1, d1, 5 + 2 * k, 8, 4, 1)
        stack = parts[3]
        for q in range(3):
            stack = jnp.where(quarter == q, parts[q], stack)
        l2_own[k // 2, 4 * (k % 2) : 4 * (k % 2) + 4] = stack
        packed = jnp.where(quarter == k, pair(block_sum(vb, 5 + 2 * k, 8, 4), 1), packed)
    l2_own[2, 0:4] = packed
    ship_a[0:3] = l2_own[...]
    ship_b[0:3] = l2_own[...]
    for t in range(4):
        first, second = l1_own[2 * t], l1_own[2 * t + 1]
        low = row_of(first) < 4
        up = jnp.where(low, roll(first, -4, 0), second)
        down = jnp.where(low, first, roll(second, 4, 0))
        ship_a[3 + t] = jnp.where(y_even, up, down)
        ship_b[3 + t] = jnp.where(y_even, down, up)


def window_kernel(l2_own, l1_own, a1a, a1b, a2a, a2b, main, ship_a, ship_b, l1_ext):
    y_even = is_even("gy", 1)
    pl.when(y_even)(lambda: join_y(l2_own, l1_own, a1b, a1a, a2a, a2b, main, l1_ext))
    pl.when(jnp.logical_not(y_even))(lambda: join_y(l2_own, l1_own, a1a, a1b, a2a, a2b, main, l1_ext))
    x_even = is_even("gx", 1).astype(jnp.int32)
    ship_a[0:15] = main[...]
    ship_b[0:15] = main[...]
    ship_a[15:23] = l1_ext[pl.ds(8 * x_even, 8)]
    ship_b[15:23] = l1_ext[pl.ds(8 - 8 * x_even, 8)]


def join_y(l2_own, l1_own, a1u, a1d, a2a, a2b, main, l1_ext):
    two_even = is_even("gy", 2)
    low = lax.broadcasted_iota(jnp.int32, (8, LANES), 0) < 4
    for k in range(5):
        t, turn = k // 2, 4 * (k % 2)
        far_a, far_b = a2a[t], a2b[t]
        far_u, far_d = jnp.where(two_even, far_b, far_a), jnp.where(two_even, far_a, far_b)
        main[3 * k] = jnp.where(low, roll(far_u, -turn, 0), roll(a1u[t], 4 - turn, 0))
        main[3 * k + 1] = jnp.where(low, roll(l2_own[t], -turn, 0), roll(a1d[t], 4 - turn, 0))
        main[3 * k + 2] = jnp.where(low, roll(far_d, -turn, 0), 0.0)
    for k in range(8):
        t, turn = 3 + k // 2, 4 * (k % 2)
        l1_ext[2 * k] = jnp.where(low, roll(a1d[t], -turn, 0), roll(a1u[t], 4 - turn, 0))
        l1_ext[2 * k + 1] = l1_own[k]


def level2_kernel(
    main, c1a, c1b, c2a, c2b,
    fx, fy, fz, w, r, u, payload,
    d, b, ua, ub, coarse,
):
    one, two = is_even("gx", 1).astype(jnp.int32), is_even("gx", 2).astype(jnp.int32)
    starts = (16 * two, 4 + 8 * one, 8, 12 - 8 * one, 16 - 16 * two)
    for start, part in zip(starts, (c2a, c1a, main, c1b, c2b)):
        sides = jnp.concatenate([part[12], part[13], part[14]], axis=0)
        for k in range(4):
            plane = start + k
            tiles = jnp.concatenate([part[3 * k], part[3 * k + 1], part[3 * k + 2]], axis=0)
            fx[plane] = spread(tiles, 0, 2)
            fy[plane] = spread(tiles, 1, 2)
            fz[plane] = spread(tiles, 2, 2)
            diag = spread(tiles, 3, 2)
            side = spread(sides, k, 2)
            weight = relax_factor(diag)
            d[plane] = diag
            b[plane] = side
            w[plane] = weight
            ua[plane] = weight * side
    faces = (fx, fy, fz)
    sweep(ub, ua, b, faces, w, 1, 18, 3, 2)
    sweep(u, ub, b, faces, w, 2, 17, 4, 2)
    remains(r, u, b, faces, d, 3, 16, 2, 2)

    gx, gy = lax.axis_index("gx"), lax.axis_index("gy")
    x_odd, y_odd = lax.rem(gx, 2), lax.rem(gy, 2)
    for plane in range(2, 8):
        parts = coarse_stencil(faces, d, 2 * plane, 0, 8, 2)
        side = pair(block_sum(r, 2 * plane, 0, 8), 2)
        rows = row_of(side)
        x_face = jnp.where(2 * gx + plane - 4 == 0, 0.0, parts[0])
        y_face = jnp.where(2 * gy + rows - 4 == 0, 0.0, parts[1])
        for index, values in enumerate((x_face, y_face, parts[2], parts[3], side)):
            coarse[index, plane] = jnp.where(y_odd == 1, roll(values, -2, 0), roll(values, -4, 0))
    x_start = 4 - 2 * x_odd
    rows = lax.broadcasted_iota(jnp.int32, (8, LANES), 0)
    slot = lax.broadcasted_iota(jnp.int32, (8, LANES), 1) & 7
    for index in range(5):
        for lead in range(2):
            total = jnp.where(slot == 2 * rows, coarse[index, x_start + lead], 0.0)
            total = total + jnp.where(slot == 2 * rows + 1, coarse[index, x_start + 2 + lead], 0.0)
            line = jnp.sum(total, axis=0, keepdims=True)
            payload[pl.ds(2 * index + lead, 64, stride=10), :] = jnp.broadcast_to(line, (64, LANES))


def level3_beside(v0, v1, faces):
    (x0, x1), (y0, y1), (z0, z1) = faces
    x_bit = bit_of(v0, 0)
    quarter = (lane_of(v0) >> 1) & 3
    from_low = jnp.where(x_bit, roll(v1, 1, 1), roll(roll(v1, -1, 1), 8, 0))
    product = x0 * v0
    from_high = jnp.where(x_bit, roll(roll(product, 1, 1), -8, 0), roll(product, -1, 1))
    totals = [x0 * from_low + x1 * v1, x1 * v0 + from_high]
    for lead, (v, y_face, z_face) in enumerate(((v0, y0, z0), (v1, y1, z1))):
        low = jnp.where(quarter == 0, roll(roll(v, -6, 1), 1, 0), roll(v, 2, 1))
        product = y_face * v
        high = jnp.where(quarter == 3, roll(roll(product, 6, 1), -1, 0), roll(product, -2, 1))
        totals[lead] = totals[lead] + y_face * low + high
        totals[lead] = totals[lead] + z_face * roll(v, 8, 1) + roll(z_face * v, -8, 1)
    return totals


def level4_beside(v, x_face, y_face, z_face):
    x_bit, y_bit = bit_of(v, 0), bit_of(v, 2)
    low = jnp.where(x_bit, roll(v, 1, 1), roll(roll(v, -1, 1), 8, 0))
    product = x_face * v
    high = jnp.where(x_bit, roll(roll(product, 1, 1), -8, 0), roll(product, -1, 1))
    total = x_face * low + high
    low = jnp.where(y_bit, roll(v, 4, 1), roll(roll(v, -4, 1), 1, 0))
    product = y_face * v
    high = jnp.where(y_bit, roll(roll(product, 4, 1), -1, 0), roll(product, -4, 1))
    total = total + y_face * low + high
    return total + z_face * roll(v, 16, 1) + roll(z_face * v, -16, 1)


def coarse_levels(got):
    lines = [[got[pl.ds(2 * index + lead, 64, stride=10), :] for lead in range(2)] for index in range(5)]
    faces, diag, side = lines[0:3], lines[3], lines[4]
    weight = [relax_factor(d) for d in diag]

    def sweep3(v, side):
        total = level3_beside(v[0], v[1], faces)
        return [(1.0 - OMEGA) * v[k] + weight[k] * (side[k] + total[k]) for k in range(2)]

    u = [weight[k] * side[k] for k in range(2)]
    u = sweep3(u, side)
    u = sweep3(u, side)
    total = level3_beside(u[0], u[1], faces)
    r = [side[k] - diag[k] * u[k] + total[k] for k in range(2)]

    (x0, x1), (y0, y1), (z0, z1) = faces
    y_sum, z_sum = pair(y0 + y1, 3), pair(z0 + z1, 1)
    x4, y4, z4 = pair(pair(x0, 1), 3), keep(y_sum, 1, 0), keep(z_sum, 3, 0)
    inner = pair(pair(x1, 1), 3) + keep(y_sum, 1, 1) + keep(z_sum, 3, 1)
    w4 = relax_factor(pair(pair(diag[0] + diag[1], 1), 3) - 2.0 * inner)
    b4 = pair(pair(r[0] + r[1], 1), 3)
    v = w4 * b4
    for _ in range(5):
        v = (1.0 - OMEGA) * v + w4 * (b4 + level4_beside(v, x4, y4, z4))

    c = [v, v]
    for _ in range(3):
        c = sweep3(c, r)
    return [u[k] + c[k] for k in range(2)]


def up_kernel(
    got, u0, fx0, fy0, fz0, w0, r0,
    fx1, fy1, fz1, w1, l1_ext, c1a, c1b,
    fx2, fy2, fz2, w2, r2, u2,
    out,
    u3, e3, ea2, eb2, r1, u1, ea1, eb1, ea0, eb0,
):
    gx, gy = lax.axis_index("gx"), lax.axis_index("gy")
    x_odd, y_odd = lax.rem(gx, 2), lax.rem(gy, 2)
    solved = coarse_levels(got)
    for lead in range(2):
        u3[lead, 16:80] = solved[lead]
    corner = 16 + 8 * (lax.div(gx, 2) - 1) + lax.div(gy, 2) - 1
    for lead in range(2):
        for a in range(3):
            three = u3[lead, pl.ds(corner + 8 * a, 8), :]
            for q in range(8):
                values = spread(three, q, 3)
                e3[4 * a + 2 * (q % 2) + lead, pl.ds(q // 2, 3, stride=4), :] = values[0:3]

    def start2(plane):
        values = e3[2 * x_odd + plane]
        values = jnp.where(y_odd == 1, roll(values, -2, 0), values)[0:12]
        for k in range(2):
            ea2[2 * plane + k, pl.ds(0, 12, stride=2), :] = values
            ea2[2 * plane + k, pl.ds(1, 12, stride=2), :] = values

    loop(1, 8, 1, start2)

    def inside(values, weight, first, last, step):
        def body(plane):
            here = pl.ds(plane, step)
            values[here] = jnp.where(weight[here] > 0.0, values[here], 0.0)

        loop(first, last, step, body)

    inside(ea2, w2, 2, 17, 4)
    faces = (fx2, fy2, fz2)
    sweep(eb2, ea2, r2, faces, w2, 3, 16, 2, 2)
    sweep(ea2, eb2, r2, faces, w2, 4, 15, 4, 2)
    sweep(eb2, ea2, r2, faces, w2, 5, 14, 2, 2)

    even = is_even("gx", 1).astype(jnp.int32)
    for part, first, tile, count in ((c1a, 1 + 12 * even, 15, 4), (l1_ext, 5, 0, 8), (c1b, 13 - 12 * even, 15, 4)):
        for k in range(count):
            sides, own = part[tile + 2 * k], part[tile + 2 * k + 1]
            for ref, which in ((r1, 0), (u1, 1)):
                edge = keep(sides, 0, which)
                ref[first + k, 0:8] = edge
                ref[first + k, 8:16] = keep(own, 0, which)
                ref[first + k, 16:24] = edge

    def start1(plane):
        values = (u2[plane] + eb2[plane])[5:15]
        return values

    for plane in range(5, 15):
        values = start1(plane)
        for k in range(2):
            target = 5 + 2 * (plane - 8) + k
            if 0 <= target < 18:
                ea1[target, pl.ds(2, 10, stride=2), :] = values
                ea1[target, pl.ds(3, 10, stride=2), :] = values
    inside(ea1, w1, 1, 16, 4)
    faces = (fx1, fy1, fz1)
    for plane in (0, 17):
        ea1[plane] = jnp.where(edge_inside(gx, plane), ea1[plane], 0.0)
    sweep(eb1, ea1, r1, faces, w1, 1, 16, 4, 1)
    sweep(ea1, eb1, r1, faces, w1, 2, 15, 2, 1)
    sweep(eb1, ea1, r1, faces, w1, 3, 14, 4, 1)

    for plane in range(3, 15):
        values = u1[plane] + eb1[plane]
        for k in range(2):
            target = 3 + 2 * (plane - 5) + k
            if 0 <= target < 22:
                for parity in range(2):
                    ea0[target, pl.ds(4 + parity, 10, stride=2), :] = values[6:16]
                    ea0[target, pl.ds(parity, 2, stride=2), :] = values[16:18]
    inside(ea0, w0, 0, 21, 2)
    faces = (fx0, fy0, fz0)
    sweep(eb0, ea0, r0, faces, w0, 1, 20, 2, 0)
    sweep(ea0, eb0, r0, faces, w0, 2, 19, 2, 0)

    def last(plane):
        v, total = beside(ea0, faces, plane, 2, 0)
        here = pl.ds(plane, 2)
        values = (1.0 - OMEGA) * v + w0[here] * (r0[here] + total)
        out[pl.ds(plane - 3, 2)] = u0[pl.ds(plane - 3, 2)] + values[:, 8:24]

    loop(3, 18, 2, last)


def edge_inside(gx, plane):
    where = 8 * gx + plane - 5
    return (where >= 0) & (where < 8 * lax.axis_size("gx"))


def swapped(values, axis, step, odd):
    pairs = []
    for k in range(lax.axis_size(axis) - step):
        if (k // step) % 2 == odd:
            pairs += [(k, k + step), (k + step, k)]
    return lax.ppermute(values, axis, pairs)


def is_even(axis, step):
    return lax.rem(lax.div(lax.axis_index(axis), step), 2) == 0


def local(source, dielectric, screening):
    fields = (dielectric, source, screening)
    sems = [pltpu.SemaphoreType.DMA((6,))]
    xa, xb = call(x_strips_kernel, [array(28, 16, LANES)] * 2, sems, 2, 10_000, *fields, space=pl.ANY)
    xa, xb = swapped(xa, "gx", 1, 0), swapped(xb, "gx", 1, 1)
    ya, yb = call(y_strips_kernel, [array(130, 8, LANES)] * 2, [], 2, 10_000, *fields, xa, xb)
    ya, yb = swapped(ya, "gy", 1, 0), swapped(yb, "gy", 1, 1)

    big, mid = pltpu.VMEM((36, 40, LANES), F32), pltpu.VMEM((18, 24, LANES), F32)
    outs = [array(16, 16, LANES)] + [array(22, 24, LANES)] * 5 + [array(18, 24, LANES)] * 4
    outs += [array(8, 8, LANES), array(3, 8, LANES), array(7, 8, LANES), array(7, 8, LANES)]
    made = call(down_kernel, outs, [big] * 10 + [mid] * 4, 12, 10_000_000, *fields, xa, xb, ya, yb)
    fine, level1, (l1_own, l2_own, sa, sb) = made[0:6], made[6:10], made[10:14]

    a1a, a1b = swapped(sa, "gy", 1, 0), swapped(sb, "gy", 1, 1)
    a2a, a2b = swapped(l2_own, "gy", 2, 0), swapped(l2_own, "gy", 2, 1)
    outs = [array(15, 8, LANES), array(23, 8, LANES), array(23, 8, LANES), array(16, 8, LANES)]
    main, sa, sb, l1_ext = call(window_kernel, outs, [], 2, 10_000, l2_own, l1_own, a1a, a1b, a2a, a2b)
    c1a, c1b = swapped(sa, "gx", 1, 0), swapped(sb, "gx", 1, 1)
    c2a, c2b = swapped(main, "gx", 2, 0), swapped(main, "gx", 2, 1)

    two = pltpu.VMEM((20, 24, LANES), F32)
    outs = [array(20, 24, LANES)] * 6 + [array(640, LANES)]
    scratch = [two] * 4 + [pltpu.VMEM((5, 10, 8, LANES), F32)]
    *level2, payload = call(level2_kernel, outs, scratch, 4, 5_000_000, main, c1a, c1b, c2a, c2b)

    n_x, n_y = lax.axis_size("gx"), lax.axis_size("gy")
    groups = [
        [(2 * a + p) * n_y + 2 * b + q for a in range(n_x // 2) for b in range(n_y // 2)]
        for p in range(2)
        for q in range(2)
    ]
    payload = payload.reshape(320, 2, LANES)
    got = lax.all_to_all(payload, ("gx", "gy"), 0, 0, tiled=True, axis_index_groups=groups)
    got = got.reshape(640, LANES)

    scratch = [pltpu.VMEM((2, 96, LANES), F32), pltpu.VMEM((12, 16, LANES), F32)]
    scratch += [two] * 2 + [mid] * 4 + [pltpu.VMEM((22, 24, LANES), F32)] * 2
    (result,) = call(
        up_kernel, [array(16, 16, LANES)], scratch, 6, 10_000_000,
        got, *fine, *level1, l1_ext, c1a, c1b, *level2,
    )
    return result


def solution(mesh):
    spec = P("gx", "gy", None)
    return jax.shard_map(local, mesh=mesh, in_specs=(spec,) * 3, out_specs=spec, check_vma=False)
```

```python
import jax
import jax.numpy as jnp
from jax import lax
from jax.experimental import pallas as pl
from jax.experimental.pallas import tpu as pltpu
from jax.sharding import PartitionSpec as P

OMEGA = 0.8
F32 = jnp.float32
LANES = 128


def roll(values, shift, dim):
    return pltpu.roll(values, shift % values.shape[dim], dim)


def lane_of(values):
    return lax.broadcasted_iota(jnp.int32, values.shape, values.ndim - 1)


def row_of(values):
    return lax.broadcasted_iota(jnp.int32, values.shape, values.ndim - 2)


def bit_of(values, bit):
    return ((lane_of(values) >> bit) & 1) == 1


def pair(values, bit):
    step, dim = 1 << bit, values.ndim - 1
    other = jnp.where(bit_of(values, bit), roll(values, step, dim), roll(values, -step, dim))
    return values + other


def keep(values, bit, want):
    step, dim = 1 << bit, values.ndim - 1
    if want:
        return jnp.where(bit_of(values, bit), values, roll(values, -step, dim))
    return jnp.where(bit_of(values, bit), roll(values, step, dim), values)


def spread(values, which, bits):
    for bit in range(bits):
        values = keep(values, bit, (which >> bit) & 1)
    return values


def relax_factor(diag):
    good = diag > 0.0
    return jnp.where(good, OMEGA / jnp.where(good, diag, 1.0), 0.0)


def loop(first, last, step, body, unroll=4):
    count = (last - first + 1) // step
    assert count * step == last - first + 1
    trips = count // unroll

    def run(index, carry):
        for k in range(unroll):
            body(first + (index * unroll + k) * step)
        return carry

    if trips > 1:
        lax.fori_loop(0, trips, run, 0)
    else:
        trips = 0
    for k in range(trips * unroll, count):
        body(first + k * step)


def beside(vals, faces, plane, count, level, rows):
    fx, fy, fz = faces
    shift = 1 << level
    here = pl.ds(plane, count)
    v = vals[here, rows]
    y_face, z_face = fy[here, rows], fz[here, rows]
    total = fx[here, rows] * vals[pl.ds(plane - 1, count), rows]
    total = total + fx[pl.ds(plane + 1, count), rows] * vals[pl.ds(plane + 1, count), rows]
    total = total + y_face * roll(v, 1, 1) + roll(y_face * v, -1, 1)
    total = total + z_face * roll(v, shift, 2) + roll(z_face * v, -shift, 2)
    return v, total


def sweep(out, vals, side, faces, weight, first, last, step, level, unroll=4, rows=slice(None)):
    def body(plane):
        v, total = beside(vals, faces, plane, step, level, rows)
        here = pl.ds(plane, step)
        out[here, rows] = (1.0 - OMEGA) * v + weight[here, rows] * (side[here, rows] + total)

    loop(first, last, step, body, unroll)


def remains(out, vals, side, faces, diag, first, last, step, level, unroll=4, rows=slice(None)):
    def body(plane):
        v, total = beside(vals, faces, plane, step, level, rows)
        here = pl.ds(plane, step)
        out[here, rows] = side[here, rows] - diag[here, rows] * v + total

    loop(first, last, step, body, unroll)


def block_sum(ref, plane, start, count):
    even, odd = pl.ds(start, count, stride=2), pl.ds(start + 1, count, stride=2)
    low = ref[plane, even, :] + ref[plane, odd, :]
    return low + (ref[plane + 1, even, :] + ref[plane + 1, odd, :])


def coarse_stencil(faces, diag, plane, start, count, level):
    fx, fy, fz = faces
    even, odd = pl.ds(start, count, stride=2), pl.ds(start + 1, count, stride=2)
    x_low = fx[plane, even, :] + fx[plane, odd, :]
    x_mid = fx[plane + 1, even, :] + fx[plane + 1, odd, :]
    y_low = fy[plane, even, :] + fy[plane + 1, even, :]
    y_mid = fy[plane, odd, :] + fy[plane + 1, odd, :]
    z_sum = block_sum(fz, plane, start, count)
    d_sum = block_sum(diag, plane, start, count)
    d_new = pair(d_sum - 2.0 * (x_mid + y_mid), level) - 2.0 * keep(z_sum, level, 1)
    return pair(x_low, level), pair(y_low, level), keep(z_sum, level, 0), d_new


def call(body, outs, scratch, limit, flops, *args, space=pltpu.VMEM):
    nbytes = sum(4 * a.size for a in args) + sum(4 * o.size for o in outs)
    return pl.pallas_call(
        body,
        out_shape=outs,
        in_specs=[pl.BlockSpec(memory_space=space)] * len(args),
        out_specs=[pl.BlockSpec(memory_space=pltpu.VMEM)] * len(outs),
        scratch_shapes=scratch,
        compiler_params=pltpu.CompilerParams(vmem_limit_bytes=limit << 20),
        cost_estimate=pl.CostEstimate(flops=flops, bytes_accessed=nbytes, transcendentals=0),
    )(*args)


def array(*shape):
    return jax.ShapeDtypeStruct(shape, F32)


def y_strips_kernel(eps, src, scr, xa, xb, first, second):
    x_even = is_even("gx", 1)
    y_even = is_even("gy", 1)

    def fill(up, down, xl, xr):
        at = 0
        for own, start, wide in ((eps, 0, 9), (src, 10, 8), (scr, 19, 8)):
            for part, low, count in ((xl, start + 1, wide), (own, 0, 16), (xr, start, wide)):
                up[at : at + count] = part[low : low + count, 8:16]
                down[at : at + count] = part[low : low + count, 0:8]
                at += count
        edges = [(xl, 9)] + [(eps, k) for k in range(16)] + [(xr, 0)]
        edges += [(src, k) for k in range(16)] + [(scr, k) for k in range(16)]
        for k, (part, plane) in enumerate(edges):
            tile, row = 98 + k // 4, 2 * (k % 4)
            up[tile, row : row + 2] = part[plane, 6:8]
            down[tile, row : row + 2] = part[plane, 8:10]

    for x_want, (xl, xr) in ((True, (xb, xa)), (False, (xa, xb))):
        for y_want, (up, down) in ((True, (first, second)), (False, (second, first))):
            pl.when((x_even == x_want) & (y_even == y_want))(
                lambda up=up, down=down, xl=xl, xr=xr: fill(up, down, xl, xr)
            )


def down_kernel(
    eps, src, scr, xa, xb, ya, yb,
    u0_out, fx0_out, fy0_out, fz0_out, w0_out, r0_out,
    fx1, fy1, fz1, w1, l1_own, s2, b2, ship_a, ship_b,
    e, b, s, fx, fy, fz, w, d, ua, ub, b1, d1, va, vb,
):
    x_even = is_even("gx", 1).astype(jnp.int32)
    y_even = is_even("gy", 1)
    row_a = pl.multiple_of(8 + 24 * y_even.astype(jnp.int32), 8)
    row_b = pl.multiple_of(32 - 24 * y_even.astype(jnp.int32), 8)
    at, edge = 0, 0
    blank = jnp.zeros((8, LANES), F32)
    for ref, own, start, wide, margin in ((e, eps, 0, 10, 1), (b, src, 10, 9, 0), (s, scr, 19, 9, 0)):
        first, planes = 11 - wide, 14 + 2 * wide
        ref[10:26, 16:32] = own[...]
        ref[pl.ds(first - 1 + (27 - first) * x_even, wide), 16:32] = xa[start : start + wide]
        ref[pl.ds(26 - (27 - first) * x_even, wide), 16:32] = xb[start : start + wide]
        ref[first : first + planes, pl.ds(row_a, 8)] = ya[at : at + planes]
        ref[first : first + planes, pl.ds(row_b, 8)] = yb[at : at + planes]
        for plane in (first - 1, first + planes):
            ref[plane, 8:16] = blank
            ref[plane, 32:40] = blank
        for plane in range(first - 1, first + planes + 1):
            if not 10 - margin <= plane < 26 + margin:
                ref[plane, 0:8] = blank

        def fill(below_ref, above_ref, ref=ref, margin=margin, edge=edge):
            for k in range(16 + 2 * margin):
                tile, row = 98 + (edge + k) // 4, 2 * ((edge + k) % 4)
                below, above = below_ref[tile], above_ref[tile]
                rows = row_of(below)
                ref[10 - margin + k, 0:8] = jnp.where(
                    rows < 2, roll(above, -row, 0), jnp.where(rows >= 6, roll(below, 6 - row, 0), 0.0)
                )

        pl.when(y_even)(lambda fill=fill: fill(yb, ya))
        pl.when(jnp.logical_not(y_even))(lambda fill=fill: fill(ya, yb))
        at += planes
        edge += 16 + 2 * margin

    def stencil(plane):
        cells = e[pl.ds(plane - 1, 4)]
        centre = cells[1:3]
        x_face = 0.5 * (cells[0:3] + cells[1:4])
        y_face = 0.5 * (centre + roll(centre, 1, 1))
        lanes = lane_of(centre)
        z_face = jnp.where(lanes == 0, 0.0, 0.5 * (centre + roll(centre, 1, 2)))
        ends = jnp.where((lanes == 0) | (lanes == LANES - 1), 0.5 * centre, 0.0)
        here = pl.ds(plane, 2)
        screen = s[here]
        diag = x_face[0:2] + x_face[1:3] + y_face + roll(y_face, -1, 1)
        diag = diag + z_face + roll(z_face, -1, 2) + screen + ends
        diag = jnp.where(screen > 0.0, diag, 0.0)
        weight = relax_factor(diag)
        fx[pl.ds(plane, 3)] = x_face
        fy[here] = y_face
        fz[here] = z_face
        d[here] = diag
        w[here] = weight
        ua[here] = weight * b[here]

    loop(1, 34, 2, stencil, 8)
    faces = (fx, fy, fz)
    sweep(ub, ua, b, faces, w, 2, 33, 2, 0, 8)
    sweep(ua, ub, b, faces, w, 3, 32, 2, 0, 8, slice(8, 40))
    remains(ub, ua, b, faces, d, 4, 31, 2, 0, 8, slice(8, 40))
    u0_out[...] = ua[10:26, 16:32]

    def keep_window(plane):
        for out, ref in ((fx0_out, fx), (fy0_out, fy), (fz0_out, fz), (w0_out, w), (r0_out, ub)):
            out[plane, 8:24] = ref[plane + 7, 16:32]
            high, low = ref[plane + 7, 32:40], ref[plane + 7, 8:16]
            out[plane, 0:8] = jnp.where(row_of(high) < 4, high, low)

    loop(0, 21, 1, keep_window, 8)

    def to_level1(plane):
        x_face, y_face, z_face, diag = coarse_stencil(faces, d, 2 * plane, 0, 20, 0)
        fx1[plane, 0:20] = x_face
        fy1[plane, 0:20] = y_face
        fz1[plane, 0:20] = z_face
        fy1[plane, 20:21] = y_face[0:1]
        d1[plane, 0:20] = diag
        w1[plane, 0:20] = relax_factor(diag)

    for ref in (fx1, fy1, fz1, w1, d1, b1):
        ref[:, 16:24] = jnp.zeros((18, 8, LANES), F32)
    loop(1, 16, 1, to_level1, 8)
    even, odd = pl.ds(0, 20, stride=2), pl.ds(1, 20, stride=2)
    fx1[17, 0:20] = pair(fx[34, even, :] + fx[34, odd, :], 0)

    def side1(plane):
        side = pair(block_sum(ub, 2 * plane, 0, 20), 0)
        b1[plane, 0:20] = side
        va[plane, 0:20] = w1[plane, 0:20] * side

    loop(2, 15, 1, side1, 8)
    va[:, 20:24] = jnp.zeros((18, 4, LANES), F32)
    faces1 = (fx1, fy1, fz1)
    sweep(vb, va, b1, faces1, w1, 3, 14, 4, 1)
    sweep(va, vb, b1, faces1, w1, 4, 13, 2, 1)
    remains(vb, va, b1, faces1, d1, 5, 12, 4, 1)

    own = jnp.where(bit_of(va[5:13, 8:16], 0), va[5:13, 8:16], vb[5:13, 8:16])
    l1_own[...] = own
    quarter = lax.broadcasted_iota(jnp.int32, (8, LANES), 1) & 3
    for m in range(8):
        parts = coarse_stencil(faces1, d1, 1 + 2 * m, 4, 8, 1)
        stack = parts[3]
        for q in range(3):
            stack = jnp.where(quarter == q, parts[q], stack)
        s2[m] = stack
    packed = jnp.zeros((4, LANES), F32)
    for k in range(4):
        packed = jnp.where(quarter[0:4] == k, pair(block_sum(vb, 5 + 2 * k, 8, 4), 1), packed)
    b2[0, 0:4] = packed
    b2[0, 4:8] = jnp.zeros((4, LANES), F32)
    for ship in (ship_a, ship_b):
        ship[0:8] = s2[...]
        ship[8:9] = b2[...]
    for t in range(4):
        first, second = l1_own[2 * t], l1_own[2 * t + 1]
        low = row_of(first) < 4
        up = jnp.where(low, roll(first, -4, 0), second)
        down = jnp.where(low, first, roll(second, 4, 0))
        ship_a[9 + t] = jnp.where(y_even, up, down)
        ship_b[9 + t] = jnp.where(y_even, down, up)


def window_kernel(s2, b2, l1_own, a1a, a1b, s2_wide, b2_wide, l1_ext, ship_a, ship_b):
    y_even = is_even("gy", 1)
    rows = lax.broadcasted_iota(jnp.int32, (8, LANES), 0)

    def join(below, above):
        for m in range(8):
            s2_wide[2 * m] = jnp.where(rows < 6, below[m], roll(s2[m], 4, 0))
            s2_wide[2 * m + 1] = jnp.where(rows < 2, roll(s2[m], -4, 0), above[m])
        b2_wide[0] = jnp.where(rows < 6, roll(below[8], 2, 0), roll(b2[0], 6, 0))
        b2_wide[1] = jnp.where(rows < 2, roll(b2[0], -2, 0), roll(above[8], 2, 0))
        for k in range(8):
            t, turn = 9 + k // 2, 4 * (k % 2)
            l1_ext[2 * k] = jnp.where(rows < 4, roll(above[t], -turn, 0), roll(below[t], 4 - turn, 0))
            l1_ext[2 * k + 1] = l1_own[k]

    pl.when(y_even)(lambda: join(a1b, a1a))
    pl.when(jnp.logical_not(y_even))(lambda: join(a1a, a1b))
    up = is_even("gx", 1).astype(jnp.int32)
    for ship, way in ((ship_a, up), (ship_b, 1 - up)):
        ship[0:12] = s2_wide[pl.ds(4 - 4 * way, 12)]
        ship[12:14] = b2_wide[...]
        ship[14:22] = l1_ext[pl.ds(8 * way, 8)]


def level2_kernel(
    s2_wide, b2_wide, c1a, c1b,
    fx, fy, fz, w, payload,
    d, b, ua, ub, piece,
):
    up = is_even("gx", 1).astype(jnp.int32)
    b[0:2] = jnp.zeros((2, 16, LANES), F32)
    b[14:16] = jnp.zeros((2, 16, LANES), F32)
    for part, tile, first, count in ((s2_wide, 4, 6, 4), (c1a, 0, 10 * up, 6), (c1b, 0, 10 - 10 * up, 6)):
        for k in range(count):
            tiles = jnp.concatenate([part[tile + 2 * k], part[tile + 2 * k + 1]], axis=0)
            fx[first + k] = spread(tiles, 0, 2)
            fy[first + k] = spread(tiles, 1, 2)
            fz[first + k] = spread(tiles, 2, 2)
            diag = spread(tiles, 3, 2)
            d[first + k] = diag
            w[first + k] = relax_factor(diag)
    for part, tile, first in ((b2_wide, 0, 6), (c1a, 12, 2 + 8 * up), (c1b, 12, 10 - 8 * up)):
        tiles = jnp.concatenate([part[tile], part[tile + 1]], axis=0)
        for k in range(4):
            b[first + k] = spread(tiles, k, 2)

    def begin(plane):
        here = pl.ds(plane, 4)
        ua[here] = w[here] * b[here]

    loop(0, 15, 4, begin)
    faces = (fx, fy, fz)
    sweep(ub, ua, b, faces, w, 3, 12, 2, 2, 8)
    sweep(ua, ub, b, faces, w, 4, 11, 2, 2, 8)
    remains(ub, ua, b, faces, d, 6, 9, 2, 2, 8)

    gx, gy = lax.axis_index("gx"), lax.axis_index("gy")
    rows = lax.broadcasted_iota(jnp.int32, (2, LANES), 0)
    slot = lax.broadcasted_iota(jnp.int32, (2, LANES), 1) & 7
    lines = [jnp.zeros((2, LANES), F32) for _ in range(3)]
    for x in range(2):
        parts = coarse_stencil(faces, d, 6 + 2 * x, 6, 2, 2)
        x_face, y_face, z_face, diag = parts
        if x == 0:
            x_face = jnp.where(gx == 0, 0.0, x_face)
        y_face = jnp.where((gy == 0) & (rows == 0), 0.0, y_face)
        side = pair(block_sum(ub, 6 + 2 * x, 6, 2), 2)
        for index, values in enumerate((x_face, y_face, z_face, diag, side)):
            chosen = slot == x + 2 * (index % 2) + 4 * rows
            lines[index // 2] = jnp.where(chosen, values, lines[index // 2])
    for k in range(3):
        piece[k : k + 1] = jnp.sum(lines[k], axis=0, keepdims=True)
    quarter = lax.broadcasted_iota(jnp.int32, (4, LANES), 1) & 3
    for ref, row in ((ub, 3), (ua, 7)):
        stack = ref[9, 6:10]
        for k in range(3):
            stack = jnp.where(quarter == k, ref[6 + k, 6:10], stack)
        piece[row : row + 4] = stack
    piece[11:12] = jnp.zeros((1, LANES), F32)
    whole = piece[0:12]
    for k in range(payload.shape[0] // 12):
        payload[12 * k : 12 * k + 12] = whole


def relay_kernel(got, payload, around, piece):
    count = got.shape[0] // 12
    gy = lax.axis_index("gy")
    around[0:24] = jnp.zeros((24, LANES), F32)
    around[24 : 24 + 12 * count] = got[...]
    around[24 + 12 * count : 48 + 12 * count] = jnp.zeros((24, LANES), F32)
    piece[0:count] = got[pl.ds(0, count, stride=12), :]
    piece[count + 24 : 2 * count + 24] = got[pl.ds(1, count, stride=12), :]
    even, odd = got[pl.ds(2, count // 2, stride=24), :], got[pl.ds(14, count // 2, stride=24), :]
    piece[2 * count + 24 :] = jnp.where(bit_of(even, 1), roll(odd, 2, 1), even)
    for target, start, least, most in ((count, 3, -5, 9), (count + 14, 7, -3, 7)):
        for block in range(-2, 3):
            low, high = max(4 * block, least), min(4 * block + 4, most)
            if low < high:
                line = 12 * (gy + block + 2) + start + low - 4 * block
                piece[target + low - least : target + high - least] = around[pl.ds(line, high - low), :]
    whole = piece[...]
    size = piece.shape[0]
    for k in range(payload.shape[0] // size):
        payload[size * k : size * k + size] = whole


def piece_rows(n_y):
    return 5 * n_y // 2 + 24


def level3_beside(v, faces, stride):
    x_face, y_face, z_face = faces
    x_slot, y_bit = lane_of(v) & 3, bit_of(v, 2)
    low = jnp.where(x_slot == 0, roll(roll(v, -3, 1), stride, 0), roll(v, 1, 1))
    product = x_face * v
    high = jnp.where(x_slot == 3, roll(roll(product, 3, 1), -stride, 0), roll(product, -1, 1))
    total = x_face * low + high
    low = jnp.where(y_bit, roll(v, 4, 1), roll(roll(v, -4, 1), 1, 0))
    product = y_face * v
    high = jnp.where(y_bit, roll(roll(product, 4, 1), -1, 0), roll(product, -4, 1))
    total = total + y_face * low + high
    return total + z_face * roll(v, 8, 1) + roll(z_face * v, -8, 1)


def level4_beside(v, x_face, y_face, z_face, stride):
    x_bit = bit_of(v, 1)
    low = jnp.where(x_bit, roll(v, 2, 1), roll(roll(v, -2, 1), stride, 0))
    product = x_face * v
    high = jnp.where(x_bit, roll(roll(product, 2, 1), -stride, 0), roll(product, -2, 1))
    total = x_face * low + high
    total = total + y_face * roll(v, 1, 0) + roll(y_face * v, -1, 0)
    return total + z_face * roll(v, 16, 1) + roll(z_face * v, -16, 1)


def coarse_levels(got, b3, n_x, n_y):
    size = piece_rows(n_y)

    def lines(start, count):
        pair_of = []
        for parity in range(2):
            parts = [got[pl.ds((2 * a + parity) * size + start, count), :] for a in range(n_x // 2)]
            pair_of.append(jnp.concatenate(parts, axis=0))
        return pair_of

    fields = []
    for start in (0, n_y + 24):
        even, odd = lines(start, n_y)
        upper = bit_of(even, 1)
        fields.append(jnp.where(upper, roll(odd, 2, 1), even))
        fields.append(jnp.where(upper, odd, roll(even, -2, 1)))
    even, odd = lines(2 * n_y + 24, n_y // 2)
    upper = bit_of(even, 1)
    half = n_x // 2 * n_y // 2
    b3[pl.ds(0, half, stride=2), :] = jnp.where(upper, roll(odd, 2, 1), even)
    b3[pl.ds(1, half, stride=2), :] = jnp.where(upper, odd, roll(even, -2, 1))
    fields.append(b3[...])
    faces, diag, side = fields[0:3], fields[3], fields[4]
    weight = relax_factor(diag)

    def sweep3(v, side):
        return (1.0 - OMEGA) * v + weight * (side + level3_beside(v, faces, n_y))

    u = weight * side
    u = sweep3(u, side)
    u = sweep3(u, side)
    r = side - diag * u + level3_beside(u, faces, n_y)

    x_sum, y_sum, z_sum = pair(pair(faces[0], 2), 3), pair(pair(faces[1], 0), 3), pair(pair(faces[2], 0), 2)
    x4, y4, z4 = keep(x_sum, 0, 0), keep(y_sum, 2, 0), keep(z_sum, 3, 0)
    inner = keep(x_sum, 0, 1) + keep(y_sum, 2, 1) + keep(z_sum, 3, 1)
    w4 = relax_factor(pair(pair(pair(diag, 0), 2), 3) - 2.0 * inner)
    b4 = pair(pair(pair(r, 0), 2), 3)
    v = w4 * b4
    for _ in range(5):
        v = (1.0 - OMEGA) * v + w4 * (b4 + level4_beside(v, x4, y4, z4, n_y))
    for _ in range(3):
        v = sweep3(v, r)
    return u + v


def up_kernel(
    got, u0, fx0, fy0, fz0, w0, r0,
    fx1, fy1, fz1, w1, l1_ext, c1a, c1b,
    fx2, fy2, fz2, w2,
    out,
    u3, b3, e3, r2, u2, ea2, eb2, r1, u1, ea1, eb1, ea0, eb0,
):
    gx, gy = lax.axis_index("gx"), lax.axis_index("gy")
    n_x, n_y = lax.axis_size("gx"), lax.axis_size("gy")
    size = piece_rows(n_y)
    for block in range(5):
        device = jnp.clip(gx + block - 2, 0, n_x - 1)
        for ref, line in ((r2, n_y - 1), (u2, n_y + 11)):
            tiles = got[pl.ds(device * size + line, 16), :]
            for k in range(4):
                if 0 <= 4 * block - 2 + k < 16:
                    ref[4 * block - 2 + k] = spread(tiles, k, 2)

    u3[48 : 48 + n_x // 2 * n_y] = coarse_levels(got, b3, n_x, n_y)
    for block in range(5):
        device = gx + block
        line = 48 + (lax.div(device, 2) - 1) * n_y + gy - 2
        lower = u3[pl.ds(line, 8), :]
        lower = jnp.where(lax.rem(device, 2) == 1, keep(lower, 1, 1), keep(lower, 1, 0))
        for x in range(2):
            for y in range(2):
                values = keep(keep(lower, 0, x), 2, y)
                e3[2 * block + x, pl.ds(y, 5, stride=2), :] = values[0:5]

    for plane in range(16):
        values = e3[plane // 2 + 1][1:9]
        for k in range(2):
            ea2[plane, pl.ds(k, 8, stride=2), :] = values

    def inside(values, weight, first, last, step):
        def body(plane):
            here = pl.ds(plane, step)
            values[here] = jnp.where(weight[here] > 0.0, values[here], 0.0)

        loop(first, last, step, body)

    inside(ea2, w2, 0, 15, 4)
    faces = (fx2, fy2, fz2)
    sweep(eb2, ea2, r2, faces, w2, 1, 14, 2, 2)
    sweep(ea2, eb2, r2, faces, w2, 2, 13, 4, 2)
    sweep(eb2, ea2, r2, faces, w2, 3, 12, 2, 2)

    even = is_even("gx", 1).astype(jnp.int32)
    for part, first, tile, count in ((c1a, 1 + 12 * even, 14, 4), (l1_ext, 5, 0, 8), (c1b, 13 - 12 * even, 14, 4)):
        for k in range(count):
            sides, own = part[tile + 2 * k], part[tile + 2 * k + 1]
            for ref, which in ((r1, 0), (u1, 1)):
                edge = keep(sides, 0, which)
                ref[first + k, 0:8] = edge
                ref[first + k, 8:16] = keep(own, 0, which)
                ref[first + k, 16:24] = edge

    for plane in range(3, 13):
        values = (u2[plane] + eb2[plane])[3:13]
        for k in range(2):
            target = 2 * plane - 7 + k
            if 0 <= target < 18:
                ea1[target, pl.ds(2, 10, stride=2), :] = values
                ea1[target, pl.ds(3, 10, stride=2), :] = values
    inside(ea1, w1, 1, 16, 4)
    faces = (fx1, fy1, fz1)
    for plane in (0, 17):
        ea1[plane] = jnp.where(edge_inside(gx, plane), ea1[plane], 0.0)
    sweep(eb1, ea1, r1, faces, w1, 1, 16, 4, 1)
    sweep(ea1, eb1, r1, faces, w1, 2, 15, 2, 1)
    sweep(eb1, ea1, r1, faces, w1, 3, 14, 4, 1)

    for plane in range(3, 15):
        values = u1[plane] + eb1[plane]
        for k in range(2):
            target = 3 + 2 * (plane - 5) + k
            if 0 <= target < 22:
                for parity in range(2):
                    ea0[target, pl.ds(4 + parity, 10, stride=2), :] = values[6:16]
                    ea0[target, pl.ds(parity, 2, stride=2), :] = values[16:18]
    inside(ea0, w0, 0, 21, 2)
    faces = (fx0, fy0, fz0)
    sweep(eb0, ea0, r0, faces, w0, 1, 20, 2, 0)
    sweep(ea0, eb0, r0, faces, w0, 2, 19, 2, 0)

    def last(plane):
        v, total = beside(ea0, faces, plane, 2, 0, slice(None))
        here = pl.ds(plane, 2)
        values = (1.0 - OMEGA) * v + w0[here] * (r0[here] + total)
        out[pl.ds(plane - 3, 2)] = u0[pl.ds(plane - 3, 2)] + values[:, 8:24]

    loop(3, 18, 2, last)


def edge_inside(gx, plane):
    where = 8 * gx + plane - 5
    return (where >= 0) & (where < 8 * lax.axis_size("gx"))


def swapped(values, axis, step, odd):
    pairs = []
    for k in range(lax.axis_size(axis) - step):
        if (k // step) % 2 == odd:
            pairs += [(k, k + step), (k + step, k)]
    return lax.ppermute(values, axis, pairs)


def is_even(axis, step):
    return lax.rem(lax.div(lax.axis_index(axis), step), 2) == 0


def local(source, dielectric, screening):
    fields = (dielectric, source, screening)
    even = is_even("gx", 1).astype(jnp.int32)

    def strip(way):
        parts = [lax.dynamic_slice_in_dim(f, way * (16 - n), n, 0) for f, n in zip(fields, (10, 9, 9))]
        return jnp.concatenate(parts, axis=0)

    xa, xb = strip(even), strip(1 - even)
    xa, xb = swapped(xa, "gx", 1, 0), swapped(xb, "gx", 1, 1)
    ya, yb = call(y_strips_kernel, [array(111, 8, LANES)] * 2, [], 2, 10_000, *fields, xa, xb)
    ya, yb = swapped(ya, "gy", 1, 0), swapped(yb, "gy", 1, 1)

    big, mid = pltpu.VMEM((36, 40, LANES), F32), pltpu.VMEM((18, 24, LANES), F32)
    outs = [array(16, 16, LANES)] + [array(22, 24, LANES)] * 5 + [array(18, 24, LANES)] * 4
    outs += [array(8, 8, LANES), array(8, 8, LANES), array(1, 8, LANES), array(13, 8, LANES), array(13, 8, LANES)]
    made = call(down_kernel, outs, [big] * 10 + [mid] * 4, 12, 10_000_000, *fields, xa, xb, ya, yb)
    fine, level1, (l1_own, s2, b2, sa, sb) = made[0:6], made[6:10], made[10:15]

    a1a, a1b = swapped(sa, "gy", 1, 0), swapped(sb, "gy", 1, 1)
    outs = [array(16, 8, LANES), array(2, 8, LANES), array(16, 8, LANES), array(22, 8, LANES), array(22, 8, LANES)]
    s2, b2, l1_ext, sa, sb = call(window_kernel, outs, [], 2, 10_000, s2, b2, l1_own, a1a, a1b)
    c1a, c1b = swapped(sa, "gx", 1, 0), swapped(sb, "gx", 1, 1)

    n_x, n_y = lax.axis_size("gx"), lax.axis_size("gy")
    two, size = pltpu.VMEM((16, 16, LANES), F32), piece_rows(n_y)
    outs = [array(16, 16, LANES)] * 4 + [array(12 * n_y, LANES)]
    scratch = [two] * 4 + [pltpu.VMEM((16, LANES), F32)]
    *level2, payload = call(level2_kernel, outs, scratch, 4, 5_000_000, s2, b2, c1a, c1b)

    payload = payload.reshape(6 * n_y, 2, LANES)
    got = lax.all_to_all(payload, "gy", 0, 0, tiled=True).reshape(12 * n_y, LANES)
    scratch = [pltpu.VMEM((12 * n_y + 48, LANES), F32), pltpu.VMEM((size, LANES), F32)]
    (payload,) = call(relay_kernel, [array(n_x * size, LANES)], scratch, 2, 10_000, got)
    got = lax.all_to_all(payload, "gx", 0, 0, tiled=True)

    scratch = [pltpu.VMEM((n_x // 2 * n_y + extra, LANES), F32) for extra in (96, 0)]
    scratch += [pltpu.VMEM((12, 16, LANES), F32)]
    scratch += [two] * 4 + [mid] * 4 + [pltpu.VMEM((22, 24, LANES), F32)] * 2
    (result,) = call(
        up_kernel, [array(16, 16, LANES)], scratch, 6, 10_000_000,
        got, *fine, *level1, l1_ext, c1a, c1b, *level2,
    )
    return result


def solution(mesh):
    spec = P("gx", "gy", None)
    return jax.shard_map(local, mesh=mesh, in_specs=(spec,) * 3, out_specs=spec, check_vma=False)
```

```python
import jax
import jax.numpy as jnp
from jax import lax
from jax.experimental import pallas as pl
from jax.experimental.pallas import tpu as pltpu
from jax.sharding import PartitionSpec as P

OMEGA = 0.8
F32 = jnp.float32
LANES = 128


def roll(values, shift, dim):
    return pltpu.roll(values, shift % values.shape[dim], dim)


def lane_of(values):
    return lax.broadcasted_iota(jnp.int32, values.shape, values.ndim - 1)


def row_of(values):
    return lax.broadcasted_iota(jnp.int32, values.shape, values.ndim - 2)


def bit_of(values, bit):
    return ((lane_of(values) >> bit) & 1) == 1


def pair(values, bit):
    step, dim = 1 << bit, values.ndim - 1
    other = jnp.where(bit_of(values, bit), roll(values, step, dim), roll(values, -step, dim))
    return values + other


def keep(values, bit, want):
    step, dim = 1 << bit, values.ndim - 1
    if want:
        return jnp.where(bit_of(values, bit), values, roll(values, -step, dim))
    return jnp.where(bit_of(values, bit), roll(values, step, dim), values)


def spread(values, which, bits):
    for bit in range(bits):
        values = keep(values, bit, (which >> bit) & 1)
    return values


def relax_factor(diag):
    good = diag > 0.0
    return jnp.where(good, OMEGA / jnp.where(good, diag, 1.0), 0.0)


def loop(first, last, step, body, unroll=4):
    count = (last - first + 1) // step
    assert count * step == last - first + 1
    trips = count // unroll

    def run(index, carry):
        for k in range(unroll):
            body(first + (index * unroll + k) * step)
        return carry

    if trips > 1:
        lax.fori_loop(0, trips, run, 0)
    else:
        trips = 0
    for k in range(trips * unroll, count):
        body(first + k * step)


def beside(vals, faces, plane, count, level, rows):
    fx, fy, fz = faces
    shift = 1 << level
    here = pl.ds(plane, count)
    v = vals[here, rows]
    y_face, z_face = fy[here, rows], fz[here, rows]
    total = fx[here, rows] * vals[pl.ds(plane - 1, count), rows]
    total = total + fx[pl.ds(plane + 1, count), rows] * vals[pl.ds(plane + 1, count), rows]
    total = total + y_face * roll(v, 1, 1) + roll(y_face * v, -1, 1)
    total = total + z_face * roll(v, shift, 2) + roll(z_face * v, -shift, 2)
    return v, total


def sweep(out, vals, side, faces, weight, first, last, step, level, unroll=4, rows=slice(None)):
    def body(plane):
        v, total = beside(vals, faces, plane, step, level, rows)
        here = pl.ds(plane, step)
        out[here, rows] = (1.0 - OMEGA) * v + weight[here, rows] * (side[here, rows] + total)

    loop(first, last, step, body, unroll)


def remains(out, vals, side, faces, diag, first, last, step, level, unroll=4, rows=slice(None)):
    def body(plane):
        v, total = beside(vals, faces, plane, step, level, rows)
        here = pl.ds(plane, step)
        out[here, rows] = side[here, rows] - diag[here, rows] * v + total

    loop(first, last, step, body, unroll)


def block_sum(ref, plane, start, count):
    even, odd = pl.ds(start, count, stride=2), pl.ds(start + 1, count, stride=2)
    low = ref[plane, even, :] + ref[plane, odd, :]
    return low + (ref[plane + 1, even, :] + ref[plane + 1, odd, :])


def coarse_stencil(faces, diag, plane, start, count, level):
    fx, fy, fz = faces
    even, odd = pl.ds(start, count, stride=2), pl.ds(start + 1, count, stride=2)
    x_low = fx[plane, even, :] + fx[plane, odd, :]
    x_mid = fx[plane + 1, even, :] + fx[plane + 1, odd, :]
    y_low = fy[plane, even, :] + fy[plane + 1, even, :]
    y_mid = fy[plane, odd, :] + fy[plane + 1, odd, :]
    z_sum = block_sum(fz, plane, start, count)
    d_sum = block_sum(diag, plane, start, count)
    d_new = pair(d_sum - 2.0 * (x_mid + y_mid), level) - 2.0 * keep(z_sum, level, 1)
    return pair(x_low, level), pair(y_low, level), keep(z_sum, level, 0), d_new


def call(body, outs, scratch, limit, flops, *args, space=pltpu.VMEM):
    nbytes = sum(4 * a.size for a in args) + sum(4 * o.size for o in outs)
    return pl.pallas_call(
        body,
        out_shape=outs,
        in_specs=[pl.BlockSpec(memory_space=space)] * len(args),
        out_specs=[pl.BlockSpec(memory_space=pltpu.VMEM)] * len(outs),
        scratch_shapes=scratch,
        compiler_params=pltpu.CompilerParams(vmem_limit_bytes=limit << 20),
        cost_estimate=pl.CostEstimate(flops=flops, bytes_accessed=nbytes, transcendentals=0),
    )(*args)


def array(*shape):
    return jax.ShapeDtypeStruct(shape, F32)


def y_strips_kernel(eps, src, scr, xa, xb, first, second):
    x_up = first_up("gx", 1)
    y_up = first_up("gy", 1)

    def fill(up, down, xl, xr):
        at = 0
        for own, start, wide in ((eps, 0, 9), (src, 10, 8), (scr, 19, 8)):
            for part, low, count in ((xl, start + 1, wide), (own, 0, 16), (xr, start, wide)):
                up[at : at + count] = part[low : low + count, 8:16]
                down[at : at + count] = part[low : low + count, 0:8]
                at += count
        edges = [(xl, 9)] + [(eps, k) for k in range(16)] + [(xr, 0)]
        edges += [(src, k) for k in range(16)] + [(scr, k) for k in range(16)]
        for k, (part, plane) in enumerate(edges):
            tile, row = 98 + k // 4, 2 * (k % 4)
            up[tile, row : row + 2] = part[plane, 6:8]
            down[tile, row : row + 2] = part[plane, 8:10]

    for x_want, (xl, xr) in ((True, (xb, xa)), (False, (xa, xb))):
        for y_want, (up, down) in ((True, (first, second)), (False, (second, first))):
            pl.when((x_up == x_want) & (y_up == y_want))(
                lambda up=up, down=down, xl=xl, xr=xr: fill(up, down, xl, xr)
            )


def down_kernel(
    eps, src, scr, xa, xb, ya, yb,
    u0_out, fx0_out, fy0_out, fz0_out, w0_out, r0_out,
    fx1, fy1, fz1, w1, l1_own, s2, b2, ship_a, ship_b,
    e, b, s, fx, fy, fz, w, d, ua, ub, b1, d1, va, vb,
):
    x_up = first_up("gx", 1).astype(jnp.int32)
    y_up = first_up("gy", 1)
    row_a = pl.multiple_of(8 + 24 * y_up.astype(jnp.int32), 8)
    row_b = pl.multiple_of(32 - 24 * y_up.astype(jnp.int32), 8)
    at, edge = 0, 0
    blank = jnp.zeros((8, LANES), F32)
    for ref, own, start, wide, margin in ((e, eps, 0, 10, 1), (b, src, 10, 9, 0), (s, scr, 19, 9, 0)):
        first, planes = 11 - wide, 14 + 2 * wide
        ref[10:26, 16:32] = own[...]
        ref[pl.ds(first - 1 + (27 - first) * x_up, wide), 16:32] = xa[start : start + wide]
        ref[pl.ds(26 - (27 - first) * x_up, wide), 16:32] = xb[start : start + wide]
        ref[first : first + planes, pl.ds(row_a, 8)] = ya[at : at + planes]
        ref[first : first + planes, pl.ds(row_b, 8)] = yb[at : at + planes]
        for plane in (first - 1, first + planes):
            ref[plane, 8:16] = blank
            ref[plane, 32:40] = blank
        for plane in range(first - 1, first + planes + 1):
            if not 10 - margin <= plane < 26 + margin:
                ref[plane, 0:8] = blank

        def fill(below_ref, above_ref, ref=ref, margin=margin, edge=edge):
            for k in range(16 + 2 * margin):
                tile, row = 98 + (edge + k) // 4, 2 * ((edge + k) % 4)
                below, above = below_ref[tile], above_ref[tile]
                rows = row_of(below)
                ref[10 - margin + k, 0:8] = jnp.where(
                    rows < 2, roll(above, -row, 0), jnp.where(rows >= 6, roll(below, 6 - row, 0), 0.0)
                )

        pl.when(y_up)(lambda fill=fill: fill(yb, ya))
        pl.when(jnp.logical_not(y_up))(lambda fill=fill: fill(ya, yb))
        at += planes
        edge += 16 + 2 * margin

    def stencil(plane):
        cells = e[pl.ds(plane - 1, 4)]
        centre = cells[1:3]
        x_face = 0.5 * (cells[0:3] + cells[1:4])
        y_face = 0.5 * (centre + roll(centre, 1, 1))
        lanes = lane_of(centre)
        z_face = jnp.where(lanes == 0, 0.0, 0.5 * (centre + roll(centre, 1, 2)))
        ends = jnp.where((lanes == 0) | (lanes == LANES - 1), 0.5 * centre, 0.0)
        here = pl.ds(plane, 2)
        screen = s[here]
        diag = x_face[0:2] + x_face[1:3] + y_face + roll(y_face, -1, 1)
        diag = diag + z_face + roll(z_face, -1, 2) + screen + ends
        diag = jnp.where(screen > 0.0, diag, 0.0)
        weight = relax_factor(diag)
        fx[pl.ds(plane, 3)] = x_face
        fy[here] = y_face
        fz[here] = z_face
        d[here] = diag
        w[here] = weight
        ua[here] = weight * b[here]

    loop(1, 34, 2, stencil, 8)
    faces = (fx, fy, fz)
    sweep(ub, ua, b, faces, w, 2, 33, 2, 0, 8)
    sweep(ua, ub, b, faces, w, 3, 32, 2, 0, 8, slice(8, 40))
    remains(ub, ua, b, faces, d, 4, 31, 2, 0, 8, slice(8, 40))
    u0_out[...] = ua[10:26, 16:32]

    def keep_window(plane):
        for out, ref in ((fx0_out, fx), (fy0_out, fy), (fz0_out, fz), (w0_out, w), (r0_out, ub)):
            out[plane, 8:24] = ref[plane + 7, 16:32]
            high, low = ref[plane + 7, 32:40], ref[plane + 7, 8:16]
            out[plane, 0:8] = jnp.where(row_of(high) < 4, high, low)

    loop(0, 21, 1, keep_window, 8)

    def to_level1(plane):
        x_face, y_face, z_face, diag = coarse_stencil(faces, d, 2 * plane, 0, 20, 0)
        fx1[plane, 0:20] = x_face
        fy1[plane, 0:20] = y_face
        fz1[plane, 0:20] = z_face
        fy1[plane, 20:21] = y_face[0:1]
        d1[plane, 0:20] = diag
        w1[plane, 0:20] = relax_factor(diag)

    for ref in (fx1, fy1, fz1, w1, d1, b1):
        ref[:, 16:24] = jnp.zeros((18, 8, LANES), F32)
    loop(1, 16, 1, to_level1, 8)
    even, odd = pl.ds(0, 20, stride=2), pl.ds(1, 20, stride=2)
    fx1[17, 0:20] = pair(fx[34, even, :] + fx[34, odd, :], 0)

    def side1(plane):
        side = pair(block_sum(ub, 2 * plane, 0, 20), 0)
        b1[plane, 0:20] = side
        va[plane, 0:20] = w1[plane, 0:20] * side

    loop(2, 15, 1, side1, 8)
    va[:, 20:24] = jnp.zeros((18, 4, LANES), F32)
    faces1 = (fx1, fy1, fz1)
    sweep(vb, va, b1, faces1, w1, 3, 14, 4, 1)
    sweep(va, vb, b1, faces1, w1, 4, 13, 2, 1)
    remains(vb, va, b1, faces1, d1, 5, 12, 4, 1)

    own = jnp.where(bit_of(va[5:13, 8:16], 0), va[5:13, 8:16], vb[5:13, 8:16])
    l1_own[...] = own
    quarter = lax.broadcasted_iota(jnp.int32, (8, LANES), 1) & 3
    for m in range(8):
        parts = coarse_stencil(faces1, d1, 1 + 2 * m, 4, 8, 1)
        stack = parts[3]
        for q in range(3):
            stack = jnp.where(quarter == q, parts[q], stack)
        s2[m] = stack
    packed = jnp.zeros((4, LANES), F32)
    for k in range(4):
        packed = jnp.where(quarter[0:4] == k, pair(block_sum(vb, 5 + 2 * k, 8, 4), 1), packed)
    b2[0, 0:4] = packed
    b2[0, 4:8] = jnp.zeros((4, LANES), F32)
    for ship in (ship_a, ship_b):
        ship[0:8] = s2[...]
        ship[8:9] = b2[...]
    for t in range(4):
        first, second = l1_own[2 * t], l1_own[2 * t + 1]
        low = row_of(first) < 4
        up = jnp.where(low, roll(first, -4, 0), second)
        down = jnp.where(low, first, roll(second, 4, 0))
        ship_a[9 + t] = jnp.where(y_up, up, down)
        ship_b[9 + t] = jnp.where(y_up, down, up)


def window_kernel(s2, b2, l1_own, a1a, a1b, s2_wide, b2_wide, l1_ext, ship_a, ship_b):
    y_up = first_up("gy", 1)
    rows = lax.broadcasted_iota(jnp.int32, (8, LANES), 0)

    def join(below, above):
        for m in range(8):
            s2_wide[2 * m] = jnp.where(rows < 6, below[m], roll(s2[m], 4, 0))
            s2_wide[2 * m + 1] = jnp.where(rows < 2, roll(s2[m], -4, 0), above[m])
        b2_wide[0] = jnp.where(rows < 6, roll(below[8], 2, 0), roll(b2[0], 6, 0))
        b2_wide[1] = jnp.where(rows < 2, roll(b2[0], -2, 0), roll(above[8], 2, 0))
        for k in range(8):
            t, turn = 9 + k // 2, 4 * (k % 2)
            l1_ext[2 * k] = jnp.where(rows < 4, roll(above[t], -turn, 0), roll(below[t], 4 - turn, 0))
            l1_ext[2 * k + 1] = l1_own[k]

    pl.when(y_up)(lambda: join(a1b, a1a))
    pl.when(jnp.logical_not(y_up))(lambda: join(a1a, a1b))
    up = first_up("gx", 1).astype(jnp.int32)
    for ship, way in ((ship_a, up), (ship_b, 1 - up)):
        ship[0:12] = s2_wide[pl.ds(4 - 4 * way, 12)]
        ship[12:14] = b2_wide[...]
        ship[14:22] = l1_ext[pl.ds(8 * way, 8)]


def level2_kernel(
    s2_wide, b2_wide, c1a, c1b,
    fx, fy, fz, w, payload,
    d, b, ua, ub, piece,
):
    up = first_up("gx", 1).astype(jnp.int32)
    b[0:2] = jnp.zeros((2, 16, LANES), F32)
    b[14:16] = jnp.zeros((2, 16, LANES), F32)
    for part, tile, first, count in ((s2_wide, 4, 6, 4), (c1a, 0, 10 * up, 6), (c1b, 0, 10 - 10 * up, 6)):
        for k in range(count):
            tiles = jnp.concatenate([part[tile + 2 * k], part[tile + 2 * k + 1]], axis=0)
            fx[first + k] = spread(tiles, 0, 2)
            fy[first + k] = spread(tiles, 1, 2)
            fz[first + k] = spread(tiles, 2, 2)
            diag = spread(tiles, 3, 2)
            d[first + k] = diag
            w[first + k] = relax_factor(diag)
    for part, tile, first in ((b2_wide, 0, 6), (c1a, 12, 2 + 8 * up), (c1b, 12, 10 - 8 * up)):
        tiles = jnp.concatenate([part[tile], part[tile + 1]], axis=0)
        for k in range(4):
            b[first + k] = spread(tiles, k, 2)

    def begin(plane):
        here = pl.ds(plane, 4)
        ua[here] = w[here] * b[here]

    loop(0, 15, 4, begin)
    faces = (fx, fy, fz)
    sweep(ub, ua, b, faces, w, 3, 12, 2, 2, 8)
    sweep(ua, ub, b, faces, w, 4, 11, 2, 2, 8)
    remains(ub, ua, b, faces, d, 6, 9, 2, 2, 8)

    gx, gy = lax.axis_index("gx"), lax.axis_index("gy")
    rows = lax.broadcasted_iota(jnp.int32, (2, LANES), 0)
    slot = lax.broadcasted_iota(jnp.int32, (2, LANES), 1) & 7
    lines = [jnp.zeros((2, LANES), F32) for _ in range(3)]
    for x in range(2):
        parts = coarse_stencil(faces, d, 6 + 2 * x, 6, 2, 2)
        x_face, y_face, z_face, diag = parts
        if x == 0:
            x_face = jnp.where(gx == 0, 0.0, x_face)
        y_face = jnp.where((gy == 0) & (rows == 0), 0.0, y_face)
        side = pair(block_sum(ub, 6 + 2 * x, 6, 2), 2)
        for index, values in enumerate((x_face, y_face, z_face, diag, side)):
            chosen = slot == (x + 2 * rows if index == 4 else x + 2 * (index % 2) + 4 * rows)
            lines[index // 2] = jnp.where(chosen, values, lines[index // 2])
    for k in range(3):
        piece[k : k + 1] = jnp.sum(lines[k], axis=0, keepdims=True)
    quarter = lax.broadcasted_iota(jnp.int32, (4, LANES), 1) & 3
    for ref, row in ((ub, 3), (ua, 7)):
        stack = ref[9, 6:10]
        for k in range(3):
            stack = jnp.where(quarter == k, ref[6 + k, 6:10], stack)
        piece[row : row + 4] = stack
    piece[11:12] = jnp.zeros((1, LANES), F32)
    whole = piece[0:12]
    for k in range(payload.shape[0] // 12):
        payload[12 * k : 12 * k + 12] = whole


def relay_kernel(got, payload, around, piece):
    count = got.shape[0] // 12
    gy = lax.axis_index("gy")
    around[0:24] = jnp.zeros((24, LANES), F32)
    around[24 : 24 + 12 * count] = got[...]
    around[24 + 12 * count : 48 + 12 * count] = jnp.zeros((24, LANES), F32)
    first, second = got[pl.ds(0, count, stride=12), :], got[pl.ds(1, count, stride=12), :]
    upper = bit_of(first, 2)
    piece[pl.ds(0, count, stride=2), :] = jnp.where(upper, roll(second, 4, 1), first)
    piece[pl.ds(1, count, stride=2), :] = jnp.where(upper, second, roll(first, -4, 1))
    even, odd = got[pl.ds(2, count // 2, stride=24), :], got[pl.ds(14, count // 2, stride=24), :]
    piece[2 * count + 24 :] = jnp.where(bit_of(even, 2), roll(odd, 4, 1), even)
    for target, start, least, most in ((2 * count, 3, -5, 9), (2 * count + 14, 7, -3, 7)):
        for block in range(-2, 3):
            low, high = max(4 * block, least), min(4 * block + 4, most)
            if low < high:
                line = 12 * (gy + block + 2) + start + low - 4 * block
                piece[target + low - least : target + high - least] = around[pl.ds(line, high - low), :]
    whole = piece[...]
    size = piece.shape[0]
    for k in range(payload.shape[0] // size):
        payload[size * k : size * k + size] = whole


def piece_rows(n_y):
    return 5 * n_y // 2 + 24


def x_low(values, rows):
    slot = lane_of(values) & 7
    return jnp.where(slot == 0, roll(roll(values, -7, 1), rows, 0), roll(values, 1, 1))


def x_high(values, rows):
    slot = lane_of(values) & 7
    return jnp.where(slot == 7, roll(roll(values, 7, 1), -rows, 0), roll(values, -1, 1))


def yz_beside(v, y_face, z_face, level):
    total = y_face * roll(v, 1 + level, 0) + roll(y_face * v, -1 - level, 0)
    return total + z_face * roll(v, 8 + 8 * level, 1) + roll(z_face * v, -8 - 8 * level, 1)


def level3_beside(v, faces, rows):
    (x0, x1), y_faces, z_faces = faces
    totals = [x0 * x_low(v[1], rows) + x1 * v[1], x1 * v[0] + x_high(x0 * v[0], rows)]
    return [totals[k] + yz_beside(v[k], y_faces[k], z_faces[k], 0) for k in range(2)]


def row_pair(values):
    odd = (row_of(values) & 1) == 1
    return values + jnp.where(odd, roll(values, 1, 0), roll(values, -1, 0))


def row_keep(values, want):
    odd = (row_of(values) & 1) == 1
    if want:
        return jnp.where(odd, values, roll(values, -1, 0))
    return jnp.where(odd, roll(values, 1, 0), values)


def exchange_slots(tiles):
    for bit in range(3):
        step = 1 << bit
        upper = bit_of(tiles[0], bit)
        made = list(tiles)
        for k in range(8):
            if not k & step:
                made[k] = jnp.where(upper, roll(tiles[k + step], step, 1), tiles[k])
                made[k + step] = jnp.where(upper, tiles[k + step], roll(tiles[k], -step, 1))
        tiles = made
    return tiles


def coarse_levels(got, b3, n_x, n_y):
    size, rows = piece_rows(n_y), 2 * n_y
    groups = []
    for g in range(n_x // 8):
        lines = [(8 * g + q) * size for q in range(8)]
        groups.append(exchange_slots([got[line : line + rows] for line in lines]))
        sides = exchange_slots([got[line + rows + 24 : line + size] for line in lines])
        for k in range(8):
            b3[k % 2, pl.ds(g * rows + k // 2, n_y // 2, stride=4), :] = sides[k]
    fields = []
    for index in range(4):
        fields.append([jnp.concatenate([g[2 * index + x] for g in groups], axis=0) for x in range(2)])
    faces, diag = fields[0:3], fields[3]
    side = [b3[0], b3[1]]
    weight = [relax_factor(d) for d in diag]

    def sweep3(v, side):
        total = level3_beside(v, faces, rows)
        return [(1.0 - OMEGA) * v[k] + weight[k] * (side[k] + total[k]) for k in range(2)]

    u = [weight[k] * side[k] for k in range(2)]
    u = sweep3(u, side)
    u = sweep3(u, side)
    total = level3_beside(u, faces, rows)
    r = [side[k] - diag[k] * u[k] + total[k] for k in range(2)]

    (x0, x1), (y0, y1), (z0, z1) = faces
    y_sum, z_sum = pair(y0 + y1, 3), row_pair(z0 + z1)
    x4, y4, z4 = row_pair(pair(x0, 3)), row_keep(y_sum, 0), keep(z_sum, 3, 0)
    inner = row_keep(y_sum, 1) + keep(z_sum, 3, 1)
    w4 = relax_factor(row_pair(pair(diag[0] + diag[1] - 2.0 * x1, 3)) - 2.0 * inner)
    b4 = row_pair(pair(r[0] + r[1], 3))
    v = w4 * b4
    for _ in range(5):
        total = x4 * x_low(v, rows) + x_high(x4 * v, rows) + yz_beside(v, y4, z4, 1)
        v = (1.0 - OMEGA) * v + w4 * (b4 + total)
    c = [v, v]
    for _ in range(3):
        c = sweep3(c, r)
    return [u[k] + c[k] for k in range(2)]


def up_kernel(
    got, u0, fx0, fy0, fz0, w0, r0,
    fx1, fy1, fz1, w1, l1_ext, c1a, c1b,
    fx2, fy2, fz2, w2,
    out,
    u3, b3, e3, r2, u2, ea2, eb2, r1, u1, ea1, eb1, ea0, eb0,
):
    gx, gy = lax.axis_index("gx"), lax.axis_index("gy")
    n_x, n_y = lax.axis_size("gx"), lax.axis_size("gy")
    size = piece_rows(n_y)
    for block in range(5):
        device = jnp.clip(gx + block - 2, 0, n_x - 1)
        for ref, line in ((r2, 2 * n_y - 1), (u2, 2 * n_y + 11)):
            tiles = got[pl.ds(device * size + line, 16), :]
            for k in range(4):
                if 0 <= 4 * block - 2 + k < 16:
                    ref[4 * block - 2 + k] = spread(tiles, k, 2)

    solved = coarse_levels(got, b3, n_x, n_y)
    for x in range(2):
        u3[x, 8 : 8 + solved[x].shape[0]] = solved[x]
    for block in range(5):
        device = jnp.clip(gx + block - 2, 0, n_x - 1)
        line = 4 + lax.div(device, 8) * 2 * n_y + 2 * gy
        for x in range(2):
            values = pltpu.roll(u3[x, pl.ds(line, 16), :], lax.rem(LANES - lax.rem(device, 8), LANES), 1)
            e3[2 * block + x] = spread(values, 0, 3)

    for plane in range(16):
        values = e3[plane // 2 + 1][1:9]
        for k in range(2):
            ea2[plane, pl.ds(k, 8, stride=2), :] = values

    def inside(values, weight, first, last, step):
        def body(plane):
            here = pl.ds(plane, step)
            values[here] = jnp.where(weight[here] > 0.0, values[here], 0.0)

        loop(first, last, step, body)

    inside(ea2, w2, 0, 15, 4)
    faces = (fx2, fy2, fz2)
    sweep(eb2, ea2, r2, faces, w2, 1, 14, 2, 2)
    sweep(ea2, eb2, r2, faces, w2, 2, 13, 4, 2)
    sweep(eb2, ea2, r2, faces, w2, 3, 12, 2, 2)

    even = first_up("gx", 1).astype(jnp.int32)
    for part, first, tile, count in ((c1a, 1 + 12 * even, 14, 4), (l1_ext, 5, 0, 8), (c1b, 13 - 12 * even, 14, 4)):
        for k in range(count):
            sides, own = part[tile + 2 * k], part[tile + 2 * k + 1]
            for ref, which in ((r1, 0), (u1, 1)):
                edge = keep(sides, 0, which)
                ref[first + k, 0:8] = edge
                ref[first + k, 8:16] = keep(own, 0, which)
                ref[first + k, 16:24] = edge

    for plane in range(3, 13):
        values = (u2[plane] + eb2[plane])[3:13]
        for k in range(2):
            target = 2 * plane - 7 + k
            if 0 <= target < 18:
                ea1[target, pl.ds(2, 10, stride=2), :] = values
                ea1[target, pl.ds(3, 10, stride=2), :] = values
    inside(ea1, w1, 1, 16, 4)
    faces = (fx1, fy1, fz1)
    for plane in (0, 17):
        ea1[plane] = jnp.where(edge_inside(gx, plane), ea1[plane], 0.0)
    sweep(eb1, ea1, r1, faces, w1, 1, 16, 4, 1)
    sweep(ea1, eb1, r1, faces, w1, 2, 15, 2, 1)
    sweep(eb1, ea1, r1, faces, w1, 3, 14, 4, 1)

    for plane in range(3, 15):
        values = u1[plane] + eb1[plane]
        for k in range(2):
            target = 3 + 2 * (plane - 5) + k
            if 0 <= target < 22:
                for parity in range(2):
                    ea0[target, pl.ds(4 + parity, 10, stride=2), :] = values[6:16]
                    ea0[target, pl.ds(parity, 2, stride=2), :] = values[16:18]
    inside(ea0, w0, 0, 21, 2)
    faces = (fx0, fy0, fz0)
    sweep(eb0, ea0, r0, faces, w0, 1, 20, 2, 0)
    sweep(ea0, eb0, r0, faces, w0, 2, 19, 2, 0)

    def last(plane):
        v, total = beside(ea0, faces, plane, 2, 0, slice(None))
        here = pl.ds(plane, 2)
        values = (1.0 - OMEGA) * v + w0[here] * (r0[here] + total)
        out[pl.ds(plane - 3, 2)] = u0[pl.ds(plane - 3, 2)] + values[:, 8:24]

    loop(3, 18, 2, last)


def edge_inside(gx, plane):
    where = 8 * gx + plane - 5
    return (where >= 0) & (where < 8 * lax.axis_size("gx"))


def swapped(values, axis, step, second):
    pairs = []
    for k in range(lax.axis_size(axis) - step):
        if (k // step) % 2 != second:
            pairs += [(k, k + step), (k + step, k)]
    return lax.ppermute(values, axis, pairs)


def first_up(axis, step):
    return lax.rem(lax.div(lax.axis_index(axis), step), 2) == 1


def local(source, dielectric, screening):
    fields = (dielectric, source, screening)
    even = first_up("gx", 1).astype(jnp.int32)

    def strip(way):
        parts = [lax.dynamic_slice_in_dim(f, way * (16 - n), n, 0) for f, n in zip(fields, (10, 9, 9))]
        return jnp.concatenate(parts, axis=0)

    xa, xb = strip(even), strip(1 - even)
    xa, xb = swapped(xa, "gx", 1, 0), swapped(xb, "gx", 1, 1)
    ya, yb = call(y_strips_kernel, [array(111, 8, LANES)] * 2, [], 2, 10_000, *fields, xa, xb)
    ya, yb = swapped(ya, "gy", 1, 0), swapped(yb, "gy", 1, 1)

    big, mid = pltpu.VMEM((36, 40, LANES), F32), pltpu.VMEM((18, 24, LANES), F32)
    outs = [array(16, 16, LANES)] + [array(22, 24, LANES)] * 5 + [array(18, 24, LANES)] * 4
    outs += [array(8, 8, LANES), array(8, 8, LANES), array(1, 8, LANES), array(13, 8, LANES), array(13, 8, LANES)]
    made = call(down_kernel, outs, [big] * 10 + [mid] * 4, 12, 10_000_000, *fields, xa, xb, ya, yb)
    fine, level1, (l1_own, s2, b2, sa, sb) = made[0:6], made[6:10], made[10:15]

    a1a, a1b = swapped(sa, "gy", 1, 0), swapped(sb, "gy", 1, 1)
    outs = [array(16, 8, LANES), array(2, 8, LANES), array(16, 8, LANES), array(22, 8, LANES), array(22, 8, LANES)]
    s2, b2, l1_ext, sa, sb = call(window_kernel, outs, [], 2, 10_000, s2, b2, l1_own, a1a, a1b)
    c1a, c1b = swapped(sa, "gx", 1, 0), swapped(sb, "gx", 1, 1)

    n_x, n_y = lax.axis_size("gx"), lax.axis_size("gy")
    two, size = pltpu.VMEM((16, 16, LANES), F32), piece_rows(n_y)
    outs = [array(16, 16, LANES)] * 4 + [array(12 * n_y, LANES)]
    scratch = [two] * 4 + [pltpu.VMEM((16, LANES), F32)]
    *level2, payload = call(level2_kernel, outs, scratch, 4, 5_000_000, s2, b2, c1a, c1b)

    payload = payload.reshape(6 * n_y, 2, LANES)
    got = lax.all_to_all(payload, "gy", 0, 0, tiled=True).reshape(12 * n_y, LANES)
    scratch = [pltpu.VMEM((12 * n_y + 48, LANES), F32), pltpu.VMEM((size, LANES), F32)]
    (payload,) = call(relay_kernel, [array(n_x * size, LANES)], scratch, 2, 10_000, got)
    got = lax.all_to_all(payload, "gx", 0, 0, tiled=True)

    scratch = [pltpu.VMEM((2, n_x // 4 * n_y + extra, LANES), F32) for extra in (24, 0)]
    scratch += [pltpu.VMEM((12, 16, LANES), F32)]
    scratch += [two] * 4 + [mid] * 4 + [pltpu.VMEM((22, 24, LANES), F32)] * 2
    (result,) = call(
        up_kernel, [array(16, 16, LANES)], scratch, 6, 10_000_000,
        got, *fine, *level1, l1_ext, c1a, c1b, *level2,
    )
    return result


def solution(mesh):
    spec = P("gx", "gy", None)
    return jax.shard_map(local, mesh=mesh, in_specs=(spec,) * 3, out_specs=spec, check_vma=False)
```

```python
import jax
import jax.numpy as jnp
from jax import lax
from jax.experimental import pallas as pl
from jax.experimental.pallas import tpu as pltpu
from jax.sharding import PartitionSpec as P

OMEGA = 0.8
F32 = jnp.float32
LANES = 128


def roll(values, shift, dim):
    return pltpu.roll(values, shift % values.shape[dim], dim)


def lane_of(values):
    return lax.broadcasted_iota(jnp.int32, values.shape, values.ndim - 1)


def row_of(values):
    return lax.broadcasted_iota(jnp.int32, values.shape, values.ndim - 2)


def bit_of(values, bit):
    return ((lane_of(values) >> bit) & 1) == 1


def pair(values, bit):
    step, dim = 1 << bit, values.ndim - 1
    other = jnp.where(bit_of(values, bit), roll(values, step, dim), roll(values, -step, dim))
    return values + other


def keep(values, bit, want):
    step, dim = 1 << bit, values.ndim - 1
    if want:
        return jnp.where(bit_of(values, bit), values, roll(values, -step, dim))
    return jnp.where(bit_of(values, bit), roll(values, step, dim), values)


def spread(values, which, bits):
    for bit in range(bits):
        values = keep(values, bit, (which >> bit) & 1)
    return values


def relax_factor(diag):
    good = diag > 0.0
    return jnp.where(good, OMEGA / jnp.where(good, diag, 1.0), 0.0)


def loop(first, last, step, body, unroll=16):
    count = (last - first + 1) // step
    assert count * step == last - first + 1
    trips = count // unroll

    def run(index, carry):
        for k in range(unroll):
            body(first + (index * unroll + k) * step)
        return carry

    if trips > 1:
        lax.fori_loop(0, trips, run, 0)
    else:
        trips = 0
    for k in range(trips * unroll, count):
        body(first + k * step)


def beside(vals, faces, plane, count, level, rows, sides=None):
    fx, fy, fz = faces
    shift = 1 << level
    here = pl.ds(plane, count)
    v = vals[here, rows]
    y_face, z_face = fy[here, rows], fz[here, rows]
    total = fx[here, rows] * vals[pl.ds(plane - 1, count), rows]
    total = total + fx[pl.ds(plane + 1, count), rows] * vals[pl.ds(plane + 1, count), rows]
    if sides is None:
        total = total + y_face * roll(v, 1, 1) + roll(y_face * v, -1, 1)
    else:
        low, high = sides
        total = total + y_face * vals[here, low] + fy[here, high] * vals[here, high]
    total = total + z_face * roll(v, shift, 2) + roll(z_face * v, -shift, 2)
    return v, total


def sweep(out, vals, side, faces, weight, first, last, step, level, unroll=16, rows=slice(None), sides=None):
    def body(plane):
        v, total = beside(vals, faces, plane, step, level, rows, sides)
        here = pl.ds(plane, step)
        out[here, rows] = (1.0 - OMEGA) * v + weight[here, rows] * (side[here, rows] + total)

    loop(first, last, step, body, unroll)


def remains(out, vals, side, faces, diag, first, last, step, level, unroll=16, rows=slice(None), sides=None):
    def body(plane):
        v, total = beside(vals, faces, plane, step, level, rows, sides)
        here = pl.ds(plane, step)
        out[here, rows] = side[here, rows] - diag[here, rows] * v + total

    loop(first, last, step, body, unroll)


def block_sum(ref, plane, start, count):
    even, odd = pl.ds(start, count, stride=2), pl.ds(start + 1, count, stride=2)
    low = ref[plane, even, :] + ref[plane, odd, :]
    return low + (ref[plane + 1, even, :] + ref[plane + 1, odd, :])


def coarse_stencil(faces, diag, plane, start, count, level):
    fx, fy, fz = faces
    even, odd = pl.ds(start, count, stride=2), pl.ds(start + 1, count, stride=2)
    x_low = fx[plane, even, :] + fx[plane, odd, :]
    x_mid = fx[plane + 1, even, :] + fx[plane + 1, odd, :]
    y_low = fy[plane, even, :] + fy[plane + 1, even, :]
    y_mid = fy[plane, odd, :] + fy[plane + 1, odd, :]
    z_sum = block_sum(fz, plane, start, count)
    d_sum = block_sum(diag, plane, start, count)
    d_new = pair(d_sum - 2.0 * (x_mid + y_mid), level) - 2.0 * keep(z_sum, level, 1)
    return pair(x_low, level), pair(y_low, level), keep(z_sum, level, 0), d_new


def call(body, outs, scratch, limit, flops, *args, space=pltpu.VMEM):
    nbytes = sum(4 * a.size for a in args) + sum(4 * o.size for o in outs)
    return pl.pallas_call(
        body,
        out_shape=outs,
        in_specs=[pl.BlockSpec(memory_space=space)] * len(args),
        out_specs=[pl.BlockSpec(memory_space=pltpu.VMEM)] * len(outs),
        scratch_shapes=scratch,
        compiler_params=pltpu.CompilerParams(vmem_limit_bytes=limit << 20),
        cost_estimate=pl.CostEstimate(flops=flops, bytes_accessed=nbytes, transcendentals=0),
    )(*args)


def array(*shape):
    return jax.ShapeDtypeStruct(shape, F32)


def shared_tiles(reach):
    for dx in range(1, reach - 3):
        other = 2 * reach - 8 - dx
        yield (dx, other, reach - dx) if dx < other < reach else (dx, 0, 8)


def y_strips_kernel(eps, src, scr, xa, xb, first, second):
    x_up = first_up("gx", 1)
    y_up = first_up("gy", 1)

    def fill(up, down, xl, xr):
        for index, own in enumerate((eps, src, scr)):
            up[16 * index : 16 * index + 16] = own[:, 8:16]
            down[16 * index : 16 * index + 16] = own[:, 0:8]
        at = 48
        rows = lax.broadcasted_iota(jnp.int32, (8, LANES), 0)
        for start, reach in ((0, 10), (10, 9), (19, 9)):
            for part, plane_of in ((xl, lambda dx: reach - dx), (xr, lambda dx: dx - 1)):
                for dx, other, most in shared_tiles(reach):
                    plane = start + plane_of(dx)
                    above, below = part[plane, 8:16], part[plane, 0:8]
                    if other:
                        plane = start + plane_of(other)
                        above = jnp.where(rows >= 8 - most, above, roll(part[plane, 8:16], 8 - most, 0))
                        below = jnp.where(rows < most, below, roll(part[plane, 0:8], most, 0))
                    up[at], down[at] = above, below
                    at += 1
        edges = [(xl, 9)] + [(eps, k) for k in range(16)] + [(xr, 0)]
        edges += [(src, k) for k in range(16)] + [(scr, k) for k in range(16)]
        for k, (part, plane) in enumerate(edges):
            tile, row = 80 + k // 4, 2 * (k % 4)
            up[tile, row : row + 2] = part[plane, 6:8]
            down[tile, row : row + 2] = part[plane, 8:10]

    for x_want, (xl, xr) in ((True, (xb, xa)), (False, (xa, xb))):
        for y_want, (up, down) in ((True, (first, second)), (False, (second, first))):
            pl.when((x_up == x_want) & (y_up == y_want))(
                lambda up=up, down=down, xl=xl, xr=xr: fill(up, down, xl, xr)
            )


def down_kernel(
    eps, src, scr, xa, xb, ya, yb,
    u0_out, fx0_out, fy0_out, fz0_out, w0_out, r0_out,
    fx1, fy1, fz1, w1, l1_own, s2, b2, ship_a, ship_b,
    e, b, s, fx, fy, fz, w, d, ua, ub, b1, d1, va, vb,
):
    x_up = first_up("gx", 1).astype(jnp.int32)
    y_up = first_up("gy", 1)
    row_a = pl.multiple_of(8 + 24 * y_up.astype(jnp.int32), 8)
    row_b = pl.multiple_of(32 - 24 * y_up.astype(jnp.int32), 8)
    at, edge = 48, 0
    blank = jnp.zeros((8, LANES), F32)
    for index, (ref, own, start, reach, margin) in enumerate(((e, eps, 0, 10, 1), (b, src, 10, 9, 0), (s, scr, 19, 9, 0))):
        first = 10 - reach
        ref[10:26, 16:32] = own[...]
        ref[pl.ds(first + (26 - first) * x_up, reach), 16:32] = xa[start : start + reach]
        ref[pl.ds(26 - (26 - first) * x_up, reach), 16:32] = xb[start : start + reach]
        ref[10:26, pl.ds(row_a, 8)] = ya[16 * index : 16 * index + 16]
        ref[10:26, pl.ds(row_b, 8)] = yb[16 * index : 16 * index + 16]
        for plane in (first, 25 + reach):
            ref[plane, 8:16] = blank
            ref[plane, 32:40] = blank
        for plane in range(first, 26 + reach):
            if not 10 - margin <= plane < 26 + margin:
                ref[plane, 0:8] = blank

        def fill(below_ref, above_ref, ref=ref, reach=reach, margin=margin, at=at, edge=edge):
            for plane_of in (lambda dx: 10 - dx, lambda dx: 25 + dx):
                for dx, other, most in shared_tiles(reach):
                    below, above = below_ref[at], above_ref[at]
                    ref[plane_of(dx), 8:16] = below
                    ref[plane_of(dx), 32:40] = above
                    if other:
                        ref[plane_of(other), 8:16] = roll(below, most, 0)
                        ref[plane_of(other), 32:40] = roll(above, -most, 0)
                    at += 1
            for k in range(16 + 2 * margin):
                tile, row = 80 + (edge + k) // 4, 2 * ((edge + k) % 4)
                below, above = below_ref[tile], above_ref[tile]
                rows = row_of(below)
                ref[10 - margin + k, 0:8] = jnp.where(
                    rows < 2, roll(above, -row, 0), jnp.where(rows >= 6, roll(below, 6 - row, 0), 0.0)
                )

        pl.when(y_up)(lambda fill=fill: fill(yb, ya))
        pl.when(jnp.logical_not(y_up))(lambda fill=fill: fill(ya, yb))
        at += 2 * (reach - 4)
        edge += 16 + 2 * margin

    def stencil(plane):
        cells = e[pl.ds(plane - 1, 4), 0:40]
        centre = cells[1:3]
        x_face = 0.5 * (cells[0:3] + cells[1:4])
        y_face = 0.5 * (centre + roll(centre, 1, 1))
        lanes = lane_of(centre)
        z_face = jnp.where(lanes == 0, 0.0, 0.5 * (centre + roll(centre, 1, 2)))
        ends = jnp.where((lanes == 0) | (lanes == LANES - 1), 0.5 * centre, 0.0)
        here = pl.ds(plane, 2)
        screen = s[here, 0:40]
        diag = x_face[0:2] + x_face[1:3] + y_face + roll(y_face, -1, 1)
        diag = diag + z_face + roll(z_face, -1, 2) + screen + ends
        diag = jnp.where(screen > 0.0, diag, 0.0)
        weight = relax_factor(diag)
        value = weight * b[here, 0:40]
        fx[pl.ds(plane, 3), 0:40] = x_face
        fy[here, 0:40] = y_face
        fy[here, 40:48] = y_face[:, 0:8]
        fz[here, 0:40] = z_face
        d[here, 0:40] = diag
        w[here, 0:40] = weight
        ua[here, 0:40] = value
        ua[here, 40:48] = value[:, 0:8]

    loop(1, 34, 2, stencil, 8)
    faces = (fx, fy, fz)
    rows, sides = slice(8, 40), (slice(7, 39), slice(9, 41))
    sweep(ub, ua, b, faces, w, 2, 33, 2, 0, 8, rows, sides)
    sweep(ua, ub, b, faces, w, 3, 32, 2, 0, 8, rows, sides)
    remains(ub, ua, b, faces, d, 4, 31, 2, 0, 8, rows, sides)
    u0_out[...] = ua[10:26, 16:32]

    def keep_window(plane):
        for out, ref in ((fx0_out, fx), (fy0_out, fy), (fz0_out, fz), (w0_out, w), (r0_out, ub)):
            out[plane, 8:24] = ref[plane + 7, 16:32]
            high, low = ref[plane + 7, 32:40], ref[plane + 7, 8:16]
            out[plane, 0:8] = jnp.where(row_of(high) < 4, high, low)

    loop(0, 21, 1, keep_window, 8)

    def to_level1(plane):
        x_face, y_face, z_face, diag = coarse_stencil(faces, d, 2 * plane, 0, 20, 0)
        fx1[plane, 0:20] = x_face
        fy1[plane, 0:20] = y_face
        fz1[plane, 0:20] = z_face
        fy1[plane, 20:21] = y_face[0:1]
        d1[plane, 0:20] = diag
        w1[plane, 0:20] = relax_factor(diag)

    for ref in (fx1, fy1, fz1, w1, d1, b1):
        ref[:, 16:24] = jnp.zeros((18, 8, LANES), F32)
    loop(1, 16, 1, to_level1, 8)
    even, odd = pl.ds(0, 20, stride=2), pl.ds(1, 20, stride=2)
    fx1[17, 0:20] = pair(fx[34, even, :] + fx[34, odd, :], 0)

    def side1(plane):
        side = pair(block_sum(ub, 2 * plane, 0, 20), 0)
        b1[plane, 0:20] = side
        va[plane, 0:20] = w1[plane, 0:20] * side

    loop(2, 15, 1, side1, 8)
    va[:, 20:24] = jnp.zeros((18, 4, LANES), F32)
    faces1 = (fx1, fy1, fz1)
    sweep(vb, va, b1, faces1, w1, 3, 14, 4, 1)
    sweep(va, vb, b1, faces1, w1, 4, 13, 2, 1)
    remains(vb, va, b1, faces1, d1, 5, 12, 4, 1)

    own = jnp.where(bit_of(va[5:13, 8:16], 0), va[5:13, 8:16], vb[5:13, 8:16])
    l1_own[...] = own
    quarter = lax.broadcasted_iota(jnp.int32, (8, LANES), 1) & 3
    for m in range(8):
        parts = coarse_stencil(faces1, d1, 1 + 2 * m, 4, 8, 1)
        stack = parts[3]
        for q in range(3):
            stack = jnp.where(quarter == q, parts[q], stack)
        s2[m] = stack
    packed = jnp.zeros((4, LANES), F32)
    for k in range(4):
        packed = jnp.where(quarter[0:4] == k, pair(block_sum(vb, 5 + 2 * k, 8, 4), 1), packed)
    b2[0, 0:4] = packed
    b2[0, 4:8] = jnp.zeros((4, LANES), F32)
    for ship in (ship_a, ship_b):
        ship[0:8] = s2[...]
        ship[8:9] = b2[...]
    for t in range(4):
        first, second = l1_own[2 * t], l1_own[2 * t + 1]
        low = row_of(first) < 4
        up = jnp.where(low, roll(first, -4, 0), second)
        down = jnp.where(low, first, roll(second, 4, 0))
        ship_a[9 + t] = jnp.where(y_up, up, down)
        ship_b[9 + t] = jnp.where(y_up, down, up)


def window_kernel(s2, b2, l1_own, a1a, a1b, s2_wide, b2_wide, l1_ext, ship_a, ship_b):
    y_up = first_up("gy", 1)
    rows = lax.broadcasted_iota(jnp.int32, (8, LANES), 0)

    def join(below, above):
        for m in range(8):
            s2_wide[2 * m] = jnp.where(rows < 6, below[m], roll(s2[m], 4, 0))
            s2_wide[2 * m + 1] = jnp.where(rows < 2, roll(s2[m], -4, 0), above[m])
        b2_wide[0] = jnp.where(rows < 6, roll(below[8], 2, 0), roll(b2[0], 6, 0))
        b2_wide[1] = jnp.where(rows < 2, roll(b2[0], -2, 0), roll(above[8], 2, 0))
        for k in range(8):
            t, turn = 9 + k // 2, 4 * (k % 2)
            l1_ext[2 * k] = jnp.where(rows < 4, roll(above[t], -turn, 0), roll(below[t], 4 - turn, 0))
            l1_ext[2 * k + 1] = l1_own[k]

    pl.when(y_up)(lambda: join(a1b, a1a))
    pl.when(jnp.logical_not(y_up))(lambda: join(a1a, a1b))
    up = first_up("gx", 1).astype(jnp.int32)
    for ship, way in ((ship_a, up), (ship_b, 1 - up)):
        ship[0:12] = s2_wide[pl.ds(4 - 4 * way, 12)]
        ship[12:14] = b2_wide[...]
        ship[14:22] = l1_ext[pl.ds(8 * way, 8)]


def level2_kernel(
    s2_wide, b2_wide, c1a, c1b,
    fx, fy, fz, w, payload,
    d, b, ua, ub, piece,
):
    up = first_up("gx", 1).astype(jnp.int32)
    b[0:2] = jnp.zeros((2, 16, LANES), F32)
    b[14:16] = jnp.zeros((2, 16, LANES), F32)
    for part, tile, first, count in ((s2_wide, 4, 6, 4), (c1a, 0, 10 * up, 6), (c1b, 0, 10 - 10 * up, 6)):
        for k in range(count):
            tiles = jnp.concatenate([part[tile + 2 * k], part[tile + 2 * k + 1]], axis=0)
            fx[first + k] = spread(tiles, 0, 2)
            fy[first + k] = spread(tiles, 1, 2)
            fz[first + k] = spread(tiles, 2, 2)
            diag = spread(tiles, 3, 2)
            d[first + k] = diag
            w[first + k] = relax_factor(diag)
    for part, tile, first in ((b2_wide, 0, 6), (c1a, 12, 2 + 8 * up), (c1b, 12, 10 - 8 * up)):
        tiles = jnp.concatenate([part[tile], part[tile + 1]], axis=0)
        for k in range(4):
            b[first + k] = spread(tiles, k, 2)

    def begin(plane):
        here = pl.ds(plane, 4)
        ua[here] = w[here] * b[here]

    loop(0, 15, 4, begin)
    faces = (fx, fy, fz)
    sweep(ub, ua, b, faces, w, 3, 12, 2, 2, 8)
    sweep(ua, ub, b, faces, w, 4, 11, 2, 2, 8)
    remains(ub, ua, b, faces, d, 6, 9, 2, 2, 8)

    gx, gy = lax.axis_index("gx"), lax.axis_index("gy")
    rows = lax.broadcasted_iota(jnp.int32, (2, LANES), 0)
    slot = lax.broadcasted_iota(jnp.int32, (2, LANES), 1) & 7
    lines = [jnp.zeros((2, LANES), F32) for _ in range(3)]
    for x in range(2):
        parts = coarse_stencil(faces, d, 6 + 2 * x, 6, 2, 2)
        x_face, y_face, z_face, diag = parts
        if x == 0:
            x_face = jnp.where(gx == 0, 0.0, x_face)
        y_face = jnp.where((gy == 0) & (rows == 0), 0.0, y_face)
        side = pair(block_sum(ub, 6 + 2 * x, 6, 2), 2)
        for index, values in enumerate((x_face, y_face, z_face, diag, side)):
            chosen = slot == (x + 2 * rows if index == 4 else x + 2 * (index % 2) + 4 * rows)
            lines[index // 2] = jnp.where(chosen, values, lines[index // 2])
    for k in range(3):
        piece[k : k + 1] = jnp.sum(lines[k], axis=0, keepdims=True)
    quarter = lax.broadcasted_iota(jnp.int32, (4, LANES), 1) & 3
    for ref, row in ((ub, 3), (ua, 7)):
        stack = ref[9, 6:10]
        for k in range(3):
            stack = jnp.where(quarter == k, ref[6 + k, 6:10], stack)
        piece[row : row + 4] = stack
    piece[11:12] = jnp.zeros((1, LANES), F32)
    whole = piece[0:12]
    for k in range(payload.shape[0] // 12):
        payload[12 * k : 12 * k + 12] = whole


def relay_kernel(got, payload, around, piece):
    count = got.shape[0] // 12
    gy = lax.axis_index("gy")
    around[0:24] = jnp.zeros((24, LANES), F32)
    around[24 : 24 + 12 * count] = got[...]
    around[24 + 12 * count : 48 + 12 * count] = jnp.zeros((24, LANES), F32)
    first, second = got[pl.ds(0, count, stride=12), :], got[pl.ds(1, count, stride=12), :]
    upper = bit_of(first, 2)
    piece[pl.ds(0, count, stride=2), :] = jnp.where(upper, roll(second, 4, 1), first)
    piece[pl.ds(1, count, stride=2), :] = jnp.where(upper, second, roll(first, -4, 1))
    even, odd = got[pl.ds(2, count // 2, stride=24), :], got[pl.ds(14, count // 2, stride=24), :]
    piece[2 * count + 24 :] = jnp.where(bit_of(even, 2), roll(odd, 4, 1), even)
    for target, start, least, most in ((2 * count, 3, -5, 9), (2 * count + 14, 7, -3, 7)):
        for block in range(-2, 3):
            low, high = max(4 * block, least), min(4 * block + 4, most)
            if low < high:
                line = 12 * (gy + block + 2) + start + low - 4 * block
                piece[target + low - least : target + high - least] = around[pl.ds(line, high - low), :]
    whole = piece[...]
    size = piece.shape[0]
    for k in range(payload.shape[0] // size):
        payload[size * k : size * k + size] = whole


def piece_rows(n_y):
    return 5 * n_y // 2 + 24


def x_low(values, rows):
    slot = lane_of(values) & 7
    return jnp.where(slot == 0, roll(roll(values, -7, 1), rows, 0), roll(values, 1, 1))


def x_high(values, rows):
    slot = lane_of(values) & 7
    return jnp.where(slot == 7, roll(roll(values, 7, 1), -rows, 0), roll(values, -1, 1))


def yz_beside(v, y_face, z_face, level):
    total = y_face * roll(v, 1 + level, 0) + roll(y_face * v, -1 - level, 0)
    return total + z_face * roll(v, 8 + 8 * level, 1) + roll(z_face * v, -8 - 8 * level, 1)


def level3_beside(v, faces, rows):
    (x0, x1), y_faces, z_faces = faces
    totals = [x0 * x_low(v[1], rows) + x1 * v[1], x1 * v[0] + x_high(x0 * v[0], rows)]
    return [totals[k] + yz_beside(v[k], y_faces[k], z_faces[k], 0) for k in range(2)]


def row_pair(values):
    odd = (row_of(values) & 1) == 1
    return values + jnp.where(odd, roll(values, 1, 0), roll(values, -1, 0))


def row_keep(values, want):
    odd = (row_of(values) & 1) == 1
    if want:
        return jnp.where(odd, values, roll(values, -1, 0))
    return jnp.where(odd, roll(values, 1, 0), values)


def exchange_slots(tiles):
    for bit in range(3):
        step = 1 << bit
        upper = bit_of(tiles[0], bit)
        made = list(tiles)
        for k in range(8):
            if not k & step:
                made[k] = jnp.where(upper, roll(tiles[k + step], step, 1), tiles[k])
                made[k + step] = jnp.where(upper, tiles[k + step], roll(tiles[k], -step, 1))
        tiles = made
    return tiles


def coarse_levels(got, b3, n_x, n_y):
    size, rows = piece_rows(n_y), 2 * n_y
    groups = []
    for g in range(n_x // 8):
        lines = [(8 * g + q) * size for q in range(8)]
        groups.append(exchange_slots([got[line : line + rows] for line in lines]))
        sides = exchange_slots([got[line + rows + 24 : line + size] for line in lines])
        for k in range(8):
            b3[k % 2, pl.ds(g * rows + k // 2, n_y // 2, stride=4), :] = sides[k]
    fields = []
    for index in range(4):
        fields.append([jnp.concatenate([g[2 * index + x] for g in groups], axis=0) for x in range(2)])
    faces, diag = fields[0:3], fields[3]
    side = [b3[0], b3[1]]
    weight = [relax_factor(d) for d in diag]

    def sweep3(v, side):
        total = level3_beside(v, faces, rows)
        return [(1.0 - OMEGA) * v[k] + weight[k] * (side[k] + total[k]) for k in range(2)]

    u = [weight[k] * side[k] for k in range(2)]
    u = sweep3(u, side)
    u = sweep3(u, side)
    total = level3_beside(u, faces, rows)
    r = [side[k] - diag[k] * u[k] + total[k] for k in range(2)]

    (x0, x1), (y0, y1), (z0, z1) = faces
    y_sum, z_sum = pair(y0 + y1, 3), row_pair(z0 + z1)
    x4, y4, z4 = row_pair(pair(x0, 3)), row_keep(y_sum, 0), keep(z_sum, 3, 0)
    inner = row_keep(y_sum, 1) + keep(z_sum, 3, 1)
    w4 = relax_factor(row_pair(pair(diag[0] + diag[1] - 2.0 * x1, 3)) - 2.0 * inner)
    b4 = row_pair(pair(r[0] + r[1], 3))
    v = w4 * b4
    for _ in range(5):
        total = x4 * x_low(v, rows) + x_high(x4 * v, rows) + yz_beside(v, y4, z4, 1)
        v = (1.0 - OMEGA) * v + w4 * (b4 + total)
    c = [v, v]
    for _ in range(3):
        c = sweep3(c, r)
    return [u[k] + c[k] for k in range(2)]


def up_kernel(
    got, u0, fx0, fy0, fz0, w0, r0,
    fx1, fy1, fz1, w1, l1_ext, c1a, c1b,
    fx2, fy2, fz2, w2,
    out,
    u3, b3, e3, r2, u2, ea2, eb2, r1, u1, ea1, eb1, ea0, eb0,
):
    gx, gy = lax.axis_index("gx"), lax.axis_index("gy")
    n_x, n_y = lax.axis_size("gx"), lax.axis_size("gy")
    size = piece_rows(n_y)
    for block in range(5):
        device = jnp.clip(gx + block - 2, 0, n_x - 1)
        for ref, line in ((r2, 2 * n_y - 1), (u2, 2 * n_y + 11)):
            tiles = got[pl.ds(device * size + line, 16), :]
            for k in range(4):
                if 0 <= 4 * block - 2 + k < 16:
                    ref[4 * block - 2 + k] = spread(tiles, k, 2)

    solved = coarse_levels(got, b3, n_x, n_y)
    for x in range(2):
        u3[x, 8 : 8 + solved[x].shape[0]] = solved[x]
    for block in range(5):
        device = jnp.clip(gx + block - 2, 0, n_x - 1)
        line = 4 + lax.div(device, 8) * 2 * n_y + 2 * gy
        for x in range(2):
            values = pltpu.roll(u3[x, pl.ds(line, 16), :], lax.rem(LANES - lax.rem(device, 8), LANES), 1)
            e3[2 * block + x] = spread(values, 0, 3)

    for plane in range(16):
        values = e3[plane // 2 + 1][1:9]
        for k in range(2):
            ea2[plane, pl.ds(k, 8, stride=2), :] = values

    def inside(values, weight, first, last, step):
        def body(plane):
            here = pl.ds(plane, step)
            values[here] = jnp.where(weight[here] > 0.0, values[here], 0.0)

        loop(first, last, step, body)

    inside(ea2, w2, 0, 15, 4)
    faces = (fx2, fy2, fz2)
    sweep(eb2, ea2, r2, faces, w2, 1, 14, 2, 2)
    sweep(ea2, eb2, r2, faces, w2, 2, 13, 4, 2)
    sweep(eb2, ea2, r2, faces, w2, 3, 12, 2, 2)

    even = first_up("gx", 1).astype(jnp.int32)
    for part, first, tile, count in ((c1a, 1 + 12 * even, 14, 4), (l1_ext, 5, 0, 8), (c1b, 13 - 12 * even, 14, 4)):
        for k in range(count):
            sides, own = part[tile + 2 * k], part[tile + 2 * k + 1]
            for ref, which in ((r1, 0), (u1, 1)):
                edge = keep(sides, 0, which)
                ref[first + k, 0:8] = edge
                ref[first + k, 8:16] = keep(own, 0, which)
                ref[first + k, 16:24] = edge

    for plane in range(3, 13):
        values = (u2[plane] + eb2[plane])[3:13]
        for k in range(2):
            target = 2 * plane - 7 + k
            if 0 <= target < 18:
                ea1[target, pl.ds(2, 10, stride=2), :] = values
                ea1[target, pl.ds(3, 10, stride=2), :] = values
    inside(ea1, w1, 1, 16, 4)
    faces = (fx1, fy1, fz1)
    for plane in (0, 17):
        ea1[plane] = jnp.where(edge_inside(gx, plane), ea1[plane], 0.0)
    sweep(eb1, ea1, r1, faces, w1, 1, 16, 4, 1)
    sweep(ea1, eb1, r1, faces, w1, 2, 15, 2, 1)
    sweep(eb1, ea1, r1, faces, w1, 3, 14, 4, 1)

    for plane in range(3, 15):
        values = u1[plane] + eb1[plane]
        for k in range(2):
            target = 3 + 2 * (plane - 5) + k
            if 0 <= target < 22:
                for parity in range(2):
                    ea0[target, pl.ds(4 + parity, 10, stride=2), :] = values[6:16]
                    ea0[target, pl.ds(parity, 2, stride=2), :] = values[16:18]
    inside(ea0, w0, 0, 21, 2)
    faces = (fx0, fy0, fz0)
    sweep(eb0, ea0, r0, faces, w0, 1, 20, 2, 0)
    sweep(ea0, eb0, r0, faces, w0, 2, 19, 2, 0)

    def last(plane):
        v, total = beside(ea0, faces, plane, 2, 0, slice(None))
        here = pl.ds(plane, 2)
        values = (1.0 - OMEGA) * v + w0[here] * (r0[here] + total)
        out[pl.ds(plane - 3, 2)] = u0[pl.ds(plane - 3, 2)] + values[:, 8:24]

    loop(3, 18, 2, last)


def edge_inside(gx, plane):
    where = 8 * gx + plane - 5
    return (where >= 0) & (where < 8 * lax.axis_size("gx"))


def swapped(values, axis, step, second):
    pairs = []
    for k in range(lax.axis_size(axis) - step):
        if (k // step) % 2 != second:
            pairs += [(k, k + step), (k + step, k)]
    return lax.ppermute(values, axis, pairs)


def first_up(axis, step):
    return lax.rem(lax.div(lax.axis_index(axis), step), 2) == 1


def local(source, dielectric, screening):
    fields = (dielectric, source, screening)
    even = first_up("gx", 1).astype(jnp.int32)

    def strip(way):
        parts = [lax.dynamic_slice_in_dim(f, way * (16 - n), n, 0) for f, n in zip(fields, (10, 9, 9))]
        return jnp.concatenate(parts, axis=0)

    xa, xb = strip(even), strip(1 - even)
    xa, xb = swapped(xa, "gx", 1, 0), swapped(xb, "gx", 1, 1)
    ya, yb = call(y_strips_kernel, [array(93, 8, LANES)] * 2, [], 2, 10_000, *fields, xa, xb)
    ya, yb = swapped(ya, "gy", 1, 0), swapped(yb, "gy", 1, 1)

    big, mid = pltpu.VMEM((36, 48, LANES), F32), pltpu.VMEM((18, 24, LANES), F32)
    outs = [array(16, 16, LANES)] + [array(22, 24, LANES)] * 5 + [array(18, 24, LANES)] * 4
    outs += [array(8, 8, LANES), array(8, 8, LANES), array(1, 8, LANES), array(13, 8, LANES), array(13, 8, LANES)]
    made = call(down_kernel, outs, [big] * 10 + [mid] * 4, 14, 10_000_000, *fields, xa, xb, ya, yb)
    fine, level1, (l1_own, s2, b2, sa, sb) = made[0:6], made[6:10], made[10:15]

    a1a, a1b = swapped(sa, "gy", 1, 0), swapped(sb, "gy", 1, 1)
    outs = [array(16, 8, LANES), array(2, 8, LANES), array(16, 8, LANES), array(22, 8, LANES), array(22, 8, LANES)]
    s2, b2, l1_ext, sa, sb = call(window_kernel, outs, [], 2, 10_000, s2, b2, l1_own, a1a, a1b)
    c1a, c1b = swapped(sa, "gx", 1, 0), swapped(sb, "gx", 1, 1)

    n_x, n_y = lax.axis_size("gx"), lax.axis_size("gy")
    two, size = pltpu.VMEM((16, 16, LANES), F32), piece_rows(n_y)
    outs = [array(16, 16, LANES)] * 4 + [array(12 * n_y, LANES)]
    scratch = [two] * 4 + [pltpu.VMEM((16, LANES), F32)]
    *level2, payload = call(level2_kernel, outs, scratch, 4, 5_000_000, s2, b2, c1a, c1b)

    payload = payload.reshape(6 * n_y, 2, LANES)
    got = lax.all_to_all(payload, "gy", 0, 0, tiled=True).reshape(12 * n_y, LANES)
    scratch = [pltpu.VMEM((12 * n_y + 48, LANES), F32), pltpu.VMEM((size, LANES), F32)]
    (payload,) = call(relay_kernel, [array(n_x * size, LANES)], scratch, 2, 10_000, got)
    got = lax.all_to_all(payload, "gx", 0, 0, tiled=True)

    scratch = [pltpu.VMEM((2, n_x // 4 * n_y + extra, LANES), F32) for extra in (24, 0)]
    scratch += [pltpu.VMEM((12, 16, LANES), F32)]
    scratch += [two] * 4 + [mid] * 4 + [pltpu.VMEM((22, 24, LANES), F32)] * 2
    (result,) = call(
        up_kernel, [array(16, 16, LANES)], scratch, 6, 10_000_000,
        got, *fine, *level1, l1_ext, c1a, c1b, *level2,
    )
    return result


def solution(mesh):
    spec = P("gx", "gy", None)
    return jax.shard_map(local, mesh=mesh, in_specs=(spec,) * 3, out_specs=spec, check_vma=False)
```

```python
import jax
import jax.numpy as jnp
from jax import lax
from jax.experimental import pallas as pl
from jax.experimental.pallas import tpu as pltpu
from jax.sharding import PartitionSpec as P

OMEGA = 0.8
F32 = jnp.float32
LANES = 128


def roll(values, shift, dim):
    return pltpu.roll(values, shift % values.shape[dim], dim)


def lane_of(values):
    return lax.broadcasted_iota(jnp.int32, values.shape, values.ndim - 1)


def row_of(values):
    return lax.broadcasted_iota(jnp.int32, values.shape, values.ndim - 2)


def bit_of(values, bit):
    return ((lane_of(values) >> bit) & 1) == 1


def pair(values, bit):
    step, dim = 1 << bit, values.ndim - 1
    other = jnp.where(bit_of(values, bit), roll(values, step, dim), roll(values, -step, dim))
    return values + other


def keep(values, bit, want):
    step, dim = 1 << bit, values.ndim - 1
    if want:
        return jnp.where(bit_of(values, bit), values, roll(values, -step, dim))
    return jnp.where(bit_of(values, bit), roll(values, step, dim), values)


def spread(values, which, bits):
    for bit in range(bits):
        values = keep(values, bit, (which >> bit) & 1)
    return values


def relax_factor(diag):
    good = diag > 0.0
    return jnp.where(good, OMEGA / jnp.where(good, diag, 1.0), 0.0)


def loop(first, last, step, body, unroll=16):
    count = (last - first + 1) // step
    assert count * step == last - first + 1
    trips = count // unroll

    def run(index, carry):
        for k in range(unroll):
            body(first + (index * unroll + k) * step)
        return carry

    if trips > 1:
        lax.fori_loop(0, trips, run, 0)
    else:
        trips = 0
    for k in range(trips * unroll, count):
        body(first + k * step)


def beside(vals, faces, plane, count, level, rows, sides=None):
    fx, fy, fz = faces
    shift = 1 << level
    here = pl.ds(plane, count)
    v = vals[here, rows]
    y_face, z_face = fy[here, rows], fz[here, rows]
    total = fx[here, rows] * vals[pl.ds(plane - 1, count), rows]
    total = total + fx[pl.ds(plane + 1, count), rows] * vals[pl.ds(plane + 1, count), rows]
    if sides is None:
        total = total + y_face * roll(v, 1, 1) + roll(y_face * v, -1, 1)
    else:
        low, high = sides
        total = total + y_face * vals[here, low] + fy[here, high] * vals[here, high]
    total = total + z_face * roll(v, shift, 2) + roll(z_face * v, -shift, 2)
    return v, total


def sweep(out, vals, side, faces, weight, first, last, step, level, unroll=16, rows=slice(None), sides=None):
    def body(plane):
        v, total = beside(vals, faces, plane, step, level, rows, sides)
        here = pl.ds(plane, step)
        out[here, rows] = (1.0 - OMEGA) * v + weight[here, rows] * (side[here, rows] + total)

    loop(first, last, step, body, unroll)


def remains(out, vals, side, faces, diag, first, last, step, level, unroll=16, rows=slice(None), sides=None):
    def body(plane):
        v, total = beside(vals, faces, plane, step, level, rows, sides)
        here = pl.ds(plane, step)
        out[here, rows] = side[here, rows] - diag[here, rows] * v + total

    loop(first, last, step, body, unroll)


def block_sum(ref, plane, start, count):
    even, odd = pl.ds(start, count, stride=2), pl.ds(start + 1, count, stride=2)
    low = ref[plane, even, :] + ref[plane, odd, :]
    return low + (ref[plane + 1, even, :] + ref[plane + 1, odd, :])


def coarse_stencil(faces, diag, plane, start, count, level):
    fx, fy, fz = faces
    even, odd = pl.ds(start, count, stride=2), pl.ds(start + 1, count, stride=2)
    x_low = fx[plane, even, :] + fx[plane, odd, :]
    x_mid = fx[plane + 1, even, :] + fx[plane + 1, odd, :]
    y_low = fy[plane, even, :] + fy[plane + 1, even, :]
    y_mid = fy[plane, odd, :] + fy[plane + 1, odd, :]
    z_sum = block_sum(fz, plane, start, count)
    d_sum = block_sum(diag, plane, start, count)
    d_new = pair(d_sum - 2.0 * (x_mid + y_mid), level) - 2.0 * keep(z_sum, level, 1)
    return pair(x_low, level), pair(y_low, level), keep(z_sum, level, 0), d_new


def call(body, outs, scratch, limit, flops, *args, space=pltpu.VMEM):
    nbytes = sum(4 * a.size for a in args) + sum(4 * o.size for o in outs)
    return pl.pallas_call(
        body,
        out_shape=outs,
        in_specs=[pl.BlockSpec(memory_space=space)] * len(args),
        out_specs=[pl.BlockSpec(memory_space=pltpu.VMEM)] * len(outs),
        scratch_shapes=scratch,
        compiler_params=pltpu.CompilerParams(vmem_limit_bytes=limit << 20),
        cost_estimate=pl.CostEstimate(flops=flops, bytes_accessed=nbytes, transcendentals=0),
    )(*args)


def array(*shape):
    return jax.ShapeDtypeStruct(shape, F32)


def shared_tiles(reach):
    for dx in range(1, reach - 3):
        other = 2 * reach - 8 - dx
        yield (dx, other, reach - dx) if dx < other < reach else (dx, 0, 8)


def either_way(up, first, second, fill):
    pl.when(up)(lambda: fill(first, second))
    pl.when(jnp.logical_not(up))(lambda: fill(second, first))


def y_own_kernel(eps, src, scr, first, second):
    def fill(up, down):
        for index, own in enumerate((eps, src, scr)):
            up[16 * index : 16 * index + 16] = own[:, 8:16]
            down[16 * index : 16 * index + 16] = own[:, 0:8]
            for plane in range(16):
                tile, row = 48 + 4 * index + plane // 4, 2 * (plane % 4)
                up[tile, row : row + 2] = own[plane, 6:8]
                down[tile, row : row + 2] = own[plane, 8:10]

    either_way(first_up("gy", 1), first, second, fill)


def y_corner_kernel(xa, xb, first, second):
    rows = lax.broadcasted_iota(jnp.int32, (8, LANES), 0)

    def fill(up, down, xl, xr):
        at = 0
        for start, reach in ((0, 10), (10, 9), (19, 9)):
            for part, plane_of in ((xl, lambda dx: reach - dx), (xr, lambda dx: dx - 1)):
                for dx, other, most in shared_tiles(reach):
                    plane = start + plane_of(dx)
                    above, below = part[plane, 8:16], part[plane, 0:8]
                    if other:
                        plane = start + plane_of(other)
                        above = jnp.where(rows >= 8 - most, above, roll(part[plane, 8:16], 8 - most, 0))
                        below = jnp.where(rows < most, below, roll(part[plane, 0:8], most, 0))
                    up[at], down[at] = above, below
                    at += 1
        for ref, row in ((up, 6), (down, 8)):
            ref[at] = jnp.zeros((8, LANES), F32)
            ref[at, 0:2] = xl[9, row : row + 2]
            ref[at, 2:4] = xr[0, row : row + 2]

    either_way(
        first_up("gx", 1),
        xb,
        xa,
        lambda xl, xr: either_way(first_up("gy", 1), first, second, lambda up, down: fill(up, down, xl, xr)),
    )


def down_kernel(
    eps, src, scr, xa, xb, ya, yb, za, zb,
    u0_out, fx0_out, fy0_out, fz0_out, w0_out, r0_out,
    fx1, fy1, fz1, w1, l1_own, s2, b2, ship_a, ship_b,
    e, b, s, fx, fy, fz, w, d, ua, ub, b1, d1, va, vb,
):
    x_up = first_up("gx", 1).astype(jnp.int32)
    y_up = first_up("gy", 1)
    row_a = pl.multiple_of(8 + 24 * y_up.astype(jnp.int32), 8)
    row_b = pl.multiple_of(32 - 24 * y_up.astype(jnp.int32), 8)
    at = 0
    blank = jnp.zeros((8, LANES), F32)
    for index, (ref, own, start, reach, margin) in enumerate(((e, eps, 0, 10, 1), (b, src, 10, 9, 0), (s, scr, 19, 9, 0))):
        first = 10 - reach
        ref[10:26, 16:32] = own[...]
        ref[pl.ds(first + (26 - first) * x_up, reach), 16:32] = xa[start : start + reach]
        ref[pl.ds(26 - (26 - first) * x_up, reach), 16:32] = xb[start : start + reach]
        ref[10:26, pl.ds(row_a, 8)] = ya[16 * index : 16 * index + 16]
        ref[10:26, pl.ds(row_b, 8)] = yb[16 * index : 16 * index + 16]
        for plane in (first, 25 + reach):
            ref[plane, 8:16] = blank
            ref[plane, 32:40] = blank
        for plane in range(first, 26 + reach):
            if not 10 - margin <= plane < 26 + margin:
                ref[plane, 0:8] = blank

        def fill(below_ref, above_ref, below_side, above_side, ref=ref, index=index, reach=reach, margin=margin, at=at):
            for plane_of in (lambda dx: 10 - dx, lambda dx: 25 + dx):
                for dx, other, most in shared_tiles(reach):
                    below, above = below_side[at], above_side[at]
                    ref[plane_of(dx), 8:16] = below
                    ref[plane_of(dx), 32:40] = above
                    if other:
                        ref[plane_of(other), 8:16] = roll(below, most, 0)
                        ref[plane_of(other), 32:40] = roll(above, -most, 0)
                    at += 1
            edges = [(below_ref, above_ref, 48 + 4 * index + k // 4, 2 * (k % 4), 10 + k) for k in range(16)]
            if margin:
                edges += [(below_side, above_side, 32, 0, 9), (below_side, above_side, 32, 2, 26)]
            for low_ref, high_ref, tile, row, plane in edges:
                below, above = low_ref[tile], high_ref[tile]
                rows = row_of(below)
                ref[plane, 0:8] = jnp.where(
                    rows < 2, roll(above, -row, 0), jnp.where(rows >= 6, roll(below, 6 - row, 0), 0.0)
                )

        pl.when(y_up)(lambda fill=fill: fill(yb, ya, zb, za))
        pl.when(jnp.logical_not(y_up))(lambda fill=fill: fill(ya, yb, za, zb))
        at += 2 * (reach - 4)

    def stencil(plane):
        cells = e[pl.ds(plane - 1, 4), 0:40]
        centre = cells[1:3]
        x_face = 0.5 * (cells[0:3] + cells[1:4])
        y_face = 0.5 * (centre + roll(centre, 1, 1))
        lanes = lane_of(centre)
        z_face = jnp.where(lanes == 0, 0.0, 0.5 * (centre + roll(centre, 1, 2)))
        ends = jnp.where((lanes == 0) | (lanes == LANES - 1), 0.5 * centre, 0.0)
        here = pl.ds(plane, 2)
        screen = s[here, 0:40]
        diag = x_face[0:2] + x_face[1:3] + y_face + roll(y_face, -1, 1)
        diag = diag + z_face + roll(z_face, -1, 2) + screen + ends
        diag = jnp.where(screen > 0.0, diag, 0.0)
        weight = relax_factor(diag)
        value = weight * b[here, 0:40]
        fx[pl.ds(plane, 3), 0:40] = x_face
        fy[here, 0:40] = y_face
        fy[here, 40:48] = y_face[:, 0:8]
        fz[here, 0:40] = z_face
        d[here, 0:40] = diag
        w[here, 0:40] = weight
        ua[here, 0:40] = value
        ua[here, 40:48] = value[:, 0:8]

    loop(1, 34, 2, stencil, 8)
    faces = (fx, fy, fz)
    rows, sides = slice(8, 40), (slice(7, 39), slice(9, 41))
    sweep(ub, ua, b, faces, w, 2, 33, 2, 0, 8, rows, sides)
    sweep(ua, ub, b, faces, w, 3, 32, 2, 0, 8, rows, sides)
    remains(ub, ua, b, faces, d, 4, 31, 2, 0, 8, rows, sides)
    u0_out[...] = ua[10:26, 16:32]

    def keep_window(plane):
        for out, ref in ((fx0_out, fx), (fy0_out, fy), (fz0_out, fz), (w0_out, w), (r0_out, ub)):
            out[plane, 8:24] = ref[plane + 7, 16:32]
            high, low = ref[plane + 7, 32:40], ref[plane + 7, 8:16]
            out[plane, 0:8] = jnp.where(row_of(high) < 4, high, low)

    loop(0, 21, 1, keep_window, 8)

    def to_level1(plane):
        x_face, y_face, z_face, diag = coarse_stencil(faces, d, 2 * plane, 0, 20, 0)
        fx1[plane, 0:20] = x_face
        fy1[plane, 0:20] = y_face
        fz1[plane, 0:20] = z_face
        fy1[plane, 20:21] = y_face[0:1]
        d1[plane, 0:20] = diag
        w1[plane, 0:20] = relax_factor(diag)

    for ref in (fx1, fy1, fz1, w1, d1, b1):
        ref[:, 16:24] = jnp.zeros((18, 8, LANES), F32)
    loop(1, 16, 1, to_level1, 8)
    even, odd = pl.ds(0, 20, stride=2), pl.ds(1, 20, stride=2)
    fx1[17, 0:20] = pair(fx[34, even, :] + fx[34, odd, :], 0)

    def side1(plane):
        side = pair(block_sum(ub, 2 * plane, 0, 20), 0)
        b1[plane, 0:20] = side
        va[plane, 0:20] = w1[plane, 0:20] * side

    loop(2, 15, 1, side1, 8)
    va[:, 20:24] = jnp.zeros((18, 4, LANES), F32)
    faces1 = (fx1, fy1, fz1)
    sweep(vb, va, b1, faces1, w1, 3, 14, 4, 1)
    sweep(va, vb, b1, faces1, w1, 4, 13, 2, 1)
    remains(vb, va, b1, faces1, d1, 5, 12, 4, 1)

    own = jnp.where(bit_of(va[5:13, 8:16], 0), va[5:13, 8:16], vb[5:13, 8:16])
    l1_own[...] = own
    quarter = lax.broadcasted_iota(jnp.int32, (8, LANES), 1) & 3
    for m in range(8):
        parts = coarse_stencil(faces1, d1, 1 + 2 * m, 4, 8, 1)
        stack = parts[3]
        for q in range(3):
            stack = jnp.where(quarter == q, parts[q], stack)
        s2[m] = stack
    packed = jnp.zeros((4, LANES), F32)
    for k in range(4):
        packed = jnp.where(quarter[0:4] == k, pair(block_sum(vb, 5 + 2 * k, 8, 4), 1), packed)
    b2[0, 0:4] = packed
    b2[0, 4:8] = jnp.zeros((4, LANES), F32)
    for ship in (ship_a, ship_b):
        ship[0:8] = s2[...]
        ship[8:9] = b2[...]
    for t in range(4):
        first, second = l1_own[2 * t], l1_own[2 * t + 1]
        low = row_of(first) < 4
        up = jnp.where(low, roll(first, -4, 0), second)
        down = jnp.where(low, first, roll(second, 4, 0))
        ship_a[9 + t] = jnp.where(y_up, up, down)
        ship_b[9 + t] = jnp.where(y_up, down, up)


def window_kernel(s2, b2, l1_own, a1a, a1b, s2_wide, b2_wide, l1_ext, ship_a, ship_b):
    y_up = first_up("gy", 1)
    rows = lax.broadcasted_iota(jnp.int32, (8, LANES), 0)

    def join(below, above):
        for m in range(8):
            s2_wide[2 * m] = jnp.where(rows < 6, below[m], roll(s2[m], 4, 0))
            s2_wide[2 * m + 1] = jnp.where(rows < 2, roll(s2[m], -4, 0), above[m])
        b2_wide[0] = jnp.where(rows < 6, roll(below[8], 2, 0), roll(b2[0], 6, 0))
        b2_wide[1] = jnp.where(rows < 2, roll(b2[0], -2, 0), roll(above[8], 2, 0))
        for k in range(8):
            t, turn = 9 + k // 2, 4 * (k % 2)
            l1_ext[2 * k] = jnp.where(rows < 4, roll(above[t], -turn, 0), roll(below[t], 4 - turn, 0))
            l1_ext[2 * k + 1] = l1_own[k]

    pl.when(y_up)(lambda: join(a1b, a1a))
    pl.when(jnp.logical_not(y_up))(lambda: join(a1a, a1b))
    up = first_up("gx", 1).astype(jnp.int32)
    for ship, way in ((ship_a, up), (ship_b, 1 - up)):
        ship[0:12] = s2_wide[pl.ds(4 - 4 * way, 12)]
        ship[12:14] = b2_wide[...]
        ship[14:22] = l1_ext[pl.ds(8 * way, 8)]


def level2_kernel(
    s2_wide, b2_wide, c1a, c1b,
    fx, fy, fz, w, payload,
    d, b, ua, ub, piece,
):
    up = first_up("gx", 1).astype(jnp.int32)
    b[0:2] = jnp.zeros((2, 16, LANES), F32)
    b[14:16] = jnp.zeros((2, 16, LANES), F32)
    for part, tile, first, count in ((s2_wide, 4, 6, 4), (c1a, 0, 10 * up, 6), (c1b, 0, 10 - 10 * up, 6)):
        for k in range(count):
            tiles = jnp.concatenate([part[tile + 2 * k], part[tile + 2 * k + 1]], axis=0)
            fx[first + k] = spread(tiles, 0, 2)
            fy[first + k] = spread(tiles, 1, 2)
            fz[first + k] = spread(tiles, 2, 2)
            diag = spread(tiles, 3, 2)
            d[first + k] = diag
            w[first + k] = relax_factor(diag)
    for part, tile, first in ((b2_wide, 0, 6), (c1a, 12, 2 + 8 * up), (c1b, 12, 10 - 8 * up)):
        tiles = jnp.concatenate([part[tile], part[tile + 1]], axis=0)
        for k in range(4):
            b[first + k] = spread(tiles, k, 2)

    def begin(plane):
        here = pl.ds(plane, 4)
        ua[here] = w[here] * b[here]

    loop(0, 15, 4, begin)
    faces = (fx, fy, fz)
    sweep(ub, ua, b, faces, w, 3, 12, 2, 2, 8)
    sweep(ua, ub, b, faces, w, 4, 11, 2, 2, 8)
    remains(ub, ua, b, faces, d, 6, 9, 2, 2, 8)

    gx, gy = lax.axis_index("gx"), lax.axis_index("gy")
    rows = lax.broadcasted_iota(jnp.int32, (2, LANES), 0)
    slot = lax.broadcasted_iota(jnp.int32, (2, LANES), 1) & 7
    lines = [jnp.zeros((2, LANES), F32) for _ in range(3)]
    for x in range(2):
        parts = coarse_stencil(faces, d, 6 + 2 * x, 6, 2, 2)
        x_face, y_face, z_face, diag = parts
        if x == 0:
            x_face = jnp.where(gx == 0, 0.0, x_face)
        y_face = jnp.where((gy == 0) & (rows == 0), 0.0, y_face)
        side = pair(block_sum(ub, 6 + 2 * x, 6, 2), 2)
        for index, values in enumerate((x_face, y_face, z_face, diag, side)):
            chosen = slot == (x + 2 * rows if index == 4 else x + 2 * (index % 2) + 4 * rows)
            lines[index // 2] = jnp.where(chosen, values, lines[index // 2])
    for k in range(3):
        piece[k : k + 1] = jnp.sum(lines[k], axis=0, keepdims=True)
    quarter = lax.broadcasted_iota(jnp.int32, (4, LANES), 1) & 3
    for ref, row in ((ub, 3), (ua, 7)):
        stack = ref[9, 6:10]
        for k in range(3):
            stack = jnp.where(quarter == k, ref[6 + k, 6:10], stack)
        piece[row : row + 4] = stack
    piece[11:12] = jnp.zeros((1, LANES), F32)
    whole = piece[0:12]
    for k in range(payload.shape[0] // 12):
        payload[12 * k : 12 * k + 12] = whole


def relay_kernel(got, payload, around, piece):
    count = got.shape[0] // 12
    gy = lax.axis_index("gy")
    around[0:24] = jnp.zeros((24, LANES), F32)
    around[24 : 24 + 12 * count] = got[...]
    around[24 + 12 * count : 48 + 12 * count] = jnp.zeros((24, LANES), F32)
    first, second = got[pl.ds(0, count, stride=12), :], got[pl.ds(1, count, stride=12), :]
    upper = bit_of(first, 2)
    piece[pl.ds(0, count, stride=2), :] = jnp.where(upper, roll(second, 4, 1), first)
    piece[pl.ds(1, count, stride=2), :] = jnp.where(upper, second, roll(first, -4, 1))
    even, odd = got[pl.ds(2, count // 2, stride=24), :], got[pl.ds(14, count // 2, stride=24), :]
    piece[2 * count + 24 :] = jnp.where(bit_of(even, 2), roll(odd, 4, 1), even)
    for target, start, least, most in ((2 * count, 3, -5, 9), (2 * count + 14, 7, -3, 7)):
        for block in range(-2, 3):
            low, high = max(4 * block, least), min(4 * block + 4, most)
            if low < high:
                line = 12 * (gy + block + 2) + start + low - 4 * block
                piece[target + low - least : target + high - least] = around[pl.ds(line, high - low), :]
    whole = piece[...]
    size = piece.shape[0]
    for k in range(payload.shape[0] // size):
        payload[size * k : size * k + size] = whole


def piece_rows(n_y):
    return 5 * n_y // 2 + 24


def x_low(values, rows):
    slot = lane_of(values) & 7
    return jnp.where(slot == 0, roll(roll(values, -7, 1), rows, 0), roll(values, 1, 1))


def x_high(values, rows):
    slot = lane_of(values) & 7
    return jnp.where(slot == 7, roll(roll(values, 7, 1), -rows, 0), roll(values, -1, 1))


def yz_beside(v, y_face, z_face, level):
    total = y_face * roll(v, 1 + level, 0) + roll(y_face * v, -1 - level, 0)
    return total + z_face * roll(v, 8 + 8 * level, 1) + roll(z_face * v, -8 - 8 * level, 1)


def level3_beside(v, faces, rows):
    (x0, x1), y_faces, z_faces = faces
    totals = [x0 * x_low(v[1], rows) + x1 * v[1], x1 * v[0] + x_high(x0 * v[0], rows)]
    return [totals[k] + yz_beside(v[k], y_faces[k], z_faces[k], 0) for k in range(2)]


def row_pair(values):
    odd = (row_of(values) & 1) == 1
    return values + jnp.where(odd, roll(values, 1, 0), roll(values, -1, 0))


def row_keep(values, want):
    odd = (row_of(values) & 1) == 1
    if want:
        return jnp.where(odd, values, roll(values, -1, 0))
    return jnp.where(odd, roll(values, 1, 0), values)


def exchange_slots(tiles):
    for bit in range(3):
        step = 1 << bit
        upper = bit_of(tiles[0], bit)
        made = list(tiles)
        for k in range(8):
            if not k & step:
                made[k] = jnp.where(upper, roll(tiles[k + step], step, 1), tiles[k])
                made[k + step] = jnp.where(upper, tiles[k + step], roll(tiles[k], -step, 1))
        tiles = made
    return tiles


def coarse_levels(got, b3, n_x, n_y):
    size, rows = piece_rows(n_y), 2 * n_y
    groups = []
    for g in range(n_x // 8):
        lines = [(8 * g + q) * size for q in range(8)]
        groups.append(exchange_slots([got[line : line + rows] for line in lines]))
        sides = exchange_slots([got[line + rows + 24 : line + size] for line in lines])
        for k in range(8):
            b3[k % 2, pl.ds(g * rows + k // 2, n_y // 2, stride=4), :] = sides[k]
    fields = []
    for index in range(4):
        fields.append([jnp.concatenate([g[2 * index + x] for g in groups], axis=0) for x in range(2)])
    faces, diag = fields[0:3], fields[3]
    side = [b3[0], b3[1]]
    weight = [relax_factor(d) for d in diag]

    def sweep3(v, side):
        total = level3_beside(v, faces, rows)
        return [(1.0 - OMEGA) * v[k] + weight[k] * (side[k] + total[k]) for k in range(2)]

    u = [weight[k] * side[k] for k in range(2)]
    u = sweep3(u, side)
    u = sweep3(u, side)
    total = level3_beside(u, faces, rows)
    r = [side[k] - diag[k] * u[k] + total[k] for k in range(2)]

    (x0, x1), (y0, y1), (z0, z1) = faces
    y_sum, z_sum = pair(y0 + y1, 3), row_pair(z0 + z1)
    x4, y4, z4 = row_pair(pair(x0, 3)), row_keep(y_sum, 0), keep(z_sum, 3, 0)
    inner = row_keep(y_sum, 1) + keep(z_sum, 3, 1)
    w4 = relax_factor(row_pair(pair(diag[0] + diag[1] - 2.0 * x1, 3)) - 2.0 * inner)
    b4 = row_pair(pair(r[0] + r[1], 3))
    v = w4 * b4
    for _ in range(5):
        total = x4 * x_low(v, rows) + x_high(x4 * v, rows) + yz_beside(v, y4, z4, 1)
        v = (1.0 - OMEGA) * v + w4 * (b4 + total)
    c = [v, v]
    for _ in range(3):
        c = sweep3(c, r)
    return [u[k] + c[k] for k in range(2)]


def up_kernel(
    got, u0, fx0, fy0, fz0, w0, r0,
    fx1, fy1, fz1, w1, l1_ext, c1a, c1b,
    fx2, fy2, fz2, w2,
    out,
    u3, b3, e3, r2, u2, ea2, eb2, r1, u1, ea1, eb1, ea0, eb0,
):
    gx, gy = lax.axis_index("gx"), lax.axis_index("gy")
    n_x, n_y = lax.axis_size("gx"), lax.axis_size("gy")
    size = piece_rows(n_y)
    for block in range(5):
        device = jnp.clip(gx + block - 2, 0, n_x - 1)
        for ref, line in ((r2, 2 * n_y - 1), (u2, 2 * n_y + 11)):
            tiles = got[pl.ds(device * size + line, 16), :]
            for k in range(4):
                if 0 <= 4 * block - 2 + k < 16:
                    ref[4 * block - 2 + k] = spread(tiles, k, 2)

    solved = coarse_levels(got, b3, n_x, n_y)
    for x in range(2):
        u3[x, 8 : 8 + solved[x].shape[0]] = solved[x]
    for block in range(5):
        device = jnp.clip(gx + block - 2, 0, n_x - 1)
        line = 4 + lax.div(device, 8) * 2 * n_y + 2 * gy
        for x in range(2):
            values = pltpu.roll(u3[x, pl.ds(line, 16), :], lax.rem(LANES - lax.rem(device, 8), LANES), 1)
            e3[2 * block + x] = spread(values, 0, 3)

    for plane in range(16):
        values = e3[plane // 2 + 1][1:9]
        for k in range(2):
            ea2[plane, pl.ds(k, 8, stride=2), :] = values

    def inside(values, weight, first, last, step):
        def body(plane):
            here = pl.ds(plane, step)
            values[here] = jnp.where(weight[here] > 0.0, values[here], 0.0)

        loop(first, last, step, body)

    inside(ea2, w2, 0, 15, 4)
    faces = (fx2, fy2, fz2)
    sweep(eb2, ea2, r2, faces, w2, 1, 14, 2, 2)
    sweep(ea2, eb2, r2, faces, w2, 2, 13, 4, 2)
    sweep(eb2, ea2, r2, faces, w2, 3, 12, 2, 2)

    even = first_up("gx", 1).astype(jnp.int32)
    for part, first, tile, count in ((c1a, 1 + 12 * even, 14, 4), (l1_ext, 5, 0, 8), (c1b, 13 - 12 * even, 14, 4)):
        for k in range(count):
            sides, own = part[tile + 2 * k], part[tile + 2 * k + 1]
            for ref, which in ((r1, 0), (u1, 1)):
                edge = keep(sides, 0, which)
                ref[first + k, 0:8] = edge
                ref[first + k, 8:16] = keep(own, 0, which)
                ref[first + k, 16:24] = edge

    for plane in range(3, 13):
        values = (u2[plane] + eb2[plane])[3:13]
        for k in range(2):
            target = 2 * plane - 7 + k
            if 0 <= target < 18:
                ea1[target, pl.ds(2, 10, stride=2), :] = values
                ea1[target, pl.ds(3, 10, stride=2), :] = values
    inside(ea1, w1, 1, 16, 4)
    faces = (fx1, fy1, fz1)
    for plane in (0, 17):
        ea1[plane] = jnp.where(edge_inside(gx, plane), ea1[plane], 0.0)
    sweep(eb1, ea1, r1, faces, w1, 1, 16, 4, 1)
    sweep(ea1, eb1, r1, faces, w1, 2, 15, 2, 1)
    sweep(eb1, ea1, r1, faces, w1, 3, 14, 4, 1)

    for plane in range(3, 15):
        values = u1[plane] + eb1[plane]
        for k in range(2):
            target = 3 + 2 * (plane - 5) + k
            if 0 <= target < 22:
                for parity in range(2):
                    ea0[target, pl.ds(4 + parity, 10, stride=2), :] = values[6:16]
                    ea0[target, pl.ds(parity, 2, stride=2), :] = values[16:18]
    inside(ea0, w0, 0, 21, 2)
    faces = (fx0, fy0, fz0)
    sweep(eb0, ea0, r0, faces, w0, 1, 20, 2, 0)
    sweep(ea0, eb0, r0, faces, w0, 2, 19, 2, 0)

    def last(plane):
        v, total = beside(ea0, faces, plane, 2, 0, slice(None))
        here = pl.ds(plane, 2)
        values = (1.0 - OMEGA) * v + w0[here] * (r0[here] + total)
        out[pl.ds(plane - 3, 2)] = u0[pl.ds(plane - 3, 2)] + values[:, 8:24]

    loop(3, 18, 2, last)


def edge_inside(gx, plane):
    where = 8 * gx + plane - 5
    return (where >= 0) & (where < 8 * lax.axis_size("gx"))


def swapped(values, axis, step, second):
    pairs = []
    for k in range(lax.axis_size(axis) - step):
        if (k // step) % 2 != second:
            pairs += [(k, k + step), (k + step, k)]
    return lax.ppermute(values, axis, pairs)


def first_up(axis, step):
    return lax.rem(lax.div(lax.axis_index(axis), step), 2) == 1


def local(source, dielectric, screening):
    fields = (dielectric, source, screening)
    even = first_up("gx", 1).astype(jnp.int32)

    def strip(way):
        parts = [lax.dynamic_slice_in_dim(f, way * (16 - n), n, 0) for f, n in zip(fields, (10, 9, 9))]
        return jnp.concatenate(parts, axis=0)

    xa, xb = strip(even), strip(1 - even)
    xa, xb = swapped(xa, "gx", 1, 0), swapped(xb, "gx", 1, 1)
    ya, yb = call(y_own_kernel, [array(60, 8, LANES)] * 2, [], 2, 10_000, *fields)
    ya, yb = swapped(ya, "gy", 1, 0), swapped(yb, "gy", 1, 1)
    za, zb = call(y_corner_kernel, [array(33, 8, LANES)] * 2, [], 2, 10_000, xa, xb)
    za, zb = swapped(za, "gy", 1, 0), swapped(zb, "gy", 1, 1)

    big, mid = pltpu.VMEM((36, 48, LANES), F32), pltpu.VMEM((18, 24, LANES), F32)
    outs = [array(16, 16, LANES)] + [array(22, 24, LANES)] * 5 + [array(18, 24, LANES)] * 4
    outs += [array(8, 8, LANES), array(8, 8, LANES), array(1, 8, LANES), array(13, 8, LANES), array(13, 8, LANES)]
    made = call(down_kernel, outs, [big] * 10 + [mid] * 4, 14, 10_000_000, *fields, xa, xb, ya, yb, za, zb)
    fine, level1, (l1_own, s2, b2, sa, sb) = made[0:6], made[6:10], made[10:15]

    a1a, a1b = swapped(sa, "gy", 1, 0), swapped(sb, "gy", 1, 1)
    outs = [array(16, 8, LANES), array(2, 8, LANES), array(16, 8, LANES), array(22, 8, LANES), array(22, 8, LANES)]
    s2, b2, l1_ext, sa, sb = call(window_kernel, outs, [], 2, 10_000, s2, b2, l1_own, a1a, a1b)
    c1a, c1b = swapped(sa, "gx", 1, 0), swapped(sb, "gx", 1, 1)

    n_x, n_y = lax.axis_size("gx"), lax.axis_size("gy")
    two, size = pltpu.VMEM((16, 16, LANES), F32), piece_rows(n_y)
    outs = [array(16, 16, LANES)] * 4 + [array(12 * n_y, LANES)]
    scratch = [two] * 4 + [pltpu.VMEM((16, LANES), F32)]
    *level2, payload = call(level2_kernel, outs, scratch, 4, 5_000_000, s2, b2, c1a, c1b)

    payload = payload.reshape(6 * n_y, 2, LANES)
    got = lax.all_to_all(payload, "gy", 0, 0, tiled=True).reshape(12 * n_y, LANES)
    scratch = [pltpu.VMEM((12 * n_y + 48, LANES), F32), pltpu.VMEM((size, LANES), F32)]
    (payload,) = call(relay_kernel, [array(n_x * size, LANES)], scratch, 2, 10_000, got)
    got = lax.all_to_all(payload, "gx", 0, 0, tiled=True)

    scratch = [pltpu.VMEM((2, n_x // 4 * n_y + extra, LANES), F32) for extra in (24, 0)]
    scratch += [pltpu.VMEM((12, 16, LANES), F32)]
    scratch += [two] * 4 + [mid] * 4 + [pltpu.VMEM((22, 24, LANES), F32)] * 2
    (result,) = call(
        up_kernel, [array(16, 16, LANES)], scratch, 6, 10_000_000,
        got, *fine, *level1, l1_ext, c1a, c1b, *level2,
    )
    return result


def solution(mesh):
    spec = P("gx", "gy", None)
    return jax.shard_map(local, mesh=mesh, in_specs=(spec,) * 3, out_specs=spec, check_vma=False)
```

```python
import jax
import jax.numpy as jnp
from jax import lax
from jax.experimental import pallas as pl
from jax.experimental.pallas import tpu as pltpu
from jax.sharding import PartitionSpec as P

OMEGA = 0.8
F32 = jnp.float32
LANES = 128


def roll(values, shift, dim):
    return pltpu.roll(values, shift % values.shape[dim], dim)


def lane_of(values):
    return lax.broadcasted_iota(jnp.int32, values.shape, values.ndim - 1)


def row_of(values):
    return lax.broadcasted_iota(jnp.int32, values.shape, values.ndim - 2)


def bit_of(values, bit):
    return ((lane_of(values) >> bit) & 1) == 1


def pair(values, bit):
    step, dim = 1 << bit, values.ndim - 1
    other = jnp.where(bit_of(values, bit), roll(values, step, dim), roll(values, -step, dim))
    return values + other


def keep(values, bit, want):
    step, dim = 1 << bit, values.ndim - 1
    if want:
        return jnp.where(bit_of(values, bit), values, roll(values, -step, dim))
    return jnp.where(bit_of(values, bit), roll(values, step, dim), values)


def spread(values, which, bits):
    for bit in range(bits):
        values = keep(values, bit, (which >> bit) & 1)
    return values


def relax_factor(diag):
    good = diag > 0.0
    return jnp.where(good, OMEGA / jnp.where(good, diag, 1.0), 0.0)


def loop(first, last, step, body, unroll=16):
    count = (last - first + 1) // step
    assert count * step == last - first + 1
    trips = count // unroll

    def run(index, carry):
        for k in range(unroll):
            body(first + (index * unroll + k) * step)
        return carry

    if trips > 1:
        lax.fori_loop(0, trips, run, 0)
    else:
        trips = 0
    for k in range(trips * unroll, count):
        body(first + k * step)


def beside(vals, faces, plane, count, level, rows, sides=None):
    fx, fy, fz = faces
    shift = 1 << level
    here = pl.ds(plane, count)
    v = vals[here, rows]
    y_face, z_face = fy[here, rows], fz[here, rows]
    total = fx[here, rows] * vals[pl.ds(plane - 1, count), rows]
    total = total + fx[pl.ds(plane + 1, count), rows] * vals[pl.ds(plane + 1, count), rows]
    if sides is None:
        total = total + y_face * roll(v, 1, 1) + roll(y_face * v, -1, 1)
    else:
        low, high = sides
        total = total + y_face * vals[here, low] + fy[here, high] * vals[here, high]
    total = total + z_face * roll(v, shift, 2) + roll(z_face * v, -shift, 2)
    return v, total


def sweep(out, vals, side, faces, weight, first, last, step, level, unroll=16, rows=slice(None), sides=None):
    def body(plane):
        v, total = beside(vals, faces, plane, step, level, rows, sides)
        here = pl.ds(plane, step)
        out[here, rows] = (1.0 - OMEGA) * v + weight[here, rows] * (side[here, rows] + total)

    loop(first, last, step, body, unroll)


def remains(out, vals, side, faces, diag, first, last, step, level, unroll=16, rows=slice(None), sides=None):
    def body(plane):
        v, total = beside(vals, faces, plane, step, level, rows, sides)
        here = pl.ds(plane, step)
        out[here, rows] = side[here, rows] - diag[here, rows] * v + total

    loop(first, last, step, body, unroll)


def block_sum(ref, plane, start, count):
    even, odd = pl.ds(start, count, stride=2), pl.ds(start + 1, count, stride=2)
    low = ref[plane, even, :] + ref[plane, odd, :]
    return low + (ref[plane + 1, even, :] + ref[plane + 1, odd, :])


def coarse_stencil(faces, diag, plane, start, count, level):
    fx, fy, fz = faces
    even, odd = pl.ds(start, count, stride=2), pl.ds(start + 1, count, stride=2)
    x_low = fx[plane, even, :] + fx[plane, odd, :]
    x_mid = fx[plane + 1, even, :] + fx[plane + 1, odd, :]
    y_low = fy[plane, even, :] + fy[plane + 1, even, :]
    y_mid = fy[plane, odd, :] + fy[plane + 1, odd, :]
    z_sum = block_sum(fz, plane, start, count)
    d_sum = block_sum(diag, plane, start, count)
    d_new = pair(d_sum - 2.0 * (x_mid + y_mid), level) - 2.0 * keep(z_sum, level, 1)
    return pair(x_low, level), pair(y_low, level), keep(z_sum, level, 0), d_new


def call(body, outs, scratch, limit, flops, *args, space=pltpu.VMEM):
    nbytes = sum(4 * a.size for a in args) + sum(4 * o.size for o in outs)
    return pl.pallas_call(
        body,
        out_shape=outs,
        in_specs=[pl.BlockSpec(memory_space=space)] * len(args),
        out_specs=[pl.BlockSpec(memory_space=pltpu.VMEM)] * len(outs),
        scratch_shapes=scratch,
        compiler_params=pltpu.CompilerParams(vmem_limit_bytes=limit << 20),
        cost_estimate=pl.CostEstimate(flops=flops, bytes_accessed=nbytes, transcendentals=0),
    )(*args)


def array(*shape):
    return jax.ShapeDtypeStruct(shape, F32)


def shared_tiles(reach):
    for dx in range(1, reach - 3):
        other = 2 * reach - 8 - dx
        yield (dx, other, reach - dx) if dx < other < reach else (dx, 0, 8)


def either_way(up, first, second, fill):
    pl.when(up)(lambda: fill(first, second))
    pl.when(jnp.logical_not(up))(lambda: fill(second, first))


def y_own_kernel(eps, src, scr, first, second):
    def fill(up, down):
        for index, own in enumerate((eps, src, scr)):
            up[16 * index : 16 * index + 16] = own[:, 8:16]
            down[16 * index : 16 * index + 16] = own[:, 0:8]
            for plane in range(16):
                tile, row = 48 + 4 * index + plane // 4, 2 * (plane % 4)
                up[tile, row : row + 2] = own[plane, 6:8]
                down[tile, row : row + 2] = own[plane, 8:10]

    either_way(first_up("gy", 1), first, second, fill)


def y_corner_kernel(xa, xb, first, second):
    rows = lax.broadcasted_iota(jnp.int32, (8, LANES), 0)

    def fill(up, down, xl, xr):
        at = 0
        for start, reach in ((0, 10), (10, 9), (19, 9)):
            for part, plane_of in ((xl, lambda dx: reach - dx), (xr, lambda dx: dx - 1)):
                for dx, other, most in shared_tiles(reach):
                    plane = start + plane_of(dx)
                    above, below = part[plane, 8:16], part[plane, 0:8]
                    if other:
                        plane = start + plane_of(other)
                        above = jnp.where(rows >= 8 - most, above, roll(part[plane, 8:16], 8 - most, 0))
                        below = jnp.where(rows < most, below, roll(part[plane, 0:8], most, 0))
                    up[at], down[at] = above, below
                    at += 1
        for ref, row in ((up, 6), (down, 8)):
            ref[at] = jnp.zeros((8, LANES), F32)
            ref[at, 0:2] = xl[9, row : row + 2]
            ref[at, 2:4] = xr[0, row : row + 2]

    either_way(
        first_up("gx", 1),
        xb,
        xa,
        lambda xl, xr: either_way(first_up("gy", 1), first, second, lambda up, down: fill(up, down, xl, xr)),
    )


def down_kernel(
    eps, src, scr, xa, xb, ya, yb, za, zb,
    u0_out, fx0_out, fy0_out, fz0_out, w0_out, r0_out,
    fx1, fy1, fz1, w1, l1_own, s2, b2, ship_a, ship_b,
    e, b, s, fx, fy, fz, w, d, ua, ub, b1, d1, va, vb,
):
    x_up = first_up("gx", 1).astype(jnp.int32)
    y_up = first_up("gy", 1)
    row_a = pl.multiple_of(8 + 24 * y_up.astype(jnp.int32), 8)
    row_b = pl.multiple_of(32 - 24 * y_up.astype(jnp.int32), 8)
    at = 0
    blank = jnp.zeros((8, LANES), F32)
    for index, (ref, own, start, reach, margin) in enumerate(((e, eps, 0, 10, 1), (b, src, 10, 9, 0), (s, scr, 19, 9, 0))):
        first = 10 - reach
        ref[10:26, 16:32] = own[...]
        ref[pl.ds(first + (26 - first) * x_up, reach), 16:32] = xa[start : start + reach]
        ref[pl.ds(26 - (26 - first) * x_up, reach), 16:32] = xb[start : start + reach]
        ref[10:26, pl.ds(row_a, 8)] = ya[16 * index : 16 * index + 16]
        ref[10:26, pl.ds(row_b, 8)] = yb[16 * index : 16 * index + 16]
        for plane in (first, 25 + reach):
            ref[plane, 8:16] = blank
            ref[plane, 32:40] = blank
        for plane in range(first, 26 + reach):
            if not 10 - margin <= plane < 26 + margin:
                ref[plane, 0:8] = blank

        def fill(below_ref, above_ref, below_side, above_side, ref=ref, index=index, reach=reach, margin=margin, at=at):
            for plane_of in (lambda dx: 10 - dx, lambda dx: 25 + dx):
                for dx, other, most in shared_tiles(reach):
                    below, above = below_side[at], above_side[at]
                    ref[plane_of(dx), 8:16] = below
                    ref[plane_of(dx), 32:40] = above
                    if other:
                        ref[plane_of(other), 8:16] = roll(below, most, 0)
                        ref[plane_of(other), 32:40] = roll(above, -most, 0)
                    at += 1
            edges = [(below_ref, above_ref, 48 + 4 * index + k // 4, 2 * (k % 4), 10 + k) for k in range(16)]
            if margin:
                edges += [(below_side, above_side, 32, 0, 9), (below_side, above_side, 32, 2, 26)]
            for low_ref, high_ref, tile, row, plane in edges:
                below, above = low_ref[tile], high_ref[tile]
                rows = row_of(below)
                ref[plane, 0:8] = jnp.where(
                    rows < 2, roll(above, -row, 0), jnp.where(rows >= 6, roll(below, 6 - row, 0), 0.0)
                )

        pl.when(y_up)(lambda fill=fill: fill(yb, ya, zb, za))
        pl.when(jnp.logical_not(y_up))(lambda fill=fill: fill(ya, yb, za, zb))
        at += 2 * (reach - 4)

    def stencil(plane):
        cells = e[pl.ds(plane - 1, 4), 0:40]
        centre = cells[1:3]
        x_face = 0.5 * (cells[0:3] + cells[1:4])
        y_face = 0.5 * (centre + roll(centre, 1, 1))
        lanes = lane_of(centre)
        z_face = jnp.where(lanes == 0, 0.0, 0.5 * (centre + roll(centre, 1, 2)))
        ends = jnp.where((lanes == 0) | (lanes == LANES - 1), 0.5 * centre, 0.0)
        here = pl.ds(plane, 2)
        screen = s[here, 0:40]
        diag = x_face[0:2] + x_face[1:3] + y_face + roll(y_face, -1, 1)
        diag = diag + z_face + roll(z_face, -1, 2) + screen + ends
        diag = jnp.where(screen > 0.0, diag, 0.0)
        weight = relax_factor(diag)
        value = weight * b[here, 0:40]
        fx[pl.ds(plane, 3), 0:40] = x_face
        fy[here, 0:40] = y_face
        fy[here, 40:48] = y_face[:, 0:8]
        fz[here, 0:40] = z_face
        d[here, 0:40] = diag
        w[here, 0:40] = weight
        ua[here, 0:40] = value
        ua[here, 40:48] = value[:, 0:8]

    loop(1, 34, 2, stencil, 8)
    faces = (fx, fy, fz)
    rows, sides = slice(8, 40), (slice(7, 39), slice(9, 41))
    sweep(ub, ua, b, faces, w, 2, 33, 2, 0, 8, rows, sides)
    sweep(ua, ub, b, faces, w, 3, 32, 2, 0, 8, rows, sides)
    remains(ub, ua, b, faces, d, 4, 31, 2, 0, 8, rows, sides)
    u0_out[...] = ua[10:26, 16:32]

    def keep_window(plane):
        for out, ref in ((fx0_out, fx), (fy0_out, fy), (fz0_out, fz), (w0_out, w), (r0_out, ub)):
            out[plane, 8:24] = ref[plane + 7, 16:32]
            high, low = ref[plane + 7, 32:40], ref[plane + 7, 8:16]
            out[plane, 0:8] = jnp.where(row_of(high) < 4, high, low)

    loop(0, 21, 1, keep_window, 8)

    def to_level1(plane):
        x_face, y_face, z_face, diag = coarse_stencil(faces, d, 2 * plane, 0, 20, 0)
        fx1[plane, 0:20] = x_face
        fy1[plane, 0:20] = y_face
        fz1[plane, 0:20] = z_face
        fy1[plane, 20:21] = y_face[0:1]
        d1[plane, 0:20] = diag
        w1[plane, 0:20] = relax_factor(diag)

    for ref in (fx1, fy1, fz1, w1, d1, b1):
        ref[:, 16:24] = jnp.zeros((18, 8, LANES), F32)
    loop(1, 16, 1, to_level1, 16)
    even, odd = pl.ds(0, 20, stride=2), pl.ds(1, 20, stride=2)
    fx1[17, 0:20] = pair(fx[34, even, :] + fx[34, odd, :], 0)

    def side1(plane):
        side = pair(block_sum(ub, 2 * plane, 0, 20), 0)
        b1[plane, 0:20] = side
        va[plane, 0:20] = w1[plane, 0:20] * side

    loop(2, 15, 1, side1, 14)
    va[:, 20:24] = jnp.zeros((18, 4, LANES), F32)
    faces1 = (fx1, fy1, fz1)
    sweep(vb, va, b1, faces1, w1, 3, 14, 4, 1)
    sweep(va, vb, b1, faces1, w1, 4, 13, 2, 1)
    remains(vb, va, b1, faces1, d1, 5, 12, 4, 1)

    own = jnp.where(bit_of(va[5:13, 8:16], 0), va[5:13, 8:16], vb[5:13, 8:16])
    l1_own[...] = own
    quarter = lax.broadcasted_iota(jnp.int32, (8, LANES), 1) & 3
    for m in range(8):
        parts = coarse_stencil(faces1, d1, 1 + 2 * m, 4, 8, 1)
        stack = parts[3]
        for q in range(3):
            stack = jnp.where(quarter == q, parts[q], stack)
        s2[m] = stack
    packed = jnp.zeros((4, LANES), F32)
    for k in range(4):
        packed = jnp.where(quarter[0:4] == k, pair(block_sum(vb, 5 + 2 * k, 8, 4), 1), packed)
    b2[0, 0:4] = packed
    b2[0, 4:8] = jnp.zeros((4, LANES), F32)
    for ship in (ship_a, ship_b):
        ship[0:8] = s2[...]
        ship[8:9] = b2[...]
    for t in range(4):
        first, second = l1_own[2 * t], l1_own[2 * t + 1]
        low = row_of(first) < 4
        up = jnp.where(low, roll(first, -4, 0), second)
        down = jnp.where(low, first, roll(second, 4, 0))
        ship_a[9 + t] = jnp.where(y_up, up, down)
        ship_b[9 + t] = jnp.where(y_up, down, up)


def window_kernel(s2, b2, l1_own, a1a, a1b, s2_wide, b2_wide, l1_ext, ship_a, ship_b):
    y_up = first_up("gy", 1)
    rows = lax.broadcasted_iota(jnp.int32, (8, LANES), 0)

    def join(below, above):
        for m in range(8):
            s2_wide[2 * m] = jnp.where(rows < 6, below[m], roll(s2[m], 4, 0))
            s2_wide[2 * m + 1] = jnp.where(rows < 2, roll(s2[m], -4, 0), above[m])
        b2_wide[0] = jnp.where(rows < 6, roll(below[8], 2, 0), roll(b2[0], 6, 0))
        b2_wide[1] = jnp.where(rows < 2, roll(b2[0], -2, 0), roll(above[8], 2, 0))
        for k in range(8):
            t, turn = 9 + k // 2, 4 * (k % 2)
            l1_ext[2 * k] = jnp.where(rows < 4, roll(above[t], -turn, 0), roll(below[t], 4 - turn, 0))
            l1_ext[2 * k + 1] = l1_own[k]

    pl.when(y_up)(lambda: join(a1b, a1a))
    pl.when(jnp.logical_not(y_up))(lambda: join(a1a, a1b))
    up = first_up("gx", 1).astype(jnp.int32)
    for ship, way in ((ship_a, up), (ship_b, 1 - up)):
        ship[0:12] = s2_wide[pl.ds(4 - 4 * way, 12)]
        ship[12:14] = b2_wide[...]
        ship[14:22] = l1_ext[pl.ds(8 * way, 8)]


def level2_kernel(
    s2_wide, b2_wide, c1a, c1b,
    fx, fy, fz, w, payload,
    d, b, ua, ub, piece,
):
    up = first_up("gx", 1).astype(jnp.int32)
    b[0:2] = jnp.zeros((2, 16, LANES), F32)
    b[14:16] = jnp.zeros((2, 16, LANES), F32)
    for part, tile, first, count in ((s2_wide, 4, 6, 4), (c1a, 0, 10 * up, 6), (c1b, 0, 10 - 10 * up, 6)):
        for k in range(count):
            tiles = jnp.concatenate([part[tile + 2 * k], part[tile + 2 * k + 1]], axis=0)
            fx[first + k] = spread(tiles, 0, 2)
            fy[first + k] = spread(tiles, 1, 2)
            fz[first + k] = spread(tiles, 2, 2)
            diag = spread(tiles, 3, 2)
            d[first + k] = diag
            w[first + k] = relax_factor(diag)
    for part, tile, first in ((b2_wide, 0, 6), (c1a, 12, 2 + 8 * up), (c1b, 12, 10 - 8 * up)):
        tiles = jnp.concatenate([part[tile], part[tile + 1]], axis=0)
        for k in range(4):
            b[first + k] = spread(tiles, k, 2)

    def begin(plane):
        here = pl.ds(plane, 4)
        ua[here] = w[here] * b[here]

    loop(0, 15, 4, begin)
    faces = (fx, fy, fz)
    sweep(ub, ua, b, faces, w, 3, 12, 2, 2, 8)
    sweep(ua, ub, b, faces, w, 4, 11, 2, 2, 8)
    remains(ub, ua, b, faces, d, 6, 9, 2, 2, 8)

    gx, gy = lax.axis_index("gx"), lax.axis_index("gy")
    rows = lax.broadcasted_iota(jnp.int32, (2, LANES), 0)
    slot = lax.broadcasted_iota(jnp.int32, (2, LANES), 1) & 7
    lines = [jnp.zeros((2, LANES), F32) for _ in range(3)]
    for x in range(2):
        parts = coarse_stencil(faces, d, 6 + 2 * x, 6, 2, 2)
        x_face, y_face, z_face, diag = parts
        if x == 0:
            x_face = jnp.where(gx == 0, 0.0, x_face)
        y_face = jnp.where((gy == 0) & (rows == 0), 0.0, y_face)
        side = pair(block_sum(ub, 6 + 2 * x, 6, 2), 2)
        for index, values in enumerate((x_face, y_face, z_face, diag, side)):
            chosen = slot == (x + 2 * rows if index == 4 else x + 2 * (index % 2) + 4 * rows)
            lines[index // 2] = jnp.where(chosen, values, lines[index // 2])
    for k in range(3):
        piece[k : k + 1] = jnp.sum(lines[k], axis=0, keepdims=True)
    quarter = lax.broadcasted_iota(jnp.int32, (4, LANES), 1) & 3
    for ref, row in ((ub, 3), (ua, 7)):
        stack = ref[9, 6:10]
        for k in range(3):
            stack = jnp.where(quarter == k, ref[6 + k, 6:10], stack)
        piece[row : row + 4] = stack
    piece[11:12] = jnp.zeros((1, LANES), F32)
    whole = piece[0:12]
    for k in range(payload.shape[0] // 12):
        payload[12 * k : 12 * k + 12] = whole


def relay_kernel(got, payload, around, piece):
    count = got.shape[0] // 12
    gy = lax.axis_index("gy")
    around[0:24] = jnp.zeros((24, LANES), F32)
    around[24 : 24 + 12 * count] = got[...]
    around[24 + 12 * count : 48 + 12 * count] = jnp.zeros((24, LANES), F32)
    first, second = got[pl.ds(0, count, stride=12), :], got[pl.ds(1, count, stride=12), :]
    upper = bit_of(first, 2)
    piece[pl.ds(0, count, stride=2), :] = jnp.where(upper, roll(second, 4, 1), first)
    piece[pl.ds(1, count, stride=2), :] = jnp.where(upper, second, roll(first, -4, 1))
    even, odd = got[pl.ds(2, count // 2, stride=24), :], got[pl.ds(14, count // 2, stride=24), :]
    piece[2 * count + 24 :] = jnp.where(bit_of(even, 2), roll(odd, 4, 1), even)
    for target, start, least, most in ((2 * count, 3, -5, 9), (2 * count + 14, 7, -3, 7)):
        for block in range(-2, 3):
            low, high = max(4 * block, least), min(4 * block + 4, most)
            if low < high:
                line = 12 * (gy + block + 2) + start + low - 4 * block
                piece[target + low - least : target + high - least] = around[pl.ds(line, high - low), :]
    whole = piece[...]
    size = piece.shape[0]
    for k in range(payload.shape[0] // size):
        payload[size * k : size * k + size] = whole


def piece_rows(n_y):
    return 5 * n_y // 2 + 24


def x_low(values, rows):
    slot = lane_of(values) & 7
    return jnp.where(slot == 0, roll(roll(values, -7, 1), rows, 0), roll(values, 1, 1))


def x_high(values, rows):
    slot = lane_of(values) & 7
    return jnp.where(slot == 7, roll(roll(values, 7, 1), -rows, 0), roll(values, -1, 1))


def yz_beside(v, y_face, z_face, level):
    total = y_face * roll(v, 1 + level, 0) + roll(y_face * v, -1 - level, 0)
    return total + z_face * roll(v, 8 + 8 * level, 1) + roll(z_face * v, -8 - 8 * level, 1)


def level3_beside(v, faces, rows):
    (x0, x1), y_faces, z_faces = faces
    totals = [x0 * x_low(v[1], rows) + x1 * v[1], x1 * v[0] + x_high(x0 * v[0], rows)]
    return [totals[k] + yz_beside(v[k], y_faces[k], z_faces[k], 0) for k in range(2)]


def row_pair(values):
    odd = (row_of(values) & 1) == 1
    return values + jnp.where(odd, roll(values, 1, 0), roll(values, -1, 0))


def row_keep(values, want):
    odd = (row_of(values) & 1) == 1
    if want:
        return jnp.where(odd, values, roll(values, -1, 0))
    return jnp.where(odd, roll(values, 1, 0), values)


def exchange_slots(tiles):
    for bit in range(3):
        step = 1 << bit
        upper = bit_of(tiles[0], bit)
        made = list(tiles)
        for k in range(8):
            if not k & step:
                made[k] = jnp.where(upper, roll(tiles[k + step], step, 1), tiles[k])
                made[k + step] = jnp.where(upper, tiles[k + step], roll(tiles[k], -step, 1))
        tiles = made
    return tiles


def coarse_levels(got, b3, n_x, n_y):
    size, rows = piece_rows(n_y), 2 * n_y
    groups = []
    for g in range(n_x // 8):
        lines = [(8 * g + q) * size for q in range(8)]
        groups.append(exchange_slots([got[line : line + rows] for line in lines]))
        sides = exchange_slots([got[line + rows + 24 : line + size] for line in lines])
        for k in range(8):
            b3[k % 2, pl.ds(g * rows + k // 2, n_y // 2, stride=4), :] = sides[k]
    fields = []
    for index in range(4):
        fields.append([jnp.concatenate([g[2 * index + x] for g in groups], axis=0) for x in range(2)])
    faces, diag = fields[0:3], fields[3]
    side = [b3[0], b3[1]]
    weight = [relax_factor(d) for d in diag]

    def sweep3(v, side):
        total = level3_beside(v, faces, rows)
        return [(1.0 - OMEGA) * v[k] + weight[k] * (side[k] + total[k]) for k in range(2)]

    u = [weight[k] * side[k] for k in range(2)]
    u = sweep3(u, side)
    u = sweep3(u, side)
    total = level3_beside(u, faces, rows)
    r = [side[k] - diag[k] * u[k] + total[k] for k in range(2)]

    (x0, x1), (y0, y1), (z0, z1) = faces
    y_sum, z_sum = pair(y0 + y1, 3), row_pair(z0 + z1)
    x4, y4, z4 = row_pair(pair(x0, 3)), row_keep(y_sum, 0), keep(z_sum, 3, 0)
    inner = row_keep(y_sum, 1) + keep(z_sum, 3, 1)
    w4 = relax_factor(row_pair(pair(diag[0] + diag[1] - 2.0 * x1, 3)) - 2.0 * inner)
    b4 = row_pair(pair(r[0] + r[1], 3))
    v = w4 * b4
    for _ in range(5):
        total = x4 * x_low(v, rows) + x_high(x4 * v, rows) + yz_beside(v, y4, z4, 1)
        v = (1.0 - OMEGA) * v + w4 * (b4 + total)
    c = [v, v]
    for _ in range(3):
        c = sweep3(c, r)
    return [u[k] + c[k] for k in range(2)]


def up_kernel(
    got, u0, fx0, fy0, fz0, w0, r0,
    fx1, fy1, fz1, w1, l1_ext, c1a, c1b,
    fx2, fy2, fz2, w2,
    out,
    u3, b3, e3, r2, u2, ea2, eb2, r1, u1, ea1, eb1, ea0, eb0,
):
    gx, gy = lax.axis_index("gx"), lax.axis_index("gy")
    n_x, n_y = lax.axis_size("gx"), lax.axis_size("gy")
    size = piece_rows(n_y)
    for block in range(5):
        device = jnp.clip(gx + block - 2, 0, n_x - 1)
        for ref, line in ((r2, 2 * n_y - 1), (u2, 2 * n_y + 11)):
            tiles = got[pl.ds(device * size + line, 16), :]
            for k in range(4):
                if 0 <= 4 * block - 2 + k < 16:
                    ref[4 * block - 2 + k] = spread(tiles, k, 2)

    solved = coarse_levels(got, b3, n_x, n_y)
    for x in range(2):
        u3[x, 8 : 8 + solved[x].shape[0]] = solved[x]
    for block in range(5):
        device = jnp.clip(gx + block - 2, 0, n_x - 1)
        line = 4 + lax.div(device, 8) * 2 * n_y + 2 * gy
        for x in range(2):
            values = pltpu.roll(u3[x, pl.ds(line, 16), :], lax.rem(LANES - lax.rem(device, 8), LANES), 1)
            e3[2 * block + x] = spread(values, 0, 3)

    for plane in range(16):
        values = e3[plane // 2 + 1][1:9]
        for k in range(2):
            ea2[plane, pl.ds(k, 8, stride=2), :] = values

    def inside(values, weight, first, last, step):
        def body(plane):
            here = pl.ds(plane, step)
            values[here] = jnp.where(weight[here] > 0.0, values[here], 0.0)

        loop(first, last, step, body)

    inside(ea2, w2, 0, 15, 4)
    faces = (fx2, fy2, fz2)
    sweep(eb2, ea2, r2, faces, w2, 1, 14, 2, 2)
    sweep(ea2, eb2, r2, faces, w2, 2, 13, 4, 2)
    sweep(eb2, ea2, r2, faces, w2, 3, 12, 2, 2)

    even = first_up("gx", 1).astype(jnp.int32)
    for part, first, tile, count in ((c1a, 1 + 12 * even, 14, 4), (l1_ext, 5, 0, 8), (c1b, 13 - 12 * even, 14, 4)):
        for k in range(count):
            sides, own = part[tile + 2 * k], part[tile + 2 * k + 1]
            for ref, which in ((r1, 0), (u1, 1)):
                edge = keep(sides, 0, which)
                ref[first + k, 0:8] = edge
                ref[first + k, 8:16] = keep(own, 0, which)
                ref[first + k, 16:24] = edge

    for plane in range(3, 13):
        values = (u2[plane] + eb2[plane])[3:13]
        for k in range(2):
            target = 2 * plane - 7 + k
            if 0 <= target < 18:
                ea1[target, pl.ds(2, 10, stride=2), :] = values
                ea1[target, pl.ds(3, 10, stride=2), :] = values
    inside(ea1, w1, 1, 16, 4)
    faces = (fx1, fy1, fz1)
    for plane in (0, 17):
        ea1[plane] = jnp.where(edge_inside(gx, plane), ea1[plane], 0.0)
    sweep(eb1, ea1, r1, faces, w1, 1, 16, 4, 1)
    sweep(ea1, eb1, r1, faces, w1, 2, 15, 2, 1)
    sweep(eb1, ea1, r1, faces, w1, 3, 14, 4, 1)

    for plane in range(3, 15):
        values = u1[plane] + eb1[plane]
        for k in range(2):
            target = 3 + 2 * (plane - 5) + k
            if 0 <= target < 22:
                for parity in range(2):
                    ea0[target, pl.ds(4 + parity, 10, stride=2), :] = values[6:16]
                    ea0[target, pl.ds(parity, 2, stride=2), :] = values[16:18]
    inside(ea0, w0, 0, 21, 2)
    faces = (fx0, fy0, fz0)
    sweep(eb0, ea0, r0, faces, w0, 1, 20, 2, 0)
    sweep(ea0, eb0, r0, faces, w0, 2, 19, 2, 0)

    def last(plane):
        v, total = beside(ea0, faces, plane, 2, 0, slice(None))
        here = pl.ds(plane, 2)
        values = (1.0 - OMEGA) * v + w0[here] * (r0[here] + total)
        out[pl.ds(plane - 3, 2)] = u0[pl.ds(plane - 3, 2)] + values[:, 8:24]

    loop(3, 18, 2, last)


def edge_inside(gx, plane):
    where = 8 * gx + plane - 5
    return (where >= 0) & (where < 8 * lax.axis_size("gx"))


def swapped(values, axis, step, second):
    pairs = []
    for k in range(lax.axis_size(axis) - step):
        if (k // step) % 2 != second:
            pairs += [(k, k + step), (k + step, k)]
    return lax.ppermute(values, axis, pairs)


def first_up(axis, step):
    return lax.rem(lax.div(lax.axis_index(axis), step), 2) == 1


def local(source, dielectric, screening):
    fields = (dielectric, source, screening)
    even = first_up("gx", 1).astype(jnp.int32)

    def strip(way):
        parts = [lax.dynamic_slice_in_dim(f, way * (16 - n), n, 0) for f, n in zip(fields, (10, 9, 9))]
        return jnp.concatenate(parts, axis=0)

    xa, xb = strip(even), strip(1 - even)
    xa, xb = swapped(xa, "gx", 1, 0), swapped(xb, "gx", 1, 1)
    ya, yb = call(y_own_kernel, [array(60, 8, LANES)] * 2, [], 2, 10_000, *fields)
    ya, yb = swapped(ya, "gy", 1, 0), swapped(yb, "gy", 1, 1)
    za, zb = call(y_corner_kernel, [array(33, 8, LANES)] * 2, [], 2, 10_000, xa, xb)
    za, zb = swapped(za, "gy", 1, 0), swapped(zb, "gy", 1, 1)

    big, mid = pltpu.VMEM((36, 48, LANES), F32), pltpu.VMEM((18, 24, LANES), F32)
    outs = [array(16, 16, LANES)] + [array(22, 24, LANES)] * 5 + [array(18, 24, LANES)] * 4
    outs += [array(8, 8, LANES), array(8, 8, LANES), array(1, 8, LANES), array(13, 8, LANES), array(13, 8, LANES)]
    made = call(down_kernel, outs, [big] * 10 + [mid] * 4, 14, 10_000_000, *fields, xa, xb, ya, yb, za, zb)
    fine, level1, (l1_own, s2, b2, sa, sb) = made[0:6], made[6:10], made[10:15]

    a1a, a1b = swapped(sa, "gy", 1, 0), swapped(sb, "gy", 1, 1)
    outs = [array(16, 8, LANES), array(2, 8, LANES), array(16, 8, LANES), array(22, 8, LANES), array(22, 8, LANES)]
    s2, b2, l1_ext, sa, sb = call(window_kernel, outs, [], 2, 10_000, s2, b2, l1_own, a1a, a1b)
    c1a, c1b = swapped(sa, "gx", 1, 0), swapped(sb, "gx", 1, 1)

    n_x, n_y = lax.axis_size("gx"), lax.axis_size("gy")
    two, size = pltpu.VMEM((16, 16, LANES), F32), piece_rows(n_y)
    outs = [array(16, 16, LANES)] * 4 + [array(12 * n_y, LANES)]
    scratch = [two] * 4 + [pltpu.VMEM((16, LANES), F32)]
    *level2, payload = call(level2_kernel, outs, scratch, 4, 5_000_000, s2, b2, c1a, c1b)

    payload = payload.reshape(6 * n_y, 2, LANES)
    got = lax.all_to_all(payload, "gy", 0, 0, tiled=True).reshape(12 * n_y, LANES)
    scratch = [pltpu.VMEM((12 * n_y + 48, LANES), F32), pltpu.VMEM((size, LANES), F32)]
    (payload,) = call(relay_kernel, [array(n_x * size, LANES)], scratch, 2, 10_000, got)
    got = lax.all_to_all(payload, "gx", 0, 0, tiled=True)

    scratch = [pltpu.VMEM((2, n_x // 4 * n_y + extra, LANES), F32) for extra in (24, 0)]
    scratch += [pltpu.VMEM((12, 16, LANES), F32)]
    scratch += [two] * 4 + [mid] * 4 + [pltpu.VMEM((22, 24, LANES), F32)] * 2
    (result,) = call(
        up_kernel, [array(16, 16, LANES)], scratch, 6, 10_000_000,
        got, *fine, *level1, l1_ext, c1a, c1b, *level2,
    )
    return result


def solution(mesh):
    spec = P("gx", "gy", None)
    return jax.shard_map(local, mesh=mesh, in_specs=(spec,) * 3, out_specs=spec, check_vma=False)
```
